32 devices in a mesh: seq: 2 (over y), fsdp: 16 (over z, x, core).
Axes of the slice: x: 2, y: 2, z: 4, core: 2. Of those that a mesh axis runs over, the one named last changes fastest.
Arguments:
- latents: bfloat16 [32, 512, 1024], P('fsdp', 'seq'), may hold values from -6 to 6
- timesteps: int32 [32], replicated, may hold values from 0 to 999
- class_ids: int32 [32], replicated, may hold values from 0 to 1000
- class_table: bfloat16 [1001, 1024], P(None, 'fsdp'), may hold values from -6 to 6
- w_mod: bfloat16 [1024, 6144], P('fsdp'), may hold values from -0.1875 to 0.1875
- b_mod: bfloat16 [6144], P('fsdp'), may hold values from -3 to 3
- w_qkv: bfloat16 [1024, 3072], P('fsdp'), may hold values from -0.1875 to 0.1875
- b_q: bfloat16 [1024], P('fsdp'), may hold values from -3 to 3
- b_v: bfloat16 [1024], P('fsdp'), may hold values from -0.29882812 to 0.29882812
- w_out: bfloat16 [1024, 1024], P('fsdp'), may hold values from -1.5 to 1.5
- b_out: bfloat16 [1024], P('fsdp'), may hold values from -2 to 2
- w_fc1: bfloat16 [1024, 4096], P('fsdp'), may hold values from -0.1875 to 0.1875
- b_fc1: bfloat16 [4096], P('fsdp'), may hold values from -3 to 3
- w_fc2: bfloat16 [4096, 1024], P('fsdp'), may hold values from -0.09375 to 0.09375
- b_fc2: bfloat16 [1024], P('fsdp'), may hold values from -2 to 2
- out_cotangent: bfloat16 [32, 512, 1024], P('fsdp', 'seq'), may hold values from -6 to 6
Outputs:
- result: bfloat16 [32, 512, 1024], P('fsdp', 'seq')
- grad_latents: float32 [32, 512, 1024], P('fsdp', 'seq')
- grad_table: float32 [1001, 1024], P(None, 'fsdp')
- grad_w_mod: float32 [1024, 6144], P('fsdp')
- grad_b_mod: float32 [6144], P('fsdp')
- grad_w_qkv: float32 [1024, 3072], P('fsdp')
- grad_b_q: float32 [1024], P('fsdp')
- grad_b_v: float32 [1024], P('fsdp')
- grad_w_out: float32 [1024, 1024], P('fsdp')
- grad_b_out: float32 [1024], P('fsdp')
- grad_w_fc1: float32 [1024, 4096], P('fsdp')
- grad_b_fc1: float32 [4096], P('fsdp')
- grad_w_fc2: float32 [4096, 1024], P('fsdp')
- grad_b_fc2: float32 [1024], P('fsdp')
The draws below stay inside these ranges and needn't reach their ends.
All inputs are finite; a program needn't handle non-finite values.
Results may differ from the reference program's by a relative error of at most 0.014.
The reference program's roundings to bfloat16 on the way count: a program that leaves them out, or rounds other values in their place, can miss the bound.
Values may be sent and summed in bfloat16 or wider, within the bound.
No kernel may reach another device: no remote copies, remote signals or barrier semaphores. Data moves between devices by JAX's collectives and lax.ppermute only.
A program may use at most 256 MiB of HBM per device.

```python
import math
import jax
import jax.numpy as jnp
from jax import lax

D = 1024
HEADS = 16
HEAD_DIM = 64
FF = 4096
CLASSES = 1001
LENGTH = 512
LATENTS = 32
QBLOCK = 512


def set_ends(values, stream_key, smallest, high):
    place = [jax.random.randint(jax.random.fold_in(stream_key, axis), (), 0, length) for axis, length in enumerate(values.shape)]
    longest = values.shape.index(max(values.shape))
    next_to = place[:longest] + [(place[longest] + 1) % values.shape[longest]] + place[longest + 1:]
    return values.at[tuple(place)].set(smallest).at[tuple(next_to)].set(high)


def steps_of(stream_key, shape, split, least, high):
    level = 1.0
    for axis_at, blocks in split:
        steps = jax.random.uniform(jax.random.fold_in(jax.random.fold_in(stream_key, 6), axis_at), (blocks,), jnp.float32, least / len(split), high / len(split))
        level = level * jnp.repeat(jnp.exp(steps), shape[axis_at] // blocks).reshape((-1,) + (1,) * (len(shape) - 1 - axis_at))
    return level


def normal_values(stream_key, extent, deviation, limit, split=(), held_as=jnp.bfloat16):
    factor_of = steps_of(stream_key, extent, split, -0.22, 0.18) if split else 1.0
    result = jax.random.normal(stream_key, extent, jnp.float32) * deviation * factor_of
    return jnp.minimum(jnp.maximum(result, -limit), limit).astype(held_as)


def setup_inputs(seed: int = 0) -> dict:
    splits = jax.random.split(jax.random.key(seed), 17)
    latents = normal_values(splits[0], (LATENTS, LENGTH, D), 1.0, 6.0, ((0, 16), (1, 2)))
    timesteps = set_ends(jax.random.randint(splits[1], (LATENTS,), 0, 1000), jax.random.fold_in(splits[1], 1), 0, 999).astype(jnp.int32)
    class_ids = set_ends(jax.random.randint(splits[2], (LATENTS,), 0, CLASSES), jax.random.fold_in(splits[2], 1), 0, CLASSES - 1).astype(jnp.int32)
    class_table = normal_values(splits[3], (CLASSES, D), 1.0, 6.0, ((1, 16),))
    w_mod = normal_values(splits[4], (D, 6 * D), D ** -0.5, 0.1875, ((0, 16),))
    b_mod = normal_values(splits[5], (6 * D,), 0.5, 3.0, ((0, 16),))
    w_qkv = normal_values(splits[6], (D, 3 * D), D ** -0.5, 0.1875, ((0, 16),))
    b_q = normal_values(splits[7], (D,), 0.5, 3.0, ((0, 16),))
    b_v = normal_values(splits[8], (D,), 0.05, 0.29882812, ((0, 16),))
    w_out = normal_values(splits[9], (D, D), (max(1, D // 64)) ** -0.5, 1.5, ((0, 16),))
    b_out = normal_values(splits[10], (D,), 0.3, 2.0, ((0, 16),))
    w_fc1 = normal_values(splits[11], (D, FF), D ** -0.5, 0.1875, ((0, 16),))
    b_fc1 = normal_values(splits[12], (FF,), 0.5, 3.0, ((0, 16),))
    w_fc2 = normal_values(splits[13], (FF, D), FF ** -0.5, 0.09375, ((0, 16),))
    b_fc2 = normal_values(splits[14], (D,), 0.3, 2.0, ((0, 16),))
    out_cotangent = normal_values(splits[15], (LATENTS, LENGTH, D), 1.0, 6.0, ((0, 16), (1, 2)))
    return {"latents": latents, "timesteps": timesteps, "class_ids": class_ids, "class_table": class_table, "w_mod": w_mod, "b_mod": b_mod, "w_qkv": w_qkv, "b_q": b_q, "b_v": b_v, "w_out": w_out, "b_out": b_out, "w_fc1": w_fc1, "b_fc1": b_fc1, "w_fc2": w_fc2, "b_fc2": b_fc2, "out_cotangent": out_cotangent}


@jax.custom_vjp
def low(v):
    return lax.optimization_barrier(v.astype(jnp.bfloat16)).astype(jnp.float32)

@jax.custom_vjp
def low_back(v):
    return v

def low_keep(v):
    return (low(v), None)

def low_pass(kept, grad):
    return (grad,)

def back_keep(v):
    return (v, None)

def back_low(kept, grad):
    return (low(grad),)
low.defvjp(low_keep, low_pass)
low_back.defvjp(back_keep, back_low)

def matmul_high(earlier_value, latter):
    return jnp.dot(earlier_value, latter, precision=lax.Precision.HIGHEST, preferred_element_type=jnp.float32)

def rounded_both(tensor):
    return low(low_back(tensor))

def normalize(tensor):
    centered = tensor - lax.optimization_barrier(jnp.mean(tensor, axis=-1, keepdims=True))
    variance = lax.optimization_barrier(jnp.mean(centered * centered, axis=-1, keepdims=True))
    return centered * lax.rsqrt(variance + 1e-06)

def gelu_tanh(tensor):
    return 0.5 * tensor * (1.0 + jnp.tanh(0.7978845608028654 * (tensor + 0.044715 * tensor * tensor * tensor)))

def time_features(step_ids, columns):
    half_width = columns // 2
    freqs = jnp.exp(-math.log(10000.0) * jnp.arange(half_width, dtype=jnp.float32) / half_width)
    angles = step_ids.astype(jnp.float32)[:, None] * freqs[None, :]
    return jnp.concatenate([jnp.cos(angles), jnp.sin(angles)], axis=1)

def attend(queries, keys_all, values_all):
    scaling = HEAD_DIM ** (-0.5)

    def one_block(query_block):
        scores = jnp.einsum('qhd,khd->hqk', query_block, keys_all, precision=lax.Precision.HIGHEST) * scaling
        scores = low_back(scores)
        highest = lax.optimization_barrier(jnp.max(scores, axis=-1, keepdims=True))
        powers = jnp.exp(scores - highest)
        weight_tensors = low(powers / lax.optimization_barrier(jnp.sum(powers, axis=-1, keepdims=True)))
        return jnp.einsum('hqk,khd->qhd', weight_tensors, values_all, precision=lax.Precision.HIGHEST)
    blocks = queries.reshape(LENGTH // QBLOCK, QBLOCK, HEADS, HEAD_DIM)
    mixed = lax.map(jax.checkpoint(one_block), blocks)
    return mixed.reshape(LENGTH, HEADS * HEAD_DIM)

def attend_trio(trio):
    return attend(trio[0], trio[1], trio[2])

def diffusion_transformer_block(latent_bundle, modulation_bundle, weight_tensors):
    w_qkv, b_q, b_v, w_out, b_out, w_fc1, b_fc1, w_fc2, b_fc2 = weight_tensors
    latent_count = latent_bundle.shape[0]
    pieces = [modulation_bundle[:, None, position * D:(position + 1) * D] for position in range(6)]
    shift_one, scale_one, gate_one, shift_two, scale_two, gate_two = pieces
    normed_one = low(normalize(latent_bundle) * (1.0 + scale_one) + shift_one)
    projected = matmul_high(normed_one.reshape(-1, D), w_qkv)
    queries = rounded_both(projected[:, :D] + b_q)
    keys_all = rounded_both(projected[:, D:2 * D])
    values_all = rounded_both(projected[:, 2 * D:] + b_v)
    heads_shape = (latent_count, LENGTH, HEADS, HEAD_DIM)
    mixed = lax.map(attend_trio, (queries.reshape(heads_shape), keys_all.reshape(heads_shape), values_all.reshape(heads_shape)))
    mixed = rounded_both(mixed.reshape(-1, D))
    branch_one = low_back(matmul_high(mixed, w_out) + b_out).reshape(latent_count, LENGTH, D)
    middle = latent_bundle + gate_one * branch_one
    normed_two = low(normalize(middle) * (1.0 + scale_two) + shift_two)
    hidden = low_back(matmul_high(normed_two.reshape(-1, D), w_fc1) + b_fc1)
    active = low(gelu_tanh(hidden))
    branch_two = low_back(matmul_high(active, w_fc2) + b_fc2).reshape(latent_count, LENGTH, D)
    return middle + gate_two * branch_two

def forward(latents, class_table, w_mod, b_mod, w_qkv, b_q, b_v, w_out, b_out, w_fc1, b_fc1, w_fc2, b_fc2, timesteps, class_ids):
    condition = class_table[class_ids] + time_features(timesteps, D)
    lifted = low(condition * jax.nn.sigmoid(condition))
    modulation = low_back(matmul_high(lifted, w_mod) + b_mod)
    group_size = math.gcd(LATENTS, max(1, 4096 // LENGTH))
    weight_tensors = (w_qkv, b_q, b_v, w_out, b_out, w_fc1, b_fc1, w_fc2, b_fc2)

    def one_group(matched_pairs):
        return diffusion_transformer_block(matched_pairs[0], matched_pairs[1], weight_tensors)
    grouped = lax.map(jax.checkpoint(one_group), (latents.reshape(LATENTS // group_size, group_size, LENGTH, D), modulation.reshape(LATENTS // group_size, group_size, 6 * D)))
    return grouped.reshape(LATENTS, LENGTH, D)

def reference(latents, timesteps, class_ids, class_table, w_mod, b_mod, w_qkv, b_q, b_v, w_out, b_out, w_fc1, b_fc1, w_fc2, b_fc2, out_cotangent):
    floats = tuple((source.astype(jnp.float32) for source in (latents, class_table, w_mod, b_mod, w_qkv, b_q, b_v, w_out, b_out, w_fc1, b_fc1, w_fc2, b_fc2)))

    def closed(*members):
        return forward(members[0], members[1], members[2], members[3], members[4], members[5], members[6], members[7], members[8], members[9], members[10], members[11], members[12], timesteps, class_ids)
    output, pullback = jax.vjp(closed, *floats)
    grads = pullback(out_cotangent.astype(jnp.float32))
    return (output.astype(jnp.bfloat16), grads[0], grads[1], grads[2], grads[3], grads[4], grads[5], grads[6], grads[7], grads[8], grads[9], grads[10], grads[11], grads[12])
```

```python
import math

import jax
import jax.numpy as jnp
from jax import lax
from jax.experimental import pallas as pl
from jax.experimental.pallas import tpu as pltpu
from jax.sharding import PartitionSpec as P

HEAD_DIM = 64


def time_features(step_ids, columns):
    half_width = columns // 2
    freqs = jnp.exp(-math.log(10000.0) * jnp.arange(half_width, dtype=jnp.float32) / half_width)
    angles = step_ids.astype(jnp.float32)[:, None] * freqs[None, :]
    return jnp.concatenate([jnp.cos(angles), jnp.sin(angles)], axis=1)


def normalize_keep(tensor):
    centered = tensor - jnp.mean(tensor, axis=-1, keepdims=True)
    variance = jnp.mean(centered * centered, axis=-1, keepdims=True)
    inverse = lax.rsqrt(variance + 1e-06)
    return (centered * inverse, inverse)


def normalize_back(grad_hat, normed, inverse):
    mean_grad = jnp.mean(grad_hat, axis=-1, keepdims=True)
    mean_cross = jnp.mean(grad_hat * normed, axis=-1, keepdims=True)
    return inverse * (grad_hat - mean_grad - normed * mean_cross)


def gelu_tanh(tensor):
    return (
        0.5
        * tensor
        * (1.0 + jnp.tanh(0.7978845608028654 * (tensor + 0.044715 * tensor * tensor * tensor)))
    )


def lift_silu(tensor):
    return tensor * jax.nn.sigmoid(tensor)


def outer_sum(earlier_value, latter):
    return lax.dot_general(
        earlier_value, latter, (((0,), (0,)), ((), ())), preferred_element_type=jnp.float32
    )


def compared_with(earlier_value, latter):
    return lax.dot_general(
        earlier_value, latter, (((1,), (1,)), ((), ())), preferred_element_type=jnp.float32
    )


def regroup(tensor, axis_pos, outer_count, inner_count):
    extents = tensor.shape
    splitted = (
        extents[:axis_pos]
        + (outer_count, inner_count, extents[axis_pos] // (outer_count * inner_count))
        + extents[axis_pos + 1 :]
    )
    swapped = jnp.swapaxes(tensor.reshape(splitted), axis_pos, axis_pos + 1)
    return swapped.reshape(extents)


def make_term(lefts, rights, ratio):
    first_left, second_left, third_left, fourth_left = lefts
    first_right, second_right, third_right, fourth_right = rights

    def term(start, count):
        qkv_part = outer_sum(first_left, first_right)
        out_part = outer_sum(second_left, second_right)
        fc1_part = outer_sum(third_left, third_right)
        fc2_part = outer_sum(fourth_left, fourth_right).reshape(
            count, ratio * fourth_right.shape[1]
        )
        return jnp.concatenate([qkv_part, out_part, fc1_part, fc2_part], axis=1)

    return term


def attend_heads(queries, keys_all, values_all, block_rows):
    length_all = queries.shape[0]
    head_count = queries.shape[1] // HEAD_DIM
    scaling = HEAD_DIM ** (-0.5)
    query_blocks = queries.reshape(length_all // block_rows, block_rows, head_count, HEAD_DIM)
    key_heads = keys_all.reshape(length_all, head_count, HEAD_DIM)
    value_heads = values_all.reshape(length_all, head_count, HEAD_DIM)

    def one_block(query_block):
        scores = (
            jnp.einsum("qhd,khd->hqk", query_block, key_heads, preferred_element_type=jnp.float32)
            * scaling
        )
        highest = jnp.max(scores, axis=-1, keepdims=True)
        powers = jnp.exp(scores - highest)
        totals = jnp.sum(powers, axis=-1, keepdims=True)
        weight_tensors = (powers / totals).astype(jnp.bfloat16)
        mixed = jnp.einsum(
            "hqk,khd->qhd", weight_tensors, value_heads, preferred_element_type=jnp.float32
        )
        return (mixed.astype(jnp.bfloat16), (highest + jnp.log(totals))[:, :, 0])

    mixed, log_totals = lax.map(one_block, query_blocks)
    return (mixed.reshape(length_all, head_count * HEAD_DIM), log_totals)


def attend_back(queries, keys_all, values_all, grad_mixed, log_totals, block_rows):
    length_all = queries.shape[0]
    head_count = queries.shape[1] // HEAD_DIM
    scaling = HEAD_DIM ** (-0.5)
    block_count = length_all // block_rows
    query_blocks = queries.reshape(block_count, block_rows, head_count, HEAD_DIM)
    grad_blocks = grad_mixed.reshape(block_count, block_rows, head_count, HEAD_DIM)
    key_heads = keys_all.reshape(length_all, head_count, HEAD_DIM)
    value_heads = values_all.reshape(length_all, head_count, HEAD_DIM)

    def one_block(carried, blocked):
        grad_keys, grad_values = carried
        query_block, grad_block, log_block = blocked
        scores = (
            jnp.einsum("qhd,khd->hqk", query_block, key_heads, preferred_element_type=jnp.float32)
            * scaling
        )
        probs = jnp.exp(scores - log_block[:, :, None])
        grad_values = grad_values + jnp.einsum(
            "hqk,qhd->khd",
            probs.astype(jnp.bfloat16),
            grad_block,
            preferred_element_type=jnp.float32,
        )
        grad_probs = jnp.einsum(
            "qhd,khd->hqk", grad_block, value_heads, preferred_element_type=jnp.float32
        )
        grad_scores = (
            probs * (grad_probs - jnp.sum(grad_probs * probs, axis=-1, keepdims=True))
        ).astype(jnp.bfloat16)
        grad_query = (
            jnp.einsum("hqk,khd->qhd", grad_scores, key_heads, preferred_element_type=jnp.float32)
            * scaling
        )
        grad_keys = (
            grad_keys
            + jnp.einsum(
                "hqk,qhd->khd", grad_scores, query_block, preferred_element_type=jnp.float32
            )
            * scaling
        )
        return ((grad_keys, grad_values), grad_query.astype(jnp.bfloat16))

    zeroed = jnp.zeros((length_all, head_count, HEAD_DIM), jnp.float32)
    (grad_keys, grad_values), grad_queries = lax.scan(
        one_block, (zeroed, zeroed), (query_blocks, grad_blocks, log_totals)
    )
    flat_width = head_count * HEAD_DIM
    return (
        grad_queries.reshape(length_all, flat_width),
        grad_keys.reshape(length_all, flat_width).astype(jnp.bfloat16),
        grad_values.reshape(length_all, flat_width).astype(jnp.bfloat16),
    )


def local(
    latents,
    timesteps,
    class_ids,
    class_table,
    w_mod,
    b_mod,
    w_qkv,
    b_q,
    b_v,
    w_out,
    b_out,
    w_fc1,
    b_fc1,
    w_fc2,
    b_fc2,
    out_cotangent,
):
    micro_count, row_count, width_all = latents.shape
    tokens_here = micro_count * row_count
    columns = class_table.shape[1]
    owner = lax.axis_index("fsdp")
    seq_count = lax.axis_size("seq")
    fsdp_count = lax.axis_size("fsdp")
    class_range = jnp.arange(class_table.shape[0], dtype=jnp.int32)
    one_hot = (class_ids[:, None] == class_range[None, :]).astype(jnp.bfloat16)
    looked_up = jnp.dot(one_hot, class_table, preferred_element_type=jnp.float32)
    timing = lax.dynamic_slice_in_dim(
        time_features(timesteps, width_all), owner * columns, columns, 1
    )
    condition = looked_up + timing
    lifted_full, lift_pull = jax.vjp(lift_silu, condition)
    lifted = lifted_full.astype(jnp.bfloat16)
    mod_width = w_mod.shape[1]
    mod_cols = b_mod.shape[0]
    bias_line = lax.dynamic_update_slice_in_dim(
        jnp.zeros((mod_width,), jnp.float32), b_mod.astype(jnp.float32), owner * mod_cols, 0
    )
    modulation = lax.psum_scatter(
        jnp.dot(lifted, w_mod, preferred_element_type=jnp.float32) + bias_line[None, :],
        "fsdp",
        scatter_dimension=0,
        tiled=True,
    )
    mod_parts = [
        modulation[:, None, position * width_all : (position + 1) * width_all]
        for position in range(6)
    ]
    shift_one, scale_one, gate_one, shift_two, scale_two, gate_two = mod_parts
    gathered = (
        lax.all_gather(w_qkv, "fsdp", axis=0, tiled=True),
        lax.all_gather(b_q, "fsdp", axis=0, tiled=True),
        lax.all_gather(b_v, "fsdp", axis=0, tiled=True),
        lax.all_gather(w_out, "fsdp", axis=0, tiled=True),
        lax.all_gather(b_out, "fsdp", axis=0, tiled=True),
        lax.all_gather(w_fc1, "fsdp", axis=0, tiled=True),
        lax.all_gather(b_fc1, "fsdp", axis=0, tiled=True),
        lax.all_gather(w_fc2, "fsdp", axis=0, tiled=True),
        lax.all_gather(b_fc2, "fsdp", axis=0, tiled=True),
    )
    (
        full_qkv,
        query_bias,
        value_bias,
        full_out,
        out_bias,
        full_fc1,
        up_bias,
        gathered_down_weight,
        down_bias,
    ) = gathered
    ratio = gathered_down_weight.shape[0] // width_all
    inputs_full = latents.astype(jnp.float32)
    normed_one, inverse_one = normalize_keep(inputs_full)
    entry_one = (
        (normed_one * (1.0 + scale_one) + shift_one)
        .astype(jnp.bfloat16)
        .reshape(tokens_here, width_all)
    )
    projected = jnp.dot(entry_one, full_qkv, preferred_element_type=jnp.float32)
    token_shape = (micro_count, row_count, width_all)
    queries = (
        (projected[:, :width_all] + query_bias.astype(jnp.float32))
        .astype(jnp.bfloat16)
        .reshape(token_shape)
    )
    keys_here = projected[:, width_all : 2 * width_all].astype(jnp.bfloat16).reshape(token_shape)
    values_here = (
        (projected[:, 2 * width_all :] + value_bias.astype(jnp.float32))
        .astype(jnp.bfloat16)
        .reshape(token_shape)
    )
    head_queries, head_keys, head_values = (
        lax.all_to_all(queries, "seq", split_axis=2, concat_axis=1, tiled=True),
        lax.all_to_all(keys_here, "seq", split_axis=2, concat_axis=1, tiled=True),
        lax.all_to_all(values_here, "seq", split_axis=2, concat_axis=1, tiled=True),
    )
    block_rows = min(1024, head_queries.shape[1])

    def attend_one(trio):
        return attend_heads(trio[0], trio[1], trio[2], block_rows)

    head_mixed, log_totals = lax.map(attend_one, (head_queries, head_keys, head_values))
    token_mixed = lax.all_to_all(
        head_mixed, "seq", split_axis=1, concat_axis=2, tiled=True
    ).reshape(tokens_here, width_all)
    branch_one = (
        jnp.dot(token_mixed, full_out, preferred_element_type=jnp.float32)
        + out_bias.astype(jnp.float32)
    ).reshape(token_shape)
    middle = inputs_full + gate_one * branch_one
    normed_two, inverse_two = normalize_keep(middle)
    entry_two = (
        (normed_two * (1.0 + scale_two) + shift_two)
        .astype(jnp.bfloat16)
        .reshape(tokens_here, width_all)
    )
    hidden = jnp.dot(entry_two, full_fc1, preferred_element_type=jnp.float32) + up_bias.astype(
        jnp.float32
    )
    active_full, gelu_pull = jax.vjp(gelu_tanh, hidden)
    active = active_full.astype(jnp.bfloat16)
    branch_two = (
        jnp.dot(active, gathered_down_weight, preferred_element_type=jnp.float32)
        + down_bias.astype(jnp.float32)
    ).reshape(token_shape)
    result = (middle + gate_two * branch_two).astype(jnp.bfloat16)
    grad_output = out_cotangent.astype(jnp.float32)
    grad_gate_two = jnp.sum(grad_output * branch_two, axis=1)
    grad_branch_two = (gate_two * grad_output).astype(jnp.bfloat16).reshape(tokens_here, width_all)
    grad_active = compared_with(grad_branch_two, gathered_down_weight)
    grad_hidden = gelu_pull(grad_active)[0].astype(jnp.bfloat16)
    grad_entry_two = compared_with(grad_hidden, full_fc1).reshape(token_shape)
    grad_shift_two = jnp.sum(grad_entry_two, axis=1)
    grad_scale_two = jnp.sum(grad_entry_two * normed_two, axis=1)
    grad_middle = grad_output + normalize_back(
        grad_entry_two * (1.0 + scale_two), normed_two, inverse_two
    )
    grad_gate_one = jnp.sum(grad_middle * branch_one, axis=1)
    grad_branch_one = (gate_one * grad_middle).astype(jnp.bfloat16).reshape(tokens_here, width_all)
    grad_mixed = compared_with(grad_branch_one, full_out).astype(jnp.bfloat16).reshape(token_shape)
    head_grads = lax.all_to_all(grad_mixed, "seq", split_axis=2, concat_axis=1, tiled=True)

    def back_one(grouped):
        return attend_back(grouped[0], grouped[1], grouped[2], grouped[3], grouped[4], block_rows)

    grad_heads_q, grad_heads_k, grad_heads_v = lax.map(
        back_one, (head_queries, head_keys, head_values, head_grads, log_totals)
    )
    grad_queries, grad_keys, grad_values = (
        lax.all_to_all(grad_heads_q, "seq", split_axis=1, concat_axis=2, tiled=True),
        lax.all_to_all(grad_heads_k, "seq", split_axis=1, concat_axis=2, tiled=True),
        lax.all_to_all(grad_heads_v, "seq", split_axis=1, concat_axis=2, tiled=True),
    )
    grad_project = jnp.concatenate([grad_queries, grad_keys, grad_values], axis=2).reshape(
        tokens_here, 3 * width_all
    )
    grad_entry_one = compared_with(grad_project, full_qkv).reshape(token_shape)
    grad_shift_one = jnp.sum(grad_entry_one, axis=1)
    grad_scale_one = jnp.sum(grad_entry_one * normed_one, axis=1)
    grad_latents = grad_middle + normalize_back(
        grad_entry_one * (1.0 + scale_one), normed_one, inverse_one
    )
    grad_mod_part = jnp.concatenate(
        [
            grad_shift_one,
            grad_scale_one,
            grad_gate_one,
            grad_shift_two,
            grad_scale_two,
            grad_gate_two,
        ],
        axis=1,
    )
    grad_mod_seq = lax.psum(grad_mod_part, "seq").astype(jnp.bfloat16)
    grad_mod_all = lax.all_gather(grad_mod_seq, "fsdp", axis=0, tiled=True)
    grad_w_mod = outer_sum(lifted, grad_mod_all)
    grad_b_mod = jnp.sum(
        lax.dynamic_slice_in_dim(grad_mod_all, owner * mod_cols, mod_cols, 1).astype(jnp.float32),
        axis=0,
    )
    grad_lifted = compared_with(grad_mod_all, w_mod)
    grad_condition = lift_pull(grad_lifted)[0]
    grad_table = jnp.dot(
        one_hot.astype(jnp.float32).T,
        grad_condition,
        precision=lax.Precision.HIGHEST,
        preferred_element_type=jnp.float32,
    )
    grad_q_bias = jnp.sum(grad_project[:, :width_all].astype(jnp.float32), axis=0)
    grad_v_bias = jnp.sum(grad_project[:, 2 * width_all :].astype(jnp.float32), axis=0)
    grad_out_bias = jnp.sum(grad_branch_one.astype(jnp.float32), axis=0)
    grad_up_bias = jnp.sum(grad_hidden.astype(jnp.float32), axis=0)
    grad_down_bias = jnp.sum(grad_branch_two.astype(jnp.float32), axis=0)
    rights = (grad_project, grad_branch_one, grad_hidden, grad_branch_two)
    lefts = (
        regroup(entry_one, 1, fsdp_count, seq_count),
        regroup(token_mixed, 1, fsdp_count, seq_count),
        regroup(entry_two, 1, fsdp_count, seq_count),
        regroup(active, 1, fsdp_count, seq_count),
    )
    wide_term = make_term(lefts, rights, ratio)
    wide = lax.psum_scatter(
        wide_term(
            jnp.int32(0), width_all // (fsdp_count * seq_count) * lax.axis_size(("seq", "fsdp"))
        ),
        ("seq", "fsdp"),
        scatter_dimension=0,
        tiled=True,
    )
    biases = (
        lax.psum_scatter(
            regroup(grad_q_bias, 0, fsdp_count, seq_count),
            ("seq", "fsdp"),
            scatter_dimension=0,
            tiled=True,
        ),
        lax.psum_scatter(
            regroup(grad_v_bias, 0, fsdp_count, seq_count),
            ("seq", "fsdp"),
            scatter_dimension=0,
            tiled=True,
        ),
        lax.psum_scatter(
            regroup(grad_out_bias, 0, fsdp_count, seq_count),
            ("seq", "fsdp"),
            scatter_dimension=0,
            tiled=True,
        ),
        lax.psum_scatter(
            regroup(grad_up_bias, 0, fsdp_count, seq_count),
            ("seq", "fsdp"),
            scatter_dimension=0,
            tiled=True,
        ),
        lax.psum_scatter(
            regroup(grad_down_bias, 0, fsdp_count, seq_count),
            ("seq", "fsdp"),
            scatter_dimension=0,
            tiled=True,
        ),
    )
    owned = (
        lax.all_gather(wide, "seq", axis=0, tiled=True),
        lax.all_gather(biases[0], "seq", axis=0, tiled=True),
        lax.all_gather(biases[1], "seq", axis=0, tiled=True),
        lax.all_gather(biases[2], "seq", axis=0, tiled=True),
        lax.all_gather(biases[3], "seq", axis=0, tiled=True),
        lax.all_gather(biases[4], "seq", axis=0, tiled=True),
    )
    wide_owned = owned[0]
    ff_width = full_fc1.shape[1]
    grad_w_qkv = wide_owned[:, : 3 * width_all]
    grad_w_out = wide_owned[:, 3 * width_all : 4 * width_all]
    grad_w_fc1 = wide_owned[:, 4 * width_all : 4 * width_all + ff_width]
    grad_w_fc2 = wide_owned[:, 4 * width_all + ff_width :].reshape(-1, width_all)
    return (
        result,
        grad_latents,
        grad_table,
        grad_w_mod,
        grad_b_mod,
        grad_w_qkv,
        owned[1],
        owned[2],
        grad_w_out,
        owned[3],
        grad_w_fc1,
        owned[4],
        grad_w_fc2,
        owned[5],
    )


def attend_kernel(q_ref, k_ref, v_ref, o_ref, lse_ref):
    for head in range(2):
        at = slice(head * HEAD_DIM, (head + 1) * HEAD_DIM)
        queries = q_ref[:, at] * jnp.bfloat16(HEAD_DIM ** (-0.5))
        scores = compared_with(k_ref[:, at], queries)
        highest = jnp.max(scores, axis=0, keepdims=True)
        powers = jnp.exp(scores - highest)
        totals = jnp.sum(powers, axis=0, keepdims=True)
        probs = (powers * (1.0 / totals)).astype(jnp.bfloat16)
        mixed = jnp.dot(v_ref[:, at].T, probs, preferred_element_type=jnp.float32)
        o_ref[:, at] = mixed.T.astype(jnp.bfloat16)
        lse_ref[0, head : head + 1, :] = highest + jnp.log(totals)


def attend_back_kernel(q_ref, k_ref, v_ref, do_ref, lse_ref, dq_ref, dk_ref, dv_ref):
    for head in range(2):
        at = slice(head * HEAD_DIM, (head + 1) * HEAD_DIM)
        queries = q_ref[:, at] * jnp.bfloat16(HEAD_DIM ** (-0.5))
        keys = k_ref[:, at]
        grad_mixed = do_ref[:, at]
        probs = jnp.exp(compared_with(keys, queries) - lse_ref[0, head : head + 1, :])
        dv_ref[:, at] = jnp.dot(
            probs.astype(jnp.bfloat16), grad_mixed, preferred_element_type=jnp.float32
        ).astype(jnp.bfloat16)
        grad_probs = compared_with(v_ref[:, at], grad_mixed)
        inner = jnp.sum(grad_probs * probs, axis=0, keepdims=True)
        grad_scores = (probs * (grad_probs - inner)).astype(jnp.bfloat16)
        dk_ref[:, at] = jnp.dot(
            grad_scores, queries, preferred_element_type=jnp.float32
        ).astype(jnp.bfloat16)
        scaled_keys = keys * jnp.bfloat16(HEAD_DIM ** (-0.5))
        grad_queries = jnp.dot(scaled_keys.T, grad_scores, preferred_element_type=jnp.float32)
        dq_ref[:, at] = grad_queries.T.astype(jnp.bfloat16)


VMEM_LIMIT = 48 * 1024 * 1024


def attend_local(projected):
    length, wide = projected.shape
    pairs = wide // 3 // 128

    def part(which):
        return pl.BlockSpec((length, 128), lambda i: (0, which * pairs + i))

    cost = pl.CostEstimate(
        flops=16 * pairs * length * length * 128,
        bytes_accessed=length * wide * 3,
        transcendentals=2 * pairs * length * length,
    )
    return pl.pallas_call(
        attend_kernel,
        grid=(pairs,),
        in_specs=[part(0), part(1), part(2)],
        out_specs=[part(0), pl.BlockSpec((1, 2, length), lambda i: (i, 0, 0))],
        out_shape=[
            jax.ShapeDtypeStruct((length, wide // 3), jnp.bfloat16),
            jax.ShapeDtypeStruct((pairs, 2, length), jnp.float32),
        ],
        compiler_params=pltpu.CompilerParams(vmem_limit_bytes=VMEM_LIMIT),
        cost_estimate=cost,
        name="attend",
    )(projected, projected, projected)


def attend_local_back(projected, grad_mixed, log_totals):
    length, wide = projected.shape
    pairs = wide // 3 // 128

    def part(which):
        return pl.BlockSpec((length, 128), lambda i: (0, which * pairs + i))

    cost = pl.CostEstimate(
        flops=40 * pairs * length * length * 128,
        bytes_accessed=length * wide * 6,
        transcendentals=2 * pairs * length * length,
    )
    grads = jax.ShapeDtypeStruct((length, wide // 3), jnp.bfloat16)
    return pl.pallas_call(
        attend_back_kernel,
        grid=(pairs,),
        in_specs=[
            part(0),
            part(1),
            part(2),
            part(0),
            pl.BlockSpec((1, 2, length), lambda i: (i, 0, 0)),
        ],
        out_specs=[part(0), part(0), part(0)],
        out_shape=[grads, grads, grads],
        compiler_params=pltpu.CompilerParams(vmem_limit_bytes=VMEM_LIMIT),
        cost_estimate=cost,
        name="attend_back",
    )(projected, projected, projected, grad_mixed, log_totals)


def swapped_pairs(count, bit):
    return [(place, place ^ bit) for place in range(count)]


def assemble_kernel(p00, p01, p10, p11, out_ref, sems):
    owner = lax.axis_index("fsdp")
    core_at = lax.rem(owner, 2)
    x_at = lax.rem(lax.div(owner, 2), 2)
    copies = []
    for place, (piece, flip_x, flip_core) in enumerate(
        ((p00, 0, 0), (p01, 0, 1), (p10, 1, 0), (p11, 1, 1))
    ):
        to_x = 1 - x_at if flip_x else x_at
        to_core = 1 - core_at if flip_core else core_at
        copies.append(
            pltpu.make_async_copy(piece, out_ref.at[:, to_x * 2 + to_core], sems.at[place])
        )
    for copy in copies:
        copy.start()
    for copy in copies:
        copy.wait()


def gather_rows(weight):
    rows, columns = weight.shape
    count = lax.axis_size("fsdp")
    depth = count // 4
    z_groups = [[base + 4 * step for step in range(depth)] for base in range(4)]
    own = lax.all_gather(weight, "fsdp", axis=0, tiled=False, axis_index_groups=z_groups)
    across = lax.ppermute(own, "fsdp", swapped_pairs(count, 2))
    own_core = lax.ppermute(own, "fsdp", swapped_pairs(count, 1))
    across_core = lax.ppermute(across, "fsdp", swapped_pairs(count, 1))
    anywhere = pl.BlockSpec(memory_space=pl.ANY)
    whole = pl.pallas_call(
        assemble_kernel,
        in_specs=[anywhere] * 4,
        out_specs=anywhere,
        out_shape=jax.ShapeDtypeStruct((depth, 4, rows, columns), weight.dtype),
        scratch_shapes=[pltpu.SemaphoreType.DMA((4,))],
        cost_estimate=pl.CostEstimate(
            flops=0, bytes_accessed=16 * depth * rows * columns, transcendentals=0
        ),
        name="assemble",
    )(own, own_core, across, across_core)
    return whole.reshape(count * rows, columns)


def low(tensor):
    return tensor.astype(jnp.bfloat16)


def wide(tensor):
    return tensor.astype(jnp.float32)


def reduce_rows(partial):
    count = lax.axis_size("fsdp")
    depth = count // 4
    owner = lax.axis_index("fsdp")
    core_at = lax.rem(owner, 2)
    x_at = lax.rem(lax.div(owner, 2), 2)
    z_at = lax.div(owner, 4)
    columns = partial.shape[1]
    blocks = low(partial).reshape(depth, 2, 2, partial.shape[0] // count, columns)

    def pick(tensor, axis, place):
        return lax.dynamic_index_in_dim(tensor, place, axis, keepdims=False)

    arrived = lax.ppermute(pick(blocks, 2, 1 - core_at), "fsdp", swapped_pairs(count, 1))
    kept = pick(blocks, 2, core_at)
    away = low(wide(pick(kept, 1, 1 - x_at)) + wide(pick(arrived, 1, 1 - x_at)))
    crossed = lax.ppermute(away, "fsdp", swapped_pairs(count, 2))
    here = wide(pick(kept, 1, x_at)) + wide(pick(arrived, 1, x_at))
    total = pick(here, 0, z_at) + wide(pick(crossed, 0, z_at))
    for shift in range(1, depth):
        target = lax.rem(z_at + shift, depth)
        leaving = low(pick(here, 0, target) + wide(pick(crossed, 0, target)))
        pairs = [(place, (place + 4 * shift) % count) for place in range(count)]
        total = total + wide(lax.ppermute(leaving, "fsdp", pairs))
    mine = low(total)
    return wide(mine) + wide(lax.ppermute(mine, "seq", swapped_pairs(2, 1)))


def local_whole_latent(
    latents,
    timesteps,
    class_ids,
    class_table,
    w_mod,
    b_mod,
    w_qkv,
    b_q,
    b_v,
    w_out,
    b_out,
    w_fc1,
    b_fc1,
    w_fc2,
    b_fc2,
    out_cotangent,
):
    rows_here, width_all = latents.shape[1:]
    columns = class_table.shape[1]
    owner = lax.axis_index("fsdp")
    mine = lax.axis_index("seq")
    fsdp_count = lax.axis_size("fsdp")
    seq_swap = swapped_pairs(2, 1)

    def whole_latent(pair):
        kept = lax.dynamic_index_in_dim(pair, mine, 0, keepdims=False)
        given = lax.dynamic_index_in_dim(pair, 1 - mine, 0, keepdims=False)
        return jnp.concatenate([kept, lax.ppermute(given, "seq", seq_swap)], axis=0)

    def both_halves(tokens):
        given = lax.ppermute(tokens[rows_here:], "seq", seq_swap)
        kept = tokens[:rows_here]
        first = jnp.where(mine == 0, kept, given)
        second = jnp.where(mine == 0, given, kept)
        return jnp.stack([first, second], axis=0)

    class_range = jnp.arange(class_table.shape[0], dtype=jnp.int32)
    one_hot = (class_ids[:, None] == class_range[None, :]).astype(jnp.bfloat16)
    looked_up = jnp.dot(one_hot, class_table, preferred_element_type=jnp.float32)
    timing = lax.dynamic_slice_in_dim(
        time_features(timesteps, width_all), owner * columns, columns, 1
    )
    condition = looked_up + timing
    lifted_full, lift_pull = jax.vjp(lift_silu, condition)
    lifted = lifted_full.astype(jnp.bfloat16)
    mod_width = w_mod.shape[1]
    mod_cols = b_mod.shape[0]
    bias_line = lax.dynamic_update_slice_in_dim(
        jnp.zeros((mod_width,), jnp.float32), b_mod.astype(jnp.float32), owner * mod_cols, 0
    )
    lifted_mine = lax.dynamic_index_in_dim(
        lifted.reshape(fsdp_count, 2, columns), mine, 1, keepdims=False
    )
    small = [b_q, b_v, b_out, b_fc1, b_fc2]
    small_line = wide(jnp.concatenate(small))
    to_owners = jnp.concatenate(
        [
            jnp.dot(lifted_mine, w_mod, preferred_element_type=jnp.float32) + bias_line[None, :],
            jnp.broadcast_to(small_line[None, :], (fsdp_count, small_line.shape[0])),
        ],
        axis=1,
    )
    from_owners = lax.all_to_all(to_owners, "fsdp", 0, 0, tiled=True)
    modulation = jnp.sum(from_owners[:, :mod_width], axis=0, keepdims=True)
    shift_one, scale_one, gate_one, shift_two, scale_two, gate_two = [
        modulation[:, position * width_all : (position + 1) * width_all] for position in range(6)
    ]
    biases = []
    begin = mod_width
    for part in small:
        end = begin + part.shape[0]
        biases.append(from_owners[:, begin:end].reshape(1, -1))
        begin = end
    query_bias, value_bias, out_bias, up_bias, down_bias = biases

    full_qkv = gather_rows(w_qkv)
    full_out = gather_rows(w_out)
    full_fc1 = gather_rows(w_fc1)
    full_fc2 = gather_rows(w_fc2)

    inputs_full = whole_latent(latents).astype(jnp.float32)
    grad_output = whole_latent(out_cotangent).astype(jnp.float32)
    normed_one, inverse_one = normalize_keep(inputs_full)
    entry_one = low(normed_one * (1.0 + scale_one) + shift_one)
    qkv_bias = jnp.concatenate([query_bias, jnp.zeros_like(query_bias), value_bias], axis=1)
    projected = low(jnp.dot(entry_one, full_qkv, preferred_element_type=jnp.float32) + qkv_bias)
    mixed, log_totals = attend_local(projected)
    branch_one = jnp.dot(mixed, full_out, preferred_element_type=jnp.float32) + out_bias
    middle = inputs_full + gate_one * branch_one
    normed_two, inverse_two = normalize_keep(middle)
    entry_two = low(normed_two * (1.0 + scale_two) + shift_two)
    hidden = jnp.dot(entry_two, full_fc1, preferred_element_type=jnp.float32) + up_bias
    active_full, gelu_pull = jax.vjp(gelu_tanh, hidden)
    active = low(active_full)
    grad_branch_two = low(gate_two * grad_output)
    sum_fc2 = reduce_rows(outer_sum(active, grad_branch_two))
    branch_two = jnp.dot(active, full_fc2, preferred_element_type=jnp.float32) + down_bias
    result = both_halves(low(middle + gate_two * branch_two))
    grad_gate_two = jnp.sum(grad_output * branch_two, axis=0, keepdims=True)
    grad_active = compared_with(grad_branch_two, full_fc2)
    grad_hidden = low(gelu_pull(grad_active)[0])
    sum_fc1 = reduce_rows(outer_sum(entry_two, grad_hidden))
    grad_entry_two = compared_with(grad_hidden, full_fc1)
    grad_shift_two = jnp.sum(grad_entry_two, axis=0, keepdims=True)
    grad_scale_two = jnp.sum(grad_entry_two * normed_two, axis=0, keepdims=True)
    grad_middle = grad_output + normalize_back(
        grad_entry_two * (1.0 + scale_two), normed_two, inverse_two
    )
    grad_gate_one = jnp.sum(grad_middle * branch_one, axis=0, keepdims=True)
    grad_branch_one = low(gate_one * grad_middle)
    sum_out = reduce_rows(outer_sum(mixed, grad_branch_one))
    grad_mixed = low(compared_with(grad_branch_one, full_out))
    grad_project = jnp.concatenate(attend_local_back(projected, grad_mixed, log_totals), axis=1)
    sum_qkv = reduce_rows(outer_sum(entry_one, grad_project))
    grad_entry_one = compared_with(grad_project, full_qkv)
    grad_shift_one = jnp.sum(grad_entry_one, axis=0, keepdims=True)
    grad_scale_one = jnp.sum(grad_entry_one * normed_one, axis=0, keepdims=True)
    grad_latents = both_halves(
        grad_middle
        + normalize_back(grad_entry_one * (1.0 + scale_one), normed_one, inverse_one)
    )
    grad_mod_mine = low(
        jnp.concatenate(
            [
                grad_shift_one,
                grad_scale_one,
                grad_gate_one,
                grad_shift_two,
                grad_scale_two,
                grad_gate_two,
            ],
            axis=1,
        )
    )
    grad_mod_all = lax.all_gather(grad_mod_mine, ("fsdp", "seq"), axis=0, tiled=True)
    grad_w_mod = outer_sum(lifted, grad_mod_all)
    grad_b_mod = jnp.sum(
        lax.dynamic_slice_in_dim(grad_mod_all, owner * mod_cols, mod_cols, 1).astype(jnp.float32),
        axis=0,
    )
    grad_lifted = compared_with(grad_mod_all, w_mod)
    grad_condition = lift_pull(grad_lifted)[0]
    grad_table = jnp.dot(
        one_hot.astype(jnp.float32).T,
        grad_condition,
        precision=lax.Precision.HIGHEST,
        preferred_element_type=jnp.float32,
    )
    grad_small = [
        wide(grad_project[:, :width_all]),
        wide(grad_project[:, 2 * width_all :]),
        wide(grad_branch_one),
        wide(grad_hidden),
        wide(grad_branch_two),
    ]
    small_sums = jnp.concatenate(
        [jnp.sum(part, axis=0).reshape(fsdp_count, -1) for part in grad_small], axis=1
    )
    small_here = jnp.sum(
        lax.all_to_all(small_sums, "fsdp", 0, 0, tiled=True), axis=0, keepdims=True
    )
    small_total = (small_here + lax.ppermute(small_here, "seq", seq_swap))[0]
    small_grads = []
    begin = 0
    for part in small:
        small_grads.append(small_total[begin : begin + part.shape[0]])
        begin += part.shape[0]
    return (
        result,
        grad_latents,
        grad_table,
        grad_w_mod,
        grad_b_mod,
        sum_qkv,
        small_grads[0],
        small_grads[1],
        sum_out,
        small_grads[2],
        sum_fc1,
        small_grads[3],
        sum_fc2,
        small_grads[4],
    )


def solution(mesh):
    placed = (
        P("fsdp", "seq", None),
        P(),
        P(),
        P(None, "fsdp"),
        P("fsdp", None),
        P("fsdp"),
        P("fsdp", None),
        P("fsdp"),
        P("fsdp"),
        P("fsdp", None),
        P("fsdp"),
        P("fsdp", None),
        P("fsdp"),
        P("fsdp", None),
        P("fsdp"),
        P("fsdp", "seq", None),
    )
    spans = mesh.shape["fsdp"]

    def body(*arrays):
        whole_fits = arrays[0].shape[0] == mesh.shape["seq"] == 2 and spans % 4 == 0
        return (local_whole_latent if whole_fits else local)(*arrays)

    return jax.shard_map(
        body,
        mesh=mesh,
        in_specs=placed,
        out_specs=(
            P("fsdp", "seq", None),
            P("fsdp", "seq", None),
            P(None, "fsdp"),
            P("fsdp", None),
            P("fsdp"),
            P("fsdp", None),
            P("fsdp"),
            P("fsdp"),
            P("fsdp", None),
            P("fsdp"),
            P("fsdp", None),
            P("fsdp"),
            P("fsdp", None),
            P("fsdp"),
        ),
        check_vma=False,
    )
```

```python
import math

import jax
import jax.numpy as jnp
from jax import lax
from jax.experimental import pallas as pl
from jax.experimental.pallas import tpu as pltpu
from jax.sharding import PartitionSpec as P

HEAD_DIM = 64


def time_features(step_ids, columns):
    half_width = columns // 2
    freqs = jnp.exp(-math.log(10000.0) * jnp.arange(half_width, dtype=jnp.float32) / half_width)
    angles = step_ids.astype(jnp.float32)[:, None] * freqs[None, :]
    return jnp.concatenate([jnp.cos(angles), jnp.sin(angles)], axis=1)


def normalize_keep(tensor):
    centered = tensor - jnp.mean(tensor, axis=-1, keepdims=True)
    variance = jnp.mean(centered * centered, axis=-1, keepdims=True)
    inverse = lax.rsqrt(variance + 1e-06)
    return (centered * inverse, inverse)


def normalize_back(grad_hat, normed, inverse):
    mean_grad = jnp.mean(grad_hat, axis=-1, keepdims=True)
    mean_cross = jnp.mean(grad_hat * normed, axis=-1, keepdims=True)
    return inverse * (grad_hat - mean_grad - normed * mean_cross)


def gelu_tanh(tensor):
    return (
        0.5
        * tensor
        * (1.0 + jnp.tanh(0.7978845608028654 * (tensor + 0.044715 * tensor * tensor * tensor)))
    )


def lift_silu(tensor):
    return tensor * jax.nn.sigmoid(tensor)


def outer_sum(earlier_value, latter):
    return lax.dot_general(
        earlier_value, latter, (((0,), (0,)), ((), ())), preferred_element_type=jnp.float32
    )


def compared_with(earlier_value, latter):
    return lax.dot_general(
        earlier_value, latter, (((1,), (1,)), ((), ())), preferred_element_type=jnp.float32
    )


def regroup(tensor, axis_pos, outer_count, inner_count):
    extents = tensor.shape
    splitted = (
        extents[:axis_pos]
        + (outer_count, inner_count, extents[axis_pos] // (outer_count * inner_count))
        + extents[axis_pos + 1 :]
    )
    swapped = jnp.swapaxes(tensor.reshape(splitted), axis_pos, axis_pos + 1)
    return swapped.reshape(extents)


def make_term(lefts, rights, ratio):
    first_left, second_left, third_left, fourth_left = lefts
    first_right, second_right, third_right, fourth_right = rights

    def term(start, count):
        qkv_part = outer_sum(first_left, first_right)
        out_part = outer_sum(second_left, second_right)
        fc1_part = outer_sum(third_left, third_right)
        fc2_part = outer_sum(fourth_left, fourth_right).reshape(
            count, ratio * fourth_right.shape[1]
        )
        return jnp.concatenate([qkv_part, out_part, fc1_part, fc2_part], axis=1)

    return term


def attend_heads(queries, keys_all, values_all, block_rows):
    length_all = queries.shape[0]
    head_count = queries.shape[1] // HEAD_DIM
    scaling = HEAD_DIM ** (-0.5)
    query_blocks = queries.reshape(length_all // block_rows, block_rows, head_count, HEAD_DIM)
    key_heads = keys_all.reshape(length_all, head_count, HEAD_DIM)
    value_heads = values_all.reshape(length_all, head_count, HEAD_DIM)

    def one_block(query_block):
        scores = (
            jnp.einsum("qhd,khd->hqk", query_block, key_heads, preferred_element_type=jnp.float32)
            * scaling
        )
        highest = jnp.max(scores, axis=-1, keepdims=True)
        powers = jnp.exp(scores - highest)
        totals = jnp.sum(powers, axis=-1, keepdims=True)
        weight_tensors = (powers / totals).astype(jnp.bfloat16)
        mixed = jnp.einsum(
            "hqk,khd->qhd", weight_tensors, value_heads, preferred_element_type=jnp.float32
        )
        return (mixed.astype(jnp.bfloat16), (highest + jnp.log(totals))[:, :, 0])

    mixed, log_totals = lax.map(one_block, query_blocks)
    return (mixed.reshape(length_all, head_count * HEAD_DIM), log_totals)


def attend_back(queries, keys_all, values_all, grad_mixed, log_totals, block_rows):
    length_all = queries.shape[0]
    head_count = queries.shape[1] // HEAD_DIM
    scaling = HEAD_DIM ** (-0.5)
    block_count = length_all // block_rows
    query_blocks = queries.reshape(block_count, block_rows, head_count, HEAD_DIM)
    grad_blocks = grad_mixed.reshape(block_count, block_rows, head_count, HEAD_DIM)
    key_heads = keys_all.reshape(length_all, head_count, HEAD_DIM)
    value_heads = values_all.reshape(length_all, head_count, HEAD_DIM)

    def one_block(carried, blocked):
        grad_keys, grad_values = carried
        query_block, grad_block, log_block = blocked
        scores = (
            jnp.einsum("qhd,khd->hqk", query_block, key_heads, preferred_element_type=jnp.float32)
            * scaling
        )
        probs = jnp.exp(scores - log_block[:, :, None])
        grad_values = grad_values + jnp.einsum(
            "hqk,qhd->khd",
            probs.astype(jnp.bfloat16),
            grad_block,
            preferred_element_type=jnp.float32,
        )
        grad_probs = jnp.einsum(
            "qhd,khd->hqk", grad_block, value_heads, preferred_element_type=jnp.float32
        )
        grad_scores = (
            probs * (grad_probs - jnp.sum(grad_probs * probs, axis=-1, keepdims=True))
        ).astype(jnp.bfloat16)
        grad_query = (
            jnp.einsum("hqk,khd->qhd", grad_scores, key_heads, preferred_element_type=jnp.float32)
            * scaling
        )
        grad_keys = (
            grad_keys
            + jnp.einsum(
                "hqk,qhd->khd", grad_scores, query_block, preferred_element_type=jnp.float32
            )
            * scaling
        )
        return ((grad_keys, grad_values), grad_query.astype(jnp.bfloat16))

    zeroed = jnp.zeros((length_all, head_count, HEAD_DIM), jnp.float32)
    (grad_keys, grad_values), grad_queries = lax.scan(
        one_block, (zeroed, zeroed), (query_blocks, grad_blocks, log_totals)
    )
    flat_width = head_count * HEAD_DIM
    return (
        grad_queries.reshape(length_all, flat_width),
        grad_keys.reshape(length_all, flat_width).astype(jnp.bfloat16),
        grad_values.reshape(length_all, flat_width).astype(jnp.bfloat16),
    )


def local(
    latents,
    timesteps,
    class_ids,
    class_table,
    w_mod,
    b_mod,
    w_qkv,
    b_q,
    b_v,
    w_out,
    b_out,
    w_fc1,
    b_fc1,
    w_fc2,
    b_fc2,
    out_cotangent,
):
    micro_count, row_count, width_all = latents.shape
    tokens_here = micro_count * row_count
    columns = class_table.shape[1]
    owner = lax.axis_index("fsdp")
    seq_count = lax.axis_size("seq")
    fsdp_count = lax.axis_size("fsdp")
    class_range = jnp.arange(class_table.shape[0], dtype=jnp.int32)
    one_hot = (class_ids[:, None] == class_range[None, :]).astype(jnp.bfloat16)
    looked_up = jnp.dot(one_hot, class_table, preferred_element_type=jnp.float32)
    timing = lax.dynamic_slice_in_dim(
        time_features(timesteps, width_all), owner * columns, columns, 1
    )
    condition = looked_up + timing
    lifted_full, lift_pull = jax.vjp(lift_silu, condition)
    lifted = lifted_full.astype(jnp.bfloat16)
    mod_width = w_mod.shape[1]
    mod_cols = b_mod.shape[0]
    bias_line = lax.dynamic_update_slice_in_dim(
        jnp.zeros((mod_width,), jnp.float32), b_mod.astype(jnp.float32), owner * mod_cols, 0
    )
    modulation = lax.psum_scatter(
        jnp.dot(lifted, w_mod, preferred_element_type=jnp.float32) + bias_line[None, :],
        "fsdp",
        scatter_dimension=0,
        tiled=True,
    )
    mod_parts = [
        modulation[:, None, position * width_all : (position + 1) * width_all]
        for position in range(6)
    ]
    shift_one, scale_one, gate_one, shift_two, scale_two, gate_two = mod_parts
    gathered = (
        lax.all_gather(w_qkv, "fsdp", axis=0, tiled=True),
        lax.all_gather(b_q, "fsdp", axis=0, tiled=True),
        lax.all_gather(b_v, "fsdp", axis=0, tiled=True),
        lax.all_gather(w_out, "fsdp", axis=0, tiled=True),
        lax.all_gather(b_out, "fsdp", axis=0, tiled=True),
        lax.all_gather(w_fc1, "fsdp", axis=0, tiled=True),
        lax.all_gather(b_fc1, "fsdp", axis=0, tiled=True),
        lax.all_gather(w_fc2, "fsdp", axis=0, tiled=True),
        lax.all_gather(b_fc2, "fsdp", axis=0, tiled=True),
    )
    (
        full_qkv,
        query_bias,
        value_bias,
        full_out,
        out_bias,
        full_fc1,
        up_bias,
        gathered_down_weight,
        down_bias,
    ) = gathered
    ratio = gathered_down_weight.shape[0] // width_all
    inputs_full = latents.astype(jnp.float32)
    normed_one, inverse_one = normalize_keep(inputs_full)
    entry_one = (
        (normed_one * (1.0 + scale_one) + shift_one)
        .astype(jnp.bfloat16)
        .reshape(tokens_here, width_all)
    )
    projected = jnp.dot(entry_one, full_qkv, preferred_element_type=jnp.float32)
    token_shape = (micro_count, row_count, width_all)
    queries = (
        (projected[:, :width_all] + query_bias.astype(jnp.float32))
        .astype(jnp.bfloat16)
        .reshape(token_shape)
    )
    keys_here = projected[:, width_all : 2 * width_all].astype(jnp.bfloat16).reshape(token_shape)
    values_here = (
        (projected[:, 2 * width_all :] + value_bias.astype(jnp.float32))
        .astype(jnp.bfloat16)
        .reshape(token_shape)
    )
    head_queries, head_keys, head_values = (
        lax.all_to_all(queries, "seq", split_axis=2, concat_axis=1, tiled=True),
        lax.all_to_all(keys_here, "seq", split_axis=2, concat_axis=1, tiled=True),
        lax.all_to_all(values_here, "seq", split_axis=2, concat_axis=1, tiled=True),
    )
    block_rows = min(1024, head_queries.shape[1])

    def attend_one(trio):
        return attend_heads(trio[0], trio[1], trio[2], block_rows)

    head_mixed, log_totals = lax.map(attend_one, (head_queries, head_keys, head_values))
    token_mixed = lax.all_to_all(
        head_mixed, "seq", split_axis=1, concat_axis=2, tiled=True
    ).reshape(tokens_here, width_all)
    branch_one = (
        jnp.dot(token_mixed, full_out, preferred_element_type=jnp.float32)
        + out_bias.astype(jnp.float32)
    ).reshape(token_shape)
    middle = inputs_full + gate_one * branch_one
    normed_two, inverse_two = normalize_keep(middle)
    entry_two = (
        (normed_two * (1.0 + scale_two) + shift_two)
        .astype(jnp.bfloat16)
        .reshape(tokens_here, width_all)
    )
    hidden = jnp.dot(entry_two, full_fc1, preferred_element_type=jnp.float32) + up_bias.astype(
        jnp.float32
    )
    active_full, gelu_pull = jax.vjp(gelu_tanh, hidden)
    active = active_full.astype(jnp.bfloat16)
    branch_two = (
        jnp.dot(active, gathered_down_weight, preferred_element_type=jnp.float32)
        + down_bias.astype(jnp.float32)
    ).reshape(token_shape)
    result = (middle + gate_two * branch_two).astype(jnp.bfloat16)
    grad_output = out_cotangent.astype(jnp.float32)
    grad_gate_two = jnp.sum(grad_output * branch_two, axis=1)
    grad_branch_two = (gate_two * grad_output).astype(jnp.bfloat16).reshape(tokens_here, width_all)
    grad_active = compared_with(grad_branch_two, gathered_down_weight)
    grad_hidden = gelu_pull(grad_active)[0].astype(jnp.bfloat16)
    grad_entry_two = compared_with(grad_hidden, full_fc1).reshape(token_shape)
    grad_shift_two = jnp.sum(grad_entry_two, axis=1)
    grad_scale_two = jnp.sum(grad_entry_two * normed_two, axis=1)
    grad_middle = grad_output + normalize_back(
        grad_entry_two * (1.0 + scale_two), normed_two, inverse_two
    )
    grad_gate_one = jnp.sum(grad_middle * branch_one, axis=1)
    grad_branch_one = (gate_one * grad_middle).astype(jnp.bfloat16).reshape(tokens_here, width_all)
    grad_mixed = compared_with(grad_branch_one, full_out).astype(jnp.bfloat16).reshape(token_shape)
    head_grads = lax.all_to_all(grad_mixed, "seq", split_axis=2, concat_axis=1, tiled=True)

    def back_one(grouped):
        return attend_back(grouped[0], grouped[1], grouped[2], grouped[3], grouped[4], block_rows)

    grad_heads_q, grad_heads_k, grad_heads_v = lax.map(
        back_one, (head_queries, head_keys, head_values, head_grads, log_totals)
    )
    grad_queries, grad_keys, grad_values = (
        lax.all_to_all(grad_heads_q, "seq", split_axis=1, concat_axis=2, tiled=True),
        lax.all_to_all(grad_heads_k, "seq", split_axis=1, concat_axis=2, tiled=True),
        lax.all_to_all(grad_heads_v, "seq", split_axis=1, concat_axis=2, tiled=True),
    )
    grad_project = jnp.concatenate([grad_queries, grad_keys, grad_values], axis=2).reshape(
        tokens_here, 3 * width_all
    )
    grad_entry_one = compared_with(grad_project, full_qkv).reshape(token_shape)
    grad_shift_one = jnp.sum(grad_entry_one, axis=1)
    grad_scale_one = jnp.sum(grad_entry_one * normed_one, axis=1)
    grad_latents = grad_middle + normalize_back(
        grad_entry_one * (1.0 + scale_one), normed_one, inverse_one
    )
    grad_mod_part = jnp.concatenate(
        [
            grad_shift_one,
            grad_scale_one,
            grad_gate_one,
            grad_shift_two,
            grad_scale_two,
            grad_gate_two,
        ],
        axis=1,
    )
    grad_mod_seq = lax.psum(grad_mod_part, "seq").astype(jnp.bfloat16)
    grad_mod_all = lax.all_gather(grad_mod_seq, "fsdp", axis=0, tiled=True)
    grad_w_mod = outer_sum(lifted, grad_mod_all)
    grad_b_mod = jnp.sum(
        lax.dynamic_slice_in_dim(grad_mod_all, owner * mod_cols, mod_cols, 1).astype(jnp.float32),
        axis=0,
    )
    grad_lifted = compared_with(grad_mod_all, w_mod)
    grad_condition = lift_pull(grad_lifted)[0]
    grad_table = jnp.dot(
        one_hot.astype(jnp.float32).T,
        grad_condition,
        precision=lax.Precision.HIGHEST,
        preferred_element_type=jnp.float32,
    )
    grad_q_bias = jnp.sum(grad_project[:, :width_all].astype(jnp.float32), axis=0)
    grad_v_bias = jnp.sum(grad_project[:, 2 * width_all :].astype(jnp.float32), axis=0)
    grad_out_bias = jnp.sum(grad_branch_one.astype(jnp.float32), axis=0)
    grad_up_bias = jnp.sum(grad_hidden.astype(jnp.float32), axis=0)
    grad_down_bias = jnp.sum(grad_branch_two.astype(jnp.float32), axis=0)
    rights = (grad_project, grad_branch_one, grad_hidden, grad_branch_two)
    lefts = (
        regroup(entry_one, 1, fsdp_count, seq_count),
        regroup(token_mixed, 1, fsdp_count, seq_count),
        regroup(entry_two, 1, fsdp_count, seq_count),
        regroup(active, 1, fsdp_count, seq_count),
    )
    wide_term = make_term(lefts, rights, ratio)
    wide = lax.psum_scatter(
        wide_term(
            jnp.int32(0), width_all // (fsdp_count * seq_count) * lax.axis_size(("seq", "fsdp"))
        ),
        ("seq", "fsdp"),
        scatter_dimension=0,
        tiled=True,
    )
    biases = (
        lax.psum_scatter(
            regroup(grad_q_bias, 0, fsdp_count, seq_count),
            ("seq", "fsdp"),
            scatter_dimension=0,
            tiled=True,
        ),
        lax.psum_scatter(
            regroup(grad_v_bias, 0, fsdp_count, seq_count),
            ("seq", "fsdp"),
            scatter_dimension=0,
            tiled=True,
        ),
        lax.psum_scatter(
            regroup(grad_out_bias, 0, fsdp_count, seq_count),
            ("seq", "fsdp"),
            scatter_dimension=0,
            tiled=True,
        ),
        lax.psum_scatter(
            regroup(grad_up_bias, 0, fsdp_count, seq_count),
            ("seq", "fsdp"),
            scatter_dimension=0,
            tiled=True,
        ),
        lax.psum_scatter(
            regroup(grad_down_bias, 0, fsdp_count, seq_count),
            ("seq", "fsdp"),
            scatter_dimension=0,
            tiled=True,
        ),
    )
    owned = (
        lax.all_gather(wide, "seq", axis=0, tiled=True),
        lax.all_gather(biases[0], "seq", axis=0, tiled=True),
        lax.all_gather(biases[1], "seq", axis=0, tiled=True),
        lax.all_gather(biases[2], "seq", axis=0, tiled=True),
        lax.all_gather(biases[3], "seq", axis=0, tiled=True),
        lax.all_gather(biases[4], "seq", axis=0, tiled=True),
    )
    wide_owned = owned[0]
    ff_width = full_fc1.shape[1]
    grad_w_qkv = wide_owned[:, : 3 * width_all]
    grad_w_out = wide_owned[:, 3 * width_all : 4 * width_all]
    grad_w_fc1 = wide_owned[:, 4 * width_all : 4 * width_all + ff_width]
    grad_w_fc2 = wide_owned[:, 4 * width_all + ff_width :].reshape(-1, width_all)
    return (
        result,
        grad_latents,
        grad_table,
        grad_w_mod,
        grad_b_mod,
        grad_w_qkv,
        owned[1],
        owned[2],
        grad_w_out,
        owned[3],
        grad_w_fc1,
        owned[4],
        grad_w_fc2,
        owned[5],
    )


def attend_kernel(q_ref, k_ref, v_ref, o_ref, lse_ref):
    for head in range(2):
        at = slice(head * HEAD_DIM, (head + 1) * HEAD_DIM)
        queries = q_ref[:, at] * jnp.bfloat16(HEAD_DIM ** (-0.5))
        scores = compared_with(k_ref[:, at], queries)
        highest = jnp.max(scores, axis=0, keepdims=True)
        powers = jnp.exp(scores - highest)
        totals = jnp.sum(powers, axis=0, keepdims=True)
        probs = (powers * (1.0 / totals)).astype(jnp.bfloat16)
        mixed = jnp.dot(v_ref[:, at].T, probs, preferred_element_type=jnp.float32)
        o_ref[:, at] = mixed.T.astype(jnp.bfloat16)
        lse_ref[0, head : head + 1, :] = highest + jnp.log(totals)


def attend_back_kernel(q_ref, k_ref, v_ref, do_ref, lse_ref, dq_ref, dk_ref, dv_ref):
    for head in range(2):
        at = slice(head * HEAD_DIM, (head + 1) * HEAD_DIM)
        queries = q_ref[:, at] * jnp.bfloat16(HEAD_DIM ** (-0.5))
        keys = k_ref[:, at]
        grad_mixed = do_ref[:, at]
        probs = jnp.exp(compared_with(keys, queries) - lse_ref[0, head : head + 1, :])
        dv_ref[:, at] = jnp.dot(
            probs.astype(jnp.bfloat16), grad_mixed, preferred_element_type=jnp.float32
        ).astype(jnp.bfloat16)
        grad_probs = compared_with(v_ref[:, at], grad_mixed)
        inner = jnp.sum(grad_probs * probs, axis=0, keepdims=True)
        grad_scores = (probs * (grad_probs - inner)).astype(jnp.bfloat16)
        dk_ref[:, at] = jnp.dot(
            grad_scores, queries, preferred_element_type=jnp.float32
        ).astype(jnp.bfloat16)
        scaled_keys = keys * jnp.bfloat16(HEAD_DIM ** (-0.5))
        grad_queries = jnp.dot(scaled_keys.T, grad_scores, preferred_element_type=jnp.float32)
        dq_ref[:, at] = grad_queries.T.astype(jnp.bfloat16)


VMEM_LIMIT = 48 * 1024 * 1024


def attend_local(projected):
    length, wide = projected.shape
    pairs = wide // 3 // 128

    def part(which):
        return pl.BlockSpec((length, 128), lambda i: (0, which * pairs + i))

    cost = pl.CostEstimate(
        flops=16 * pairs * length * length * 128,
        bytes_accessed=length * wide * 3,
        transcendentals=2 * pairs * length * length,
    )
    return pl.pallas_call(
        attend_kernel,
        grid=(pairs,),
        in_specs=[part(0), part(1), part(2)],
        out_specs=[part(0), pl.BlockSpec((1, 2, length), lambda i: (i, 0, 0))],
        out_shape=[
            jax.ShapeDtypeStruct((length, wide // 3), jnp.bfloat16),
            jax.ShapeDtypeStruct((pairs, 2, length), jnp.float32),
        ],
        compiler_params=pltpu.CompilerParams(vmem_limit_bytes=VMEM_LIMIT),
        cost_estimate=cost,
        name="attend",
    )(projected, projected, projected)


def attend_local_back(projected, grad_mixed, log_totals):
    length, wide = projected.shape
    pairs = wide // 3 // 128

    def part(which):
        return pl.BlockSpec((length, 128), lambda i: (0, which * pairs + i))

    cost = pl.CostEstimate(
        flops=40 * pairs * length * length * 128,
        bytes_accessed=length * wide * 6,
        transcendentals=2 * pairs * length * length,
    )
    grads = jax.ShapeDtypeStruct((length, wide // 3), jnp.bfloat16)
    return pl.pallas_call(
        attend_back_kernel,
        grid=(pairs,),
        in_specs=[
            part(0),
            part(1),
            part(2),
            part(0),
            pl.BlockSpec((1, 2, length), lambda i: (i, 0, 0)),
        ],
        out_specs=[part(0), part(0), part(0)],
        out_shape=[grads, grads, grads],
        compiler_params=pltpu.CompilerParams(vmem_limit_bytes=VMEM_LIMIT),
        cost_estimate=cost,
        name="attend_back",
    )(projected, projected, projected, grad_mixed, log_totals)


def swapped_pairs(count, bit):
    return [(place, place ^ bit) for place in range(count)]


def assemble_kernel(place_ref, p00, p01, p10, p11, *out_refs):
    del place_ref
    for which, piece in enumerate((p00, p01, p10, p11)):

        @pl.when(pl.program_id(0) == which)
        def _():
            begin = 0
            for out_ref in out_refs:
                end = begin + out_ref.shape[-1]
                out_ref[0, 0] = piece[0, :, begin:end]
                begin = end


def gather_rows(weight, *widths):
    rows, columns = weight.shape
    count = lax.axis_size("fsdp")
    depth = count // 4
    owner = lax.axis_index("fsdp")
    z_groups = [[base + 4 * step for step in range(depth)] for base in range(4)]
    own = lax.all_gather(weight, "fsdp", axis=0, tiled=False, axis_index_groups=z_groups)
    across = lax.ppermute(own, "fsdp", swapped_pairs(count, 2))
    own_core = lax.ppermute(own, "fsdp", swapped_pairs(count, 1))
    across_core = lax.ppermute(across, "fsdp", swapped_pairs(count, 1))
    places = jnp.bitwise_xor(lax.rem(owner, 4), jnp.arange(4, dtype=jnp.int32))

    def piece_spec(which):
        def block(p, z, place_ref):
            del place_ref
            return (jnp.where(p == which, z, jnp.where(p < which, 0, depth - 1)), 0, 0)

        return pl.BlockSpec((1, rows, columns), block)

    def out_block(p, z, place_ref):
        return (z, place_ref[p], 0, 0)

    whole = pl.pallas_call(
        assemble_kernel,
        grid_spec=pltpu.PrefetchScalarGridSpec(
            num_scalar_prefetch=1,
            grid=(4, depth),
            in_specs=[piece_spec(which) for which in range(4)],
            out_specs=[pl.BlockSpec((1, 1, rows, width), out_block) for width in widths],
        ),
        out_shape=[
            jax.ShapeDtypeStruct((depth, 4, rows, width), weight.dtype) for width in widths
        ],
        compiler_params=pltpu.CompilerParams(vmem_limit_bytes=VMEM_LIMIT),
        cost_estimate=pl.CostEstimate(
            flops=0, bytes_accessed=16 * depth * rows * columns, transcendentals=0
        ),
        name="assemble",
    )(places, own, own_core, across, across_core)
    return [part.reshape(count * rows, -1) for part in whole]


def gather_latents(line):
    count = lax.axis_size("fsdp")
    depth = count // 4
    owner = lax.axis_index("fsdp")
    z_at = lax.div(owner, 4)

    def doubled(tensor, place, axis, other):
        first = jnp.where(place == 0, tensor, other)
        second = jnp.where(place == 0, other, tensor)
        return jnp.stack([first, second], axis=axis)

    tensor = doubled(
        line, lax.axis_index("seq"), 0, lax.ppermute(line, "seq", swapped_pairs(2, 1))
    )
    tensor = doubled(
        tensor, lax.rem(owner, 2), 0, lax.ppermute(tensor, "fsdp", swapped_pairs(count, 1))
    )
    tensor = doubled(
        tensor,
        lax.rem(lax.div(owner, 2), 2),
        0,
        lax.ppermute(tensor, "fsdp", swapped_pairs(count, 2)),
    )
    tensor = tensor.reshape(8, -1)
    slots = [tensor]
    for shift in range(1, depth):
        pairs = [(place, (place + 4 * shift) % count) for place in range(count)]
        slots.append(lax.ppermute(tensor, "fsdp", pairs))
    ordered = []
    for z in range(depth):
        shift = lax.rem(z_at - z + depth, depth)
        chosen = slots[0]
        for step in range(1, depth):
            chosen = jnp.where(shift == step, slots[step], chosen)
        ordered.append(chosen)
    return jnp.concatenate(ordered, axis=0)


def low(tensor):
    return tensor.astype(jnp.bfloat16)


def wide(tensor):
    return tensor.astype(jnp.float32)


def pick(tensor, axis, place):
    return lax.dynamic_index_in_dim(tensor, place, axis, keepdims=False)


def reduce_begin(partial):
    count = lax.axis_size("fsdp")
    core_at = lax.rem(lax.axis_index("fsdp"), 2)
    rows, columns = partial.shape
    blocks = low(partial).reshape(count // 4, 2, 2, rows // count, columns)
    return pick(blocks, 2, core_at), pick(blocks, 2, 1 - core_at)


def reduce_end(kept, leaving):
    count = lax.axis_size("fsdp")
    depth = count // 4
    owner = lax.axis_index("fsdp")
    x_at = lax.rem(lax.div(owner, 2), 2)
    z_at = lax.div(owner, 4)
    arrived = lax.ppermute(leaving, "fsdp", swapped_pairs(count, 1))
    away = low(wide(pick(kept, 1, 1 - x_at)) + wide(pick(arrived, 1, 1 - x_at)))
    crossed = lax.ppermute(away, "fsdp", swapped_pairs(count, 2))
    here = wide(pick(kept, 1, x_at)) + wide(pick(arrived, 1, x_at))
    total = pick(here, 0, z_at) + wide(pick(crossed, 0, z_at))
    for shift in range(1, depth):
        target = lax.rem(z_at + shift, depth)
        leaving = low(pick(here, 0, target) + wide(pick(crossed, 0, target)))
        pairs = [(place, (place + 4 * shift) % count) for place in range(count)]
        total = total + wide(lax.ppermute(leaving, "fsdp", pairs))
    mine = low(total)
    return wide(mine) + wide(lax.ppermute(mine, "seq", swapped_pairs(2, 1)))


def local_whole_latent(
    latents,
    timesteps,
    class_ids,
    class_table,
    w_mod,
    b_mod,
    w_qkv,
    b_q,
    b_v,
    w_out,
    b_out,
    w_fc1,
    b_fc1,
    w_fc2,
    b_fc2,
    out_cotangent,
):
    rows_here, width_all = latents.shape[1:]
    columns = class_table.shape[1]
    owner = lax.axis_index("fsdp")
    mine = lax.axis_index("seq")
    fsdp_count = lax.axis_size("fsdp")
    seq_swap = swapped_pairs(2, 1)

    def whole_latent(pair):
        kept = lax.dynamic_index_in_dim(pair, mine, 0, keepdims=False)
        given = lax.dynamic_index_in_dim(pair, 1 - mine, 0, keepdims=False)
        return jnp.concatenate([kept, lax.ppermute(given, "seq", seq_swap)], axis=0)

    def both_halves(tokens):
        given = lax.ppermute(tokens[rows_here:], "seq", seq_swap)
        kept = tokens[:rows_here]
        first = jnp.where(mine == 0, kept, given)
        second = jnp.where(mine == 0, given, kept)
        return jnp.stack([first, second], axis=0)

    class_range = jnp.arange(class_table.shape[0], dtype=jnp.int32)
    one_hot = (class_ids[:, None] == class_range[None, :]).astype(jnp.bfloat16)
    looked_up = jnp.dot(one_hot, class_table, preferred_element_type=jnp.float32)
    timing = lax.dynamic_slice_in_dim(
        time_features(timesteps, width_all), owner * columns, columns, 1
    )
    condition = looked_up + timing
    lifted_full, lift_pull = jax.vjp(lift_silu, condition)
    lifted = lifted_full.astype(jnp.bfloat16)
    mod_width = w_mod.shape[1]
    mod_cols = b_mod.shape[0]
    bias_line = lax.dynamic_update_slice_in_dim(
        jnp.zeros((mod_width,), jnp.float32), b_mod.astype(jnp.float32), owner * mod_cols, 0
    )
    lifted_mine = lax.dynamic_index_in_dim(
        lifted.reshape(fsdp_count, 2, columns), mine, 1, keepdims=False
    )
    small = [b_q, b_v, b_out, b_fc1, b_fc2]
    small_line = wide(jnp.concatenate(small))
    to_owners = jnp.concatenate(
        [
            jnp.dot(lifted_mine, w_mod, preferred_element_type=jnp.float32) + bias_line[None, :],
            jnp.broadcast_to(small_line[None, :], (fsdp_count, small_line.shape[0])),
        ],
        axis=1,
    )
    from_owners = lax.all_to_all(to_owners, "fsdp", 0, 0, tiled=True)
    modulation = jnp.sum(from_owners[:, :mod_width], axis=0, keepdims=True)
    shift_one, scale_one, gate_one, shift_two, scale_two, gate_two = [
        modulation[:, position * width_all : (position + 1) * width_all] for position in range(6)
    ]
    biases = []
    begin = mod_width
    for part in small:
        end = begin + part.shape[0]
        biases.append(from_owners[:, begin:end].reshape(1, -1))
        begin = end
    query_bias, value_bias, out_bias, up_bias, down_bias = biases

    full_qkv, full_out = gather_rows(
        jnp.concatenate([w_qkv, w_out], axis=1), w_qkv.shape[1], w_out.shape[1]
    )
    (full_fc1,) = gather_rows(w_fc1, w_fc1.shape[1])
    (full_fc2,) = gather_rows(w_fc2, w_fc2.shape[1])

    inputs_full = whole_latent(latents).astype(jnp.float32)
    grad_output = whole_latent(out_cotangent).astype(jnp.float32)
    normed_one, inverse_one = normalize_keep(inputs_full)
    entry_one = low(normed_one * (1.0 + scale_one) + shift_one)
    qkv_bias = jnp.concatenate([query_bias, jnp.zeros_like(query_bias), value_bias], axis=1)
    projected = low(jnp.dot(entry_one, full_qkv, preferred_element_type=jnp.float32) + qkv_bias)
    mixed, log_totals = attend_local(projected)
    branch_one = jnp.dot(mixed, full_out, preferred_element_type=jnp.float32) + out_bias
    middle = inputs_full + gate_one * branch_one
    normed_two, inverse_two = normalize_keep(middle)
    entry_two = low(normed_two * (1.0 + scale_two) + shift_two)
    hidden = jnp.dot(entry_two, full_fc1, preferred_element_type=jnp.float32) + up_bias
    active_full, gelu_pull = jax.vjp(gelu_tanh, hidden)
    active = low(active_full)
    grad_branch_two = low(gate_two * grad_output)
    kept_fc2, leaving_fc2 = reduce_begin(outer_sum(active, grad_branch_two))
    active, grad_branch_two, leaving_fc2 = lax.optimization_barrier(
        (active, grad_branch_two, leaving_fc2)
    )
    sum_fc2 = reduce_end(kept_fc2, leaving_fc2)
    branch_two = jnp.dot(active, full_fc2, preferred_element_type=jnp.float32) + down_bias
    result = both_halves(low(middle + gate_two * branch_two))
    grad_gate_two = jnp.sum(grad_output * branch_two, axis=0, keepdims=True)
    grad_active = compared_with(grad_branch_two, full_fc2)
    grad_hidden = low(gelu_pull(grad_active)[0])
    kept_fc1, leaving_fc1 = reduce_begin(outer_sum(entry_two, grad_hidden))
    grad_hidden, leaving_fc1 = lax.optimization_barrier((grad_hidden, leaving_fc1))
    sum_fc1 = reduce_end(kept_fc1, leaving_fc1)
    grad_entry_two = compared_with(grad_hidden, full_fc1)
    grad_shift_two = jnp.sum(grad_entry_two, axis=0, keepdims=True)
    grad_scale_two = jnp.sum(grad_entry_two * normed_two, axis=0, keepdims=True)
    grad_middle = grad_output + normalize_back(
        grad_entry_two * (1.0 + scale_two), normed_two, inverse_two
    )
    grad_gate_one = jnp.sum(grad_middle * branch_one, axis=0, keepdims=True)
    grad_mod_early = gather_latents(
        low(
            jnp.concatenate(
                [grad_gate_one, grad_shift_two, grad_scale_two, grad_gate_two], axis=1
            )
        )
    )
    grad_branch_one = low(gate_one * grad_middle)
    kept_out, leaving_out = reduce_begin(outer_sum(mixed, grad_branch_one))
    grad_branch_one, leaving_out = lax.optimization_barrier((grad_branch_one, leaving_out))
    sum_out = reduce_end(kept_out, leaving_out)
    grad_mixed = low(compared_with(grad_branch_one, full_out))
    grad_project = jnp.concatenate(attend_local_back(projected, grad_mixed, log_totals), axis=1)
    kept_qkv, leaving_qkv = reduce_begin(outer_sum(entry_one, grad_project))
    grad_project, leaving_qkv = lax.optimization_barrier((grad_project, leaving_qkv))
    sum_qkv = reduce_end(kept_qkv, leaving_qkv)
    grad_entry_one = compared_with(grad_project, full_qkv)
    grad_shift_one = jnp.sum(grad_entry_one, axis=0, keepdims=True)
    grad_scale_one = jnp.sum(grad_entry_one * normed_one, axis=0, keepdims=True)
    grad_latents = both_halves(
        grad_middle
        + normalize_back(grad_entry_one * (1.0 + scale_one), normed_one, inverse_one)
    )
    grad_mod_late = low(jnp.concatenate([grad_shift_one, grad_scale_one], axis=1))
    grad_mod_all = jnp.concatenate([gather_latents(grad_mod_late), grad_mod_early], axis=1)
    grad_w_mod = outer_sum(lifted, grad_mod_all)
    grad_b_mod = jnp.sum(
        lax.dynamic_slice_in_dim(grad_mod_all, owner * mod_cols, mod_cols, 1).astype(jnp.float32),
        axis=0,
    )
    grad_lifted = compared_with(grad_mod_all, w_mod)
    grad_condition = lift_pull(grad_lifted)[0]
    grad_table = jnp.dot(
        one_hot.astype(jnp.float32).T,
        grad_condition,
        precision=lax.Precision.HIGHEST,
        preferred_element_type=jnp.float32,
    )
    grad_small = [
        wide(grad_project[:, :width_all]),
        wide(grad_project[:, 2 * width_all :]),
        wide(grad_branch_one),
        wide(grad_hidden),
        wide(grad_branch_two),
    ]
    small_sums = jnp.concatenate(
        [jnp.sum(part, axis=0).reshape(fsdp_count, -1) for part in grad_small], axis=1
    )
    small_here = jnp.sum(
        lax.all_to_all(small_sums, "fsdp", 0, 0, tiled=True), axis=0, keepdims=True
    )
    small_total = (small_here + lax.ppermute(small_here, "seq", seq_swap))[0]
    small_grads = []
    begin = 0
    for part in small:
        small_grads.append(small_total[begin : begin + part.shape[0]])
        begin += part.shape[0]
    return (
        result,
        grad_latents,
        grad_table,
        grad_w_mod,
        grad_b_mod,
        sum_qkv,
        small_grads[0],
        small_grads[1],
        sum_out,
        small_grads[2],
        sum_fc1,
        small_grads[3],
        sum_fc2,
        small_grads[4],
    )


def solution(mesh):
    placed = (
        P("fsdp", "seq", None),
        P(),
        P(),
        P(None, "fsdp"),
        P("fsdp", None),
        P("fsdp"),
        P("fsdp", None),
        P("fsdp"),
        P("fsdp"),
        P("fsdp", None),
        P("fsdp"),
        P("fsdp", None),
        P("fsdp"),
        P("fsdp", None),
        P("fsdp"),
        P("fsdp", "seq", None),
    )
    spans = mesh.shape["fsdp"]

    def body(*arrays):
        whole_fits = arrays[0].shape[0] == mesh.shape["seq"] == 2 and spans % 4 == 0
        return (local_whole_latent if whole_fits else local)(*arrays)

    return jax.shard_map(
        body,
        mesh=mesh,
        in_specs=placed,
        out_specs=(
            P("fsdp", "seq", None),
            P("fsdp", "seq", None),
            P(None, "fsdp"),
            P("fsdp", None),
            P("fsdp"),
            P("fsdp", None),
            P("fsdp"),
            P("fsdp"),
            P("fsdp", None),
            P("fsdp"),
            P("fsdp", None),
            P("fsdp"),
            P("fsdp", None),
            P("fsdp"),
        ),
        check_vma=False,
    )
```

```python
import math

import jax
import jax.numpy as jnp
from jax import lax
from jax.experimental import pallas as pl
from jax.experimental.pallas import tpu as pltpu
from jax.sharding import PartitionSpec as P

HEAD_DIM = 64


def time_features(step_ids, columns):
    half_width = columns // 2
    freqs = jnp.exp(-math.log(10000.0) * jnp.arange(half_width, dtype=jnp.float32) / half_width)
    angles = step_ids.astype(jnp.float32)[:, None] * freqs[None, :]
    return jnp.concatenate([jnp.cos(angles), jnp.sin(angles)], axis=1)


def normalize_keep(tensor):
    centered = tensor - jnp.mean(tensor, axis=-1, keepdims=True)
    variance = jnp.mean(centered * centered, axis=-1, keepdims=True)
    inverse = lax.rsqrt(variance + 1e-06)
    return (centered * inverse, inverse)


def normalize_back(grad_hat, normed, inverse):
    mean_grad = jnp.mean(grad_hat, axis=-1, keepdims=True)
    mean_cross = jnp.mean(grad_hat * normed, axis=-1, keepdims=True)
    return inverse * (grad_hat - mean_grad - normed * mean_cross)


def gelu_tanh(tensor):
    return (
        0.5
        * tensor
        * (1.0 + jnp.tanh(0.7978845608028654 * (tensor + 0.044715 * tensor * tensor * tensor)))
    )


def lift_silu(tensor):
    return tensor * jax.nn.sigmoid(tensor)


def outer_sum(earlier_value, latter):
    return lax.dot_general(
        earlier_value, latter, (((0,), (0,)), ((), ())), preferred_element_type=jnp.float32
    )


def compared_with(earlier_value, latter):
    return lax.dot_general(
        earlier_value, latter, (((1,), (1,)), ((), ())), preferred_element_type=jnp.float32
    )


def regroup(tensor, axis_pos, outer_count, inner_count):
    extents = tensor.shape
    splitted = (
        extents[:axis_pos]
        + (outer_count, inner_count, extents[axis_pos] // (outer_count * inner_count))
        + extents[axis_pos + 1 :]
    )
    swapped = jnp.swapaxes(tensor.reshape(splitted), axis_pos, axis_pos + 1)
    return swapped.reshape(extents)


def make_term(lefts, rights, ratio):
    first_left, second_left, third_left, fourth_left = lefts
    first_right, second_right, third_right, fourth_right = rights

    def term(start, count):
        qkv_part = outer_sum(first_left, first_right)
        out_part = outer_sum(second_left, second_right)
        fc1_part = outer_sum(third_left, third_right)
        fc2_part = outer_sum(fourth_left, fourth_right).reshape(
            count, ratio * fourth_right.shape[1]
        )
        return jnp.concatenate([qkv_part, out_part, fc1_part, fc2_part], axis=1)

    return term


def attend_heads(queries, keys_all, values_all, block_rows):
    length_all = queries.shape[0]
    head_count = queries.shape[1] // HEAD_DIM
    scaling = HEAD_DIM ** (-0.5)
    query_blocks = queries.reshape(length_all // block_rows, block_rows, head_count, HEAD_DIM)
    key_heads = keys_all.reshape(length_all, head_count, HEAD_DIM)
    value_heads = values_all.reshape(length_all, head_count, HEAD_DIM)

    def one_block(query_block):
        scores = (
            jnp.einsum("qhd,khd->hqk", query_block, key_heads, preferred_element_type=jnp.float32)
            * scaling
        )
        highest = jnp.max(scores, axis=-1, keepdims=True)
        powers = jnp.exp(scores - highest)
        totals = jnp.sum(powers, axis=-1, keepdims=True)
        weight_tensors = (powers / totals).astype(jnp.bfloat16)
        mixed = jnp.einsum(
            "hqk,khd->qhd", weight_tensors, value_heads, preferred_element_type=jnp.float32
        )
        return (mixed.astype(jnp.bfloat16), (highest + jnp.log(totals))[:, :, 0])

    mixed, log_totals = lax.map(one_block, query_blocks)
    return (mixed.reshape(length_all, head_count * HEAD_DIM), log_totals)


def attend_back(queries, keys_all, values_all, grad_mixed, log_totals, block_rows):
    length_all = queries.shape[0]
    head_count = queries.shape[1] // HEAD_DIM
    scaling = HEAD_DIM ** (-0.5)
    block_count = length_all // block_rows
    query_blocks = queries.reshape(block_count, block_rows, head_count, HEAD_DIM)
    grad_blocks = grad_mixed.reshape(block_count, block_rows, head_count, HEAD_DIM)
    key_heads = keys_all.reshape(length_all, head_count, HEAD_DIM)
    value_heads = values_all.reshape(length_all, head_count, HEAD_DIM)

    def one_block(carried, blocked):
        grad_keys, grad_values = carried
        query_block, grad_block, log_block = blocked
        scores = (
            jnp.einsum("qhd,khd->hqk", query_block, key_heads, preferred_element_type=jnp.float32)
            * scaling
        )
        probs = jnp.exp(scores - log_block[:, :, None])
        grad_values = grad_values + jnp.einsum(
            "hqk,qhd->khd",
            probs.astype(jnp.bfloat16),
            grad_block,
            preferred_element_type=jnp.float32,
        )
        grad_probs = jnp.einsum(
            "qhd,khd->hqk", grad_block, value_heads, preferred_element_type=jnp.float32
        )
        grad_scores = (
            probs * (grad_probs - jnp.sum(grad_probs * probs, axis=-1, keepdims=True))
        ).astype(jnp.bfloat16)
        grad_query = (
            jnp.einsum("hqk,khd->qhd", grad_scores, key_heads, preferred_element_type=jnp.float32)
            * scaling
        )
        grad_keys = (
            grad_keys
            + jnp.einsum(
                "hqk,qhd->khd", grad_scores, query_block, preferred_element_type=jnp.float32
            )
            * scaling
        )
        return ((grad_keys, grad_values), grad_query.astype(jnp.bfloat16))

    zeroed = jnp.zeros((length_all, head_count, HEAD_DIM), jnp.float32)
    (grad_keys, grad_values), grad_queries = lax.scan(
        one_block, (zeroed, zeroed), (query_blocks, grad_blocks, log_totals)
    )
    flat_width = head_count * HEAD_DIM
    return (
        grad_queries.reshape(length_all, flat_width),
        grad_keys.reshape(length_all, flat_width).astype(jnp.bfloat16),
        grad_values.reshape(length_all, flat_width).astype(jnp.bfloat16),
    )


def local(
    latents,
    timesteps,
    class_ids,
    class_table,
    w_mod,
    b_mod,
    w_qkv,
    b_q,
    b_v,
    w_out,
    b_out,
    w_fc1,
    b_fc1,
    w_fc2,
    b_fc2,
    out_cotangent,
):
    micro_count, row_count, width_all = latents.shape
    tokens_here = micro_count * row_count
    columns = class_table.shape[1]
    owner = lax.axis_index("fsdp")
    seq_count = lax.axis_size("seq")
    fsdp_count = lax.axis_size("fsdp")
    class_range = jnp.arange(class_table.shape[0], dtype=jnp.int32)
    one_hot = (class_ids[:, None] == class_range[None, :]).astype(jnp.bfloat16)
    looked_up = jnp.dot(one_hot, class_table, preferred_element_type=jnp.float32)
    timing = lax.dynamic_slice_in_dim(
        time_features(timesteps, width_all), owner * columns, columns, 1
    )
    condition = looked_up + timing
    lifted_full, lift_pull = jax.vjp(lift_silu, condition)
    lifted = lifted_full.astype(jnp.bfloat16)
    mod_width = w_mod.shape[1]
    mod_cols = b_mod.shape[0]
    bias_line = lax.dynamic_update_slice_in_dim(
        jnp.zeros((mod_width,), jnp.float32), b_mod.astype(jnp.float32), owner * mod_cols, 0
    )
    modulation = lax.psum_scatter(
        jnp.dot(lifted, w_mod, preferred_element_type=jnp.float32) + bias_line[None, :],
        "fsdp",
        scatter_dimension=0,
        tiled=True,
    )
    mod_parts = [
        modulation[:, None, position * width_all : (position + 1) * width_all]
        for position in range(6)
    ]
    shift_one, scale_one, gate_one, shift_two, scale_two, gate_two = mod_parts
    gathered = (
        lax.all_gather(w_qkv, "fsdp", axis=0, tiled=True),
        lax.all_gather(b_q, "fsdp", axis=0, tiled=True),
        lax.all_gather(b_v, "fsdp", axis=0, tiled=True),
        lax.all_gather(w_out, "fsdp", axis=0, tiled=True),
        lax.all_gather(b_out, "fsdp", axis=0, tiled=True),
        lax.all_gather(w_fc1, "fsdp", axis=0, tiled=True),
        lax.all_gather(b_fc1, "fsdp", axis=0, tiled=True),
        lax.all_gather(w_fc2, "fsdp", axis=0, tiled=True),
        lax.all_gather(b_fc2, "fsdp", axis=0, tiled=True),
    )
    (
        full_qkv,
        query_bias,
        value_bias,
        full_out,
        out_bias,
        full_fc1,
        up_bias,
        gathered_down_weight,
        down_bias,
    ) = gathered
    ratio = gathered_down_weight.shape[0] // width_all
    inputs_full = latents.astype(jnp.float32)
    normed_one, inverse_one = normalize_keep(inputs_full)
    entry_one = (
        (normed_one * (1.0 + scale_one) + shift_one)
        .astype(jnp.bfloat16)
        .reshape(tokens_here, width_all)
    )
    projected = jnp.dot(entry_one, full_qkv, preferred_element_type=jnp.float32)
    token_shape = (micro_count, row_count, width_all)
    queries = (
        (projected[:, :width_all] + query_bias.astype(jnp.float32))
        .astype(jnp.bfloat16)
        .reshape(token_shape)
    )
    keys_here = projected[:, width_all : 2 * width_all].astype(jnp.bfloat16).reshape(token_shape)
    values_here = (
        (projected[:, 2 * width_all :] + value_bias.astype(jnp.float32))
        .astype(jnp.bfloat16)
        .reshape(token_shape)
    )
    head_queries, head_keys, head_values = (
        lax.all_to_all(queries, "seq", split_axis=2, concat_axis=1, tiled=True),
        lax.all_to_all(keys_here, "seq", split_axis=2, concat_axis=1, tiled=True),
        lax.all_to_all(values_here, "seq", split_axis=2, concat_axis=1, tiled=True),
    )
    block_rows = min(1024, head_queries.shape[1])

    def attend_one(trio):
        return attend_heads(trio[0], trio[1], trio[2], block_rows)

    head_mixed, log_totals = lax.map(attend_one, (head_queries, head_keys, head_values))
    token_mixed = lax.all_to_all(
        head_mixed, "seq", split_axis=1, concat_axis=2, tiled=True
    ).reshape(tokens_here, width_all)
    branch_one = (
        jnp.dot(token_mixed, full_out, preferred_element_type=jnp.float32)
        + out_bias.astype(jnp.float32)
    ).reshape(token_shape)
    middle = inputs_full + gate_one * branch_one
    normed_two, inverse_two = normalize_keep(middle)
    entry_two = (
        (normed_two * (1.0 + scale_two) + shift_two)
        .astype(jnp.bfloat16)
        .reshape(tokens_here, width_all)
    )
    hidden = jnp.dot(entry_two, full_fc1, preferred_element_type=jnp.float32) + up_bias.astype(
        jnp.float32
    )
    active_full, gelu_pull = jax.vjp(gelu_tanh, hidden)
    active = active_full.astype(jnp.bfloat16)
    branch_two = (
        jnp.dot(active, gathered_down_weight, preferred_element_type=jnp.float32)
        + down_bias.astype(jnp.float32)
    ).reshape(token_shape)
    result = (middle + gate_two * branch_two).astype(jnp.bfloat16)
    grad_output = out_cotangent.astype(jnp.float32)
    grad_gate_two = jnp.sum(grad_output * branch_two, axis=1)
    grad_branch_two = (gate_two * grad_output).astype(jnp.bfloat16).reshape(tokens_here, width_all)
    grad_active = compared_with(grad_branch_two, gathered_down_weight)
    grad_hidden = gelu_pull(grad_active)[0].astype(jnp.bfloat16)
    grad_entry_two = compared_with(grad_hidden, full_fc1).reshape(token_shape)
    grad_shift_two = jnp.sum(grad_entry_two, axis=1)
    grad_scale_two = jnp.sum(grad_entry_two * normed_two, axis=1)
    grad_middle = grad_output + normalize_back(
        grad_entry_two * (1.0 + scale_two), normed_two, inverse_two
    )
    grad_gate_one = jnp.sum(grad_middle * branch_one, axis=1)
    grad_branch_one = (gate_one * grad_middle).astype(jnp.bfloat16).reshape(tokens_here, width_all)
    grad_mixed = compared_with(grad_branch_one, full_out).astype(jnp.bfloat16).reshape(token_shape)
    head_grads = lax.all_to_all(grad_mixed, "seq", split_axis=2, concat_axis=1, tiled=True)

    def back_one(grouped):
        return attend_back(grouped[0], grouped[1], grouped[2], grouped[3], grouped[4], block_rows)

    grad_heads_q, grad_heads_k, grad_heads_v = lax.map(
        back_one, (head_queries, head_keys, head_values, head_grads, log_totals)
    )
    grad_queries, grad_keys, grad_values = (
        lax.all_to_all(grad_heads_q, "seq", split_axis=1, concat_axis=2, tiled=True),
        lax.all_to_all(grad_heads_k, "seq", split_axis=1, concat_axis=2, tiled=True),
        lax.all_to_all(grad_heads_v, "seq", split_axis=1, concat_axis=2, tiled=True),
    )
    grad_project = jnp.concatenate([grad_queries, grad_keys, grad_values], axis=2).reshape(
        tokens_here, 3 * width_all
    )
    grad_entry_one = compared_with(grad_project, full_qkv).reshape(token_shape)
    grad_shift_one = jnp.sum(grad_entry_one, axis=1)
    grad_scale_one = jnp.sum(grad_entry_one * normed_one, axis=1)
    grad_latents = grad_middle + normalize_back(
        grad_entry_one * (1.0 + scale_one), normed_one, inverse_one
    )
    grad_mod_part = jnp.concatenate(
        [
            grad_shift_one,
            grad_scale_one,
            grad_gate_one,
            grad_shift_two,
            grad_scale_two,
            grad_gate_two,
        ],
        axis=1,
    )
    grad_mod_seq = lax.psum(grad_mod_part, "seq").astype(jnp.bfloat16)
    grad_mod_all = lax.all_gather(grad_mod_seq, "fsdp", axis=0, tiled=True)
    grad_w_mod = outer_sum(lifted, grad_mod_all)
    grad_b_mod = jnp.sum(
        lax.dynamic_slice_in_dim(grad_mod_all, owner * mod_cols, mod_cols, 1).astype(jnp.float32),
        axis=0,
    )
    grad_lifted = compared_with(grad_mod_all, w_mod)
    grad_condition = lift_pull(grad_lifted)[0]
    grad_table = jnp.dot(
        one_hot.astype(jnp.float32).T,
        grad_condition,
        precision=lax.Precision.HIGHEST,
        preferred_element_type=jnp.float32,
    )
    grad_q_bias = jnp.sum(grad_project[:, :width_all].astype(jnp.float32), axis=0)
    grad_v_bias = jnp.sum(grad_project[:, 2 * width_all :].astype(jnp.float32), axis=0)
    grad_out_bias = jnp.sum(grad_branch_one.astype(jnp.float32), axis=0)
    grad_up_bias = jnp.sum(grad_hidden.astype(jnp.float32), axis=0)
    grad_down_bias = jnp.sum(grad_branch_two.astype(jnp.float32), axis=0)
    rights = (grad_project, grad_branch_one, grad_hidden, grad_branch_two)
    lefts = (
        regroup(entry_one, 1, fsdp_count, seq_count),
        regroup(token_mixed, 1, fsdp_count, seq_count),
        regroup(entry_two, 1, fsdp_count, seq_count),
        regroup(active, 1, fsdp_count, seq_count),
    )
    wide_term = make_term(lefts, rights, ratio)
    wide = lax.psum_scatter(
        wide_term(
            jnp.int32(0), width_all // (fsdp_count * seq_count) * lax.axis_size(("seq", "fsdp"))
        ),
        ("seq", "fsdp"),
        scatter_dimension=0,
        tiled=True,
    )
    biases = (
        lax.psum_scatter(
            regroup(grad_q_bias, 0, fsdp_count, seq_count),
            ("seq", "fsdp"),
            scatter_dimension=0,
            tiled=True,
        ),
        lax.psum_scatter(
            regroup(grad_v_bias, 0, fsdp_count, seq_count),
            ("seq", "fsdp"),
            scatter_dimension=0,
            tiled=True,
        ),
        lax.psum_scatter(
            regroup(grad_out_bias, 0, fsdp_count, seq_count),
            ("seq", "fsdp"),
            scatter_dimension=0,
            tiled=True,
        ),
        lax.psum_scatter(
            regroup(grad_up_bias, 0, fsdp_count, seq_count),
            ("seq", "fsdp"),
            scatter_dimension=0,
            tiled=True,
        ),
        lax.psum_scatter(
            regroup(grad_down_bias, 0, fsdp_count, seq_count),
            ("seq", "fsdp"),
            scatter_dimension=0,
            tiled=True,
        ),
    )
    owned = (
        lax.all_gather(wide, "seq", axis=0, tiled=True),
        lax.all_gather(biases[0], "seq", axis=0, tiled=True),
        lax.all_gather(biases[1], "seq", axis=0, tiled=True),
        lax.all_gather(biases[2], "seq", axis=0, tiled=True),
        lax.all_gather(biases[3], "seq", axis=0, tiled=True),
        lax.all_gather(biases[4], "seq", axis=0, tiled=True),
    )
    wide_owned = owned[0]
    ff_width = full_fc1.shape[1]
    grad_w_qkv = wide_owned[:, : 3 * width_all]
    grad_w_out = wide_owned[:, 3 * width_all : 4 * width_all]
    grad_w_fc1 = wide_owned[:, 4 * width_all : 4 * width_all + ff_width]
    grad_w_fc2 = wide_owned[:, 4 * width_all + ff_width :].reshape(-1, width_all)
    return (
        result,
        grad_latents,
        grad_table,
        grad_w_mod,
        grad_b_mod,
        grad_w_qkv,
        owned[1],
        owned[2],
        grad_w_out,
        owned[3],
        grad_w_fc1,
        owned[4],
        grad_w_fc2,
        owned[5],
    )


def attend_kernel(q_ref, k_ref, v_ref, o_ref, lse_ref):
    for head in range(2):
        at = slice(head * HEAD_DIM, (head + 1) * HEAD_DIM)
        queries = q_ref[:, at] * jnp.bfloat16(HEAD_DIM ** (-0.5))
        scores = compared_with(k_ref[:, at], queries)
        highest = jnp.max(scores, axis=0, keepdims=True)
        powers = jnp.exp(scores - highest)
        totals = jnp.sum(powers, axis=0, keepdims=True)
        probs = (powers * (1.0 / totals)).astype(jnp.bfloat16)
        mixed = jnp.dot(v_ref[:, at].T, probs, preferred_element_type=jnp.float32)
        o_ref[:, at] = mixed.T.astype(jnp.bfloat16)
        lse_ref[0, head : head + 1, :] = highest + jnp.log(totals)


def attend_back_kernel(q_ref, k_ref, v_ref, do_ref, lse_ref, dq_ref, dk_ref, dv_ref):
    for head in range(2):
        at = slice(head * HEAD_DIM, (head + 1) * HEAD_DIM)
        queries = q_ref[:, at] * jnp.bfloat16(HEAD_DIM ** (-0.5))
        keys = k_ref[:, at]
        grad_mixed = do_ref[:, at]
        probs = jnp.exp(compared_with(keys, queries) - lse_ref[0, head : head + 1, :])
        dv_ref[:, at] = jnp.dot(
            probs.astype(jnp.bfloat16), grad_mixed, preferred_element_type=jnp.float32
        ).astype(jnp.bfloat16)
        grad_probs = compared_with(v_ref[:, at], grad_mixed)
        inner = jnp.sum(grad_probs * probs, axis=0, keepdims=True)
        grad_scores = (probs * (grad_probs - inner)).astype(jnp.bfloat16)
        dk_ref[:, at] = jnp.dot(
            grad_scores, queries, preferred_element_type=jnp.float32
        ).astype(jnp.bfloat16)
        scaled_keys = keys * jnp.bfloat16(HEAD_DIM ** (-0.5))
        grad_queries = jnp.dot(scaled_keys.T, grad_scores, preferred_element_type=jnp.float32)
        dq_ref[:, at] = grad_queries.T.astype(jnp.bfloat16)


VMEM_LIMIT = 48 * 1024 * 1024


def attend_local(projected):
    length, wide = projected.shape
    pairs = wide // 3 // 128

    def part(which):
        return pl.BlockSpec((length, 128), lambda i: (0, which * pairs + i))

    cost = pl.CostEstimate(
        flops=16 * pairs * length * length * 128,
        bytes_accessed=length * wide * 3,
        transcendentals=2 * pairs * length * length,
    )
    return pl.pallas_call(
        attend_kernel,
        grid=(pairs,),
        in_specs=[part(0), part(1), part(2)],
        out_specs=[part(0), pl.BlockSpec((1, 2, length), lambda i: (i, 0, 0))],
        out_shape=[
            jax.ShapeDtypeStruct((length, wide // 3), jnp.bfloat16),
            jax.ShapeDtypeStruct((pairs, 2, length), jnp.float32),
        ],
        compiler_params=pltpu.CompilerParams(vmem_limit_bytes=VMEM_LIMIT),
        cost_estimate=cost,
        name="attend",
    )(projected, projected, projected)


def attend_local_back(projected, grad_mixed, log_totals):
    length, wide = projected.shape
    pairs = wide // 3 // 128

    def part(which):
        return pl.BlockSpec((length, 128), lambda i: (0, which * pairs + i))

    cost = pl.CostEstimate(
        flops=40 * pairs * length * length * 128,
        bytes_accessed=length * wide * 6,
        transcendentals=2 * pairs * length * length,
    )
    grads = jax.ShapeDtypeStruct((length, wide // 3), jnp.bfloat16)
    return pl.pallas_call(
        attend_back_kernel,
        grid=(pairs,),
        in_specs=[
            part(0),
            part(1),
            part(2),
            part(0),
            pl.BlockSpec((1, 2, length), lambda i: (i, 0, 0)),
        ],
        out_specs=[part(0), part(0), part(0)],
        out_shape=[grads, grads, grads],
        compiler_params=pltpu.CompilerParams(vmem_limit_bytes=VMEM_LIMIT),
        cost_estimate=cost,
        name="attend_back",
    )(projected, projected, projected, grad_mixed, log_totals)


def swapped_pairs(count, bit):
    return [(place, place ^ bit) for place in range(count)]


def assemble_kernel(place_ref, p00, p01, p10, p11, *out_refs):
    del place_ref
    for which, piece in enumerate((p00, p01, p10, p11)):

        @pl.when(pl.program_id(0) == which)
        def _():
            begin = 0
            for out_ref in out_refs:
                end = begin + out_ref.shape[-1]
                out_ref[0, 0] = piece[0, :, begin:end]
                begin = end


def gather_z(weight):
    z_groups = [
        [base + 4 * step for step in range(lax.axis_size("fsdp") // 4)] for base in range(4)
    ]
    return lax.all_gather(weight, "fsdp", axis=0, tiled=False, axis_index_groups=z_groups)


def flip(tensor, bit):
    return lax.ppermute(tensor, "fsdp", swapped_pairs(lax.axis_size("fsdp"), bit))


def assemble(own, own_core, across, across_core, *widths):
    depth, rows, columns = own.shape
    count = 4 * depth
    weight = own
    owner = lax.axis_index("fsdp")
    places = jnp.bitwise_xor(lax.rem(owner, 4), jnp.arange(4, dtype=jnp.int32))

    def piece_spec(which):
        def block(p, z, place_ref):
            del place_ref
            return (jnp.where(p == which, z, jnp.where(p < which, 0, depth - 1)), 0, 0)

        return pl.BlockSpec((1, rows, columns), block)

    def out_block(p, z, place_ref):
        return (z, place_ref[p], 0, 0)

    whole = pl.pallas_call(
        assemble_kernel,
        grid_spec=pltpu.PrefetchScalarGridSpec(
            num_scalar_prefetch=1,
            grid=(4, depth),
            in_specs=[piece_spec(which) for which in range(4)],
            out_specs=[pl.BlockSpec((1, 1, rows, width), out_block) for width in widths],
        ),
        out_shape=[
            jax.ShapeDtypeStruct((depth, 4, rows, width), weight.dtype) for width in widths
        ],
        compiler_params=pltpu.CompilerParams(vmem_limit_bytes=VMEM_LIMIT),
        cost_estimate=pl.CostEstimate(
            flops=0, bytes_accessed=16 * depth * rows * columns, transcendentals=0
        ),
        name="assemble",
    )(places, own, own_core, across, across_core)
    return [part.reshape(count * rows, -1) for part in whole]


def gather_latents(line):
    count = lax.axis_size("fsdp")
    depth = count // 4
    owner = lax.axis_index("fsdp")
    z_at = lax.div(owner, 4)

    def doubled(tensor, place, axis, other):
        first = jnp.where(place == 0, tensor, other)
        second = jnp.where(place == 0, other, tensor)
        return jnp.stack([first, second], axis=axis)

    tensor = doubled(
        line, lax.axis_index("seq"), 0, lax.ppermute(line, "seq", swapped_pairs(2, 1))
    )
    tensor = doubled(
        tensor, lax.rem(owner, 2), 0, lax.ppermute(tensor, "fsdp", swapped_pairs(count, 1))
    )
    tensor = doubled(
        tensor,
        lax.rem(lax.div(owner, 2), 2),
        0,
        lax.ppermute(tensor, "fsdp", swapped_pairs(count, 2)),
    )
    tensor = tensor.reshape(8, -1)
    slots = [tensor]
    for shift in range(1, depth):
        pairs = [(place, (place + 4 * shift) % count) for place in range(count)]
        slots.append(lax.ppermute(tensor, "fsdp", pairs))
    ordered = []
    for z in range(depth):
        shift = lax.rem(z_at - z + depth, depth)
        chosen = slots[0]
        for step in range(1, depth):
            chosen = jnp.where(shift == step, slots[step], chosen)
        ordered.append(chosen)
    return jnp.concatenate(ordered, axis=0)


def low(tensor):
    return tensor.astype(jnp.bfloat16)


def wide(tensor):
    return tensor.astype(jnp.float32)


def pick(tensor, axis, place):
    return lax.dynamic_index_in_dim(tensor, place, axis, keepdims=False)


def split_core(partial):
    count = lax.axis_size("fsdp")
    core_at = lax.rem(lax.axis_index("fsdp"), 2)
    rows, columns = partial.shape
    blocks = low(partial).reshape(count // 4, 2, 2, rows // count, columns)
    return pick(blocks, 2, core_at), pick(blocks, 2, 1 - core_at)


def split_x(kept, arrived):
    x_at = lax.rem(lax.div(lax.axis_index("fsdp"), 2), 2)
    here = wide(pick(kept, 1, x_at)) + wide(pick(arrived, 1, x_at))
    return here, low(wide(pick(kept, 1, 1 - x_at)) + wide(pick(arrived, 1, 1 - x_at)))


def split_z(here, crossed):
    depth = here.shape[0]
    z_at = lax.div(lax.axis_index("fsdp"), 4)
    leaving = []
    for shift in range(1, depth):
        target = lax.rem(z_at + shift, depth)
        leaving.append(low(pick(here, 0, target) + wide(pick(crossed, 0, target))))
    return pick(here, 0, z_at) + wide(pick(crossed, 0, z_at)), leaving


def send_z(leaving):
    count = lax.axis_size("fsdp")
    arrived = []
    for shift, part in enumerate(leaving, 1):
        pairs = [(place, (place + 4 * shift) % count) for place in range(count)]
        arrived.append(lax.ppermute(part, "fsdp", pairs))
    return arrived


def sum_z(total, arrived):
    for part in arrived:
        total = total + wide(part)
    return low(total)


def sum_seq(mine):
    return wide(mine) + wide(lax.ppermute(mine, "seq", swapped_pairs(2, 1)))


tied = lax.optimization_barrier


def local_whole_latent(
    latents,
    timesteps,
    class_ids,
    class_table,
    w_mod,
    b_mod,
    w_qkv,
    b_q,
    b_v,
    w_out,
    b_out,
    w_fc1,
    b_fc1,
    w_fc2,
    b_fc2,
    out_cotangent,
):
    rows_here, width_all = latents.shape[1:]
    columns = class_table.shape[1]
    owner = lax.axis_index("fsdp")
    mine = lax.axis_index("seq")
    fsdp_count = lax.axis_size("fsdp")
    seq_swap = swapped_pairs(2, 1)

    def whole_latent(pair):
        kept = lax.dynamic_index_in_dim(pair, mine, 0, keepdims=False)
        given = lax.dynamic_index_in_dim(pair, 1 - mine, 0, keepdims=False)
        return jnp.concatenate([kept, lax.ppermute(given, "seq", seq_swap)], axis=0)

    def both_halves(tokens):
        given = lax.ppermute(tokens[rows_here:], "seq", seq_swap)
        kept = tokens[:rows_here]
        first = jnp.where(mine == 0, kept, given)
        second = jnp.where(mine == 0, given, kept)
        return jnp.stack([first, second], axis=0)

    class_range = jnp.arange(class_table.shape[0], dtype=jnp.int32)
    one_hot = (class_ids[:, None] == class_range[None, :]).astype(jnp.bfloat16)
    looked_up = jnp.dot(one_hot, class_table, preferred_element_type=jnp.float32)
    timing = lax.dynamic_slice_in_dim(
        time_features(timesteps, width_all), owner * columns, columns, 1
    )
    condition = looked_up + timing
    lifted_full, lift_pull = jax.vjp(lift_silu, condition)
    lifted = lifted_full.astype(jnp.bfloat16)
    mod_width = w_mod.shape[1]
    mod_cols = b_mod.shape[0]
    bias_line = lax.dynamic_update_slice_in_dim(
        jnp.zeros((mod_width,), jnp.float32), b_mod.astype(jnp.float32), owner * mod_cols, 0
    )
    lifted_mine = lax.dynamic_index_in_dim(
        lifted.reshape(fsdp_count, 2, columns), mine, 1, keepdims=False
    )
    small = [b_q, b_v, b_out, b_fc1, b_fc2]
    small_line = wide(jnp.concatenate(small))
    to_owners = jnp.concatenate(
        [
            jnp.dot(lifted_mine, w_mod, preferred_element_type=jnp.float32) + bias_line[None, :],
            jnp.broadcast_to(small_line[None, :], (fsdp_count, small_line.shape[0])),
        ],
        axis=1,
    )
    from_owners = lax.all_to_all(to_owners, "fsdp", 0, 0, tiled=True)
    modulation = jnp.sum(from_owners[:, :mod_width], axis=0, keepdims=True)
    shift_one, scale_one, gate_one, shift_two, scale_two, gate_two = [
        modulation[:, position * width_all : (position + 1) * width_all] for position in range(6)
    ]
    biases = []
    begin = mod_width
    for part in small:
        end = begin + part.shape[0]
        biases.append(from_owners[:, begin:end].reshape(1, -1))
        begin = end
    query_bias, value_bias, out_bias, up_bias, down_bias = biases

    own_a = gather_z(jnp.concatenate([w_qkv, w_out], axis=1))
    own_a, w_fc1 = tied((own_a, w_fc1))
    own_b = gather_z(w_fc1)
    core_a = flip(own_a, 1)
    across_a = flip(own_a, 2)

    inputs_full = whole_latent(latents).astype(jnp.float32)
    grad_output = whole_latent(out_cotangent).astype(jnp.float32)
    normed_one, inverse_one = normalize_keep(inputs_full)
    entry_one = low(normed_one * (1.0 + scale_one) + shift_one)
    entry_one, across_a = tied((entry_one, across_a))
    across_core_a = flip(across_a, 1)
    own_b, across_core_a, w_fc2 = tied((own_b, across_core_a, w_fc2))
    own_c = gather_z(w_fc2)
    core_b = flip(own_b, 1)
    across_b = flip(own_b, 2)
    full_qkv, full_out = assemble(
        own_a, core_a, across_a, across_core_a, w_qkv.shape[1], w_out.shape[1]
    )
    qkv_bias = jnp.concatenate([query_bias, jnp.zeros_like(query_bias), value_bias], axis=1)
    projected = low(jnp.dot(entry_one, full_qkv, preferred_element_type=jnp.float32) + qkv_bias)
    mixed, log_totals = attend_local(projected)
    mixed, across_b, core_b = tied((mixed, across_b, core_b))
    across_core_b = flip(across_b, 1)
    branch_one = jnp.dot(mixed, full_out, preferred_element_type=jnp.float32) + out_bias
    middle = inputs_full + gate_one * branch_one
    normed_two, inverse_two = normalize_keep(middle)
    entry_two = low(normed_two * (1.0 + scale_two) + shift_two)
    entry_two, across_core_b, own_c = tied((entry_two, across_core_b, own_c))
    core_c = flip(own_c, 1)
    across_c = flip(own_c, 2)
    (full_fc1,) = assemble(own_b, core_b, across_b, across_core_b, w_fc1.shape[1])
    hidden = jnp.dot(entry_two, full_fc1, preferred_element_type=jnp.float32) + up_bias
    active_full, gelu_pull = jax.vjp(gelu_tanh, hidden)
    active = low(active_full)
    grad_branch_two = low(gate_two * grad_output)
    kept_fc2, leaving_fc2 = split_core(outer_sum(active, grad_branch_two))
    leaving_fc2, across_c, core_c = tied((leaving_fc2, across_c, core_c))
    across_core_c = flip(across_c, 1)
    arrived_fc2 = flip(leaving_fc2, 1)
    (full_fc2,) = assemble(own_c, core_c, across_c, across_core_c, w_fc2.shape[1])
    branch_two = jnp.dot(active, full_fc2, preferred_element_type=jnp.float32) + down_bias
    result = both_halves(low(middle + gate_two * branch_two))
    grad_gate_two = jnp.sum(grad_output * branch_two, axis=0, keepdims=True)
    grad_active = compared_with(grad_branch_two, full_fc2)
    grad_hidden = low(gelu_pull(grad_active)[0])
    here_fc2, away_fc2 = split_x(kept_fc2, arrived_fc2)
    grad_hidden, away_fc2 = tied((grad_hidden, away_fc2))
    crossed_fc2 = flip(away_fc2, 2)
    kept_fc1, leaving_fc1 = split_core(outer_sum(entry_two, grad_hidden))
    grad_hidden, leaving_fc1 = tied((grad_hidden, leaving_fc1))
    arrived_fc1 = flip(leaving_fc1, 1)
    grad_entry_two = compared_with(grad_hidden, full_fc1)
    grad_shift_two = jnp.sum(grad_entry_two, axis=0, keepdims=True)
    grad_scale_two = jnp.sum(grad_entry_two * normed_two, axis=0, keepdims=True)
    grad_middle = grad_output + normalize_back(
        grad_entry_two * (1.0 + scale_two), normed_two, inverse_two
    )
    grad_gate_one = jnp.sum(grad_middle * branch_one, axis=0, keepdims=True)
    grad_mod_early = gather_latents(
        low(
            jnp.concatenate(
                [grad_gate_one, grad_shift_two, grad_scale_two, grad_gate_two], axis=1
            )
        )
    )
    grad_branch_one = low(gate_one * grad_middle)
    here_fc1, away_fc1 = split_x(kept_fc1, arrived_fc1)
    grad_branch_one, away_fc1 = tied((grad_branch_one, away_fc1))
    crossed_fc1 = flip(away_fc1, 2)
    kept_out, leaving_out = split_core(outer_sum(mixed, grad_branch_one))
    arrived_out = flip(leaving_out, 1)
    grad_mixed = low(compared_with(grad_branch_one, full_out))
    total_fc2, leaving_fc2 = split_z(here_fc2, crossed_fc2)
    here_out, away_out = split_x(kept_out, arrived_out)
    grad_mixed, leaving_fc2, away_out = tied((grad_mixed, leaving_fc2, away_out))
    landed_fc2 = send_z(leaving_fc2)
    crossed_out = flip(away_out, 2)
    grad_project = jnp.concatenate(attend_local_back(projected, grad_mixed, log_totals), axis=1)
    kept_qkv, leaving_qkv = split_core(outer_sum(entry_one, grad_project))
    grad_project, leaving_qkv = tied((grad_project, leaving_qkv))
    arrived_qkv = flip(leaving_qkv, 1)
    here_qkv, away_qkv = split_x(kept_qkv, arrived_qkv)
    grad_entry_one = compared_with(grad_project, full_qkv)
    grad_entry_one, away_qkv, here_fc1, total_fc2 = tied(
        (grad_entry_one, away_qkv, here_fc1, total_fc2)
    )
    crossed_qkv = flip(away_qkv, 2)
    total_fc1, leaving_fc1 = split_z(here_fc1, crossed_fc1)
    landed_fc1 = send_z(leaving_fc1)
    sum_fc2 = sum_seq(sum_z(total_fc2, landed_fc2))
    total_out, leaving_out = split_z(here_out, crossed_out)
    landed_out = send_z(leaving_out)
    total_qkv, leaving_qkv = split_z(here_qkv, crossed_qkv)
    landed_qkv = send_z(leaving_qkv)
    sum_fc1 = sum_seq(sum_z(total_fc1, landed_fc1))
    sum_out = sum_seq(sum_z(total_out, landed_out))
    sum_qkv = sum_seq(sum_z(total_qkv, landed_qkv))
    grad_shift_one = jnp.sum(grad_entry_one, axis=0, keepdims=True)
    grad_scale_one = jnp.sum(grad_entry_one * normed_one, axis=0, keepdims=True)
    grad_latents = both_halves(
        grad_middle
        + normalize_back(grad_entry_one * (1.0 + scale_one), normed_one, inverse_one)
    )
    grad_mod_late = low(jnp.concatenate([grad_shift_one, grad_scale_one], axis=1))
    grad_mod_all = jnp.concatenate([gather_latents(grad_mod_late), grad_mod_early], axis=1)
    grad_w_mod = outer_sum(lifted, grad_mod_all)
    grad_b_mod = jnp.sum(
        lax.dynamic_slice_in_dim(grad_mod_all, owner * mod_cols, mod_cols, 1).astype(jnp.float32),
        axis=0,
    )
    grad_lifted = compared_with(grad_mod_all, w_mod)
    grad_condition = lift_pull(grad_lifted)[0]
    grad_table = jnp.dot(
        one_hot.astype(jnp.float32).T,
        grad_condition,
        precision=lax.Precision.HIGHEST,
        preferred_element_type=jnp.float32,
    )
    grad_small = [
        wide(grad_project[:, :width_all]),
        wide(grad_project[:, 2 * width_all :]),
        wide(grad_branch_one),
        wide(grad_hidden),
        wide(grad_branch_two),
    ]
    small_sums = jnp.concatenate(
        [jnp.sum(part, axis=0).reshape(fsdp_count, -1) for part in grad_small], axis=1
    )
    small_here = jnp.sum(
        lax.all_to_all(small_sums, "fsdp", 0, 0, tiled=True), axis=0, keepdims=True
    )
    small_total = (small_here + lax.ppermute(small_here, "seq", seq_swap))[0]
    small_grads = []
    begin = 0
    for part in small:
        small_grads.append(small_total[begin : begin + part.shape[0]])
        begin += part.shape[0]
    return (
        result,
        grad_latents,
        grad_table,
        grad_w_mod,
        grad_b_mod,
        sum_qkv,
        small_grads[0],
        small_grads[1],
        sum_out,
        small_grads[2],
        sum_fc1,
        small_grads[3],
        sum_fc2,
        small_grads[4],
    )


def solution(mesh):
    placed = (
        P("fsdp", "seq", None),
        P(),
        P(),
        P(None, "fsdp"),
        P("fsdp", None),
        P("fsdp"),
        P("fsdp", None),
        P("fsdp"),
        P("fsdp"),
        P("fsdp", None),
        P("fsdp"),
        P("fsdp", None),
        P("fsdp"),
        P("fsdp", None),
        P("fsdp"),
        P("fsdp", "seq", None),
    )
    spans = mesh.shape["fsdp"]

    def body(*arrays):
        whole_fits = arrays[0].shape[0] == mesh.shape["seq"] == 2 and spans % 4 == 0
        return (local_whole_latent if whole_fits else local)(*arrays)

    return jax.shard_map(
        body,
        mesh=mesh,
        in_specs=placed,
        out_specs=(
            P("fsdp", "seq", None),
            P("fsdp", "seq", None),
            P(None, "fsdp"),
            P("fsdp", None),
            P("fsdp"),
            P("fsdp", None),
            P("fsdp"),
            P("fsdp"),
            P("fsdp", None),
            P("fsdp"),
            P("fsdp", None),
            P("fsdp"),
            P("fsdp", None),
            P("fsdp"),
        ),
        check_vma=False,
    )
```

```python
import math

import jax
import jax.numpy as jnp
from jax import lax
from jax.experimental import pallas as pl
from jax.experimental.pallas import tpu as pltpu
from jax.sharding import PartitionSpec as P

HEAD_DIM = 64


def time_features(step_ids, columns):
    half_width = columns // 2
    freqs = jnp.exp(-math.log(10000.0) * jnp.arange(half_width, dtype=jnp.float32) / half_width)
    angles = step_ids.astype(jnp.float32)[:, None] * freqs[None, :]
    return jnp.concatenate([jnp.cos(angles), jnp.sin(angles)], axis=1)


def normalize_keep(tensor):
    centered = tensor - jnp.mean(tensor, axis=-1, keepdims=True)
    variance = jnp.mean(centered * centered, axis=-1, keepdims=True)
    inverse = lax.rsqrt(variance + 1e-06)
    return (centered * inverse, inverse)


def normalize_back(grad_hat, normed, inverse):
    mean_grad = jnp.mean(grad_hat, axis=-1, keepdims=True)
    mean_cross = jnp.mean(grad_hat * normed, axis=-1, keepdims=True)
    return inverse * (grad_hat - mean_grad - normed * mean_cross)


def gelu_tanh(tensor):
    return (
        0.5
        * tensor
        * (1.0 + jnp.tanh(0.7978845608028654 * (tensor + 0.044715 * tensor * tensor * tensor)))
    )


def lift_silu(tensor):
    return tensor * jax.nn.sigmoid(tensor)


def outer_sum(earlier_value, latter):
    return lax.dot_general(
        earlier_value, latter, (((0,), (0,)), ((), ())), preferred_element_type=jnp.float32
    )


def compared_with(earlier_value, latter):
    return lax.dot_general(
        earlier_value, latter, (((1,), (1,)), ((), ())), preferred_element_type=jnp.float32
    )


def regroup(tensor, axis_pos, outer_count, inner_count):
    extents = tensor.shape
    splitted = (
        extents[:axis_pos]
        + (outer_count, inner_count, extents[axis_pos] // (outer_count * inner_count))
        + extents[axis_pos + 1 :]
    )
    swapped = jnp.swapaxes(tensor.reshape(splitted), axis_pos, axis_pos + 1)
    return swapped.reshape(extents)


def make_term(lefts, rights, ratio):
    first_left, second_left, third_left, fourth_left = lefts
    first_right, second_right, third_right, fourth_right = rights

    def term(start, count):
        qkv_part = outer_sum(first_left, first_right)
        out_part = outer_sum(second_left, second_right)
        fc1_part = outer_sum(third_left, third_right)
        fc2_part = outer_sum(fourth_left, fourth_right).reshape(
            count, ratio * fourth_right.shape[1]
        )
        return jnp.concatenate([qkv_part, out_part, fc1_part, fc2_part], axis=1)

    return term


def attend_heads(queries, keys_all, values_all, block_rows):
    length_all = queries.shape[0]
    head_count = queries.shape[1] // HEAD_DIM
    scaling = HEAD_DIM ** (-0.5)
    query_blocks = queries.reshape(length_all // block_rows, block_rows, head_count, HEAD_DIM)
    key_heads = keys_all.reshape(length_all, head_count, HEAD_DIM)
    value_heads = values_all.reshape(length_all, head_count, HEAD_DIM)

    def one_block(query_block):
        scores = (
            jnp.einsum("qhd,khd->hqk", query_block, key_heads, preferred_element_type=jnp.float32)
            * scaling
        )
        highest = jnp.max(scores, axis=-1, keepdims=True)
        powers = jnp.exp(scores - highest)
        totals = jnp.sum(powers, axis=-1, keepdims=True)
        weight_tensors = (powers / totals).astype(jnp.bfloat16)
        mixed = jnp.einsum(
            "hqk,khd->qhd", weight_tensors, value_heads, preferred_element_type=jnp.float32
        )
        return (mixed.astype(jnp.bfloat16), (highest + jnp.log(totals))[:, :, 0])

    mixed, log_totals = lax.map(one_block, query_blocks)
    return (mixed.reshape(length_all, head_count * HEAD_DIM), log_totals)


def attend_back(queries, keys_all, values_all, grad_mixed, log_totals, block_rows):
    length_all = queries.shape[0]
    head_count = queries.shape[1] // HEAD_DIM
    scaling = HEAD_DIM ** (-0.5)
    block_count = length_all // block_rows
    query_blocks = queries.reshape(block_count, block_rows, head_count, HEAD_DIM)
    grad_blocks = grad_mixed.reshape(block_count, block_rows, head_count, HEAD_DIM)
    key_heads = keys_all.reshape(length_all, head_count, HEAD_DIM)
    value_heads = values_all.reshape(length_all, head_count, HEAD_DIM)

    def one_block(carried, blocked):
        grad_keys, grad_values = carried
        query_block, grad_block, log_block = blocked
        scores = (
            jnp.einsum("qhd,khd->hqk", query_block, key_heads, preferred_element_type=jnp.float32)
            * scaling
        )
        probs = jnp.exp(scores - log_block[:, :, None])
        grad_values = grad_values + jnp.einsum(
            "hqk,qhd->khd",
            probs.astype(jnp.bfloat16),
            grad_block,
            preferred_element_type=jnp.float32,
        )
        grad_probs = jnp.einsum(
            "qhd,khd->hqk", grad_block, value_heads, preferred_element_type=jnp.float32
        )
        grad_scores = (
            probs * (grad_probs - jnp.sum(grad_probs * probs, axis=-1, keepdims=True))
        ).astype(jnp.bfloat16)
        grad_query = (
            jnp.einsum("hqk,khd->qhd", grad_scores, key_heads, preferred_element_type=jnp.float32)
            * scaling
        )
        grad_keys = (
            grad_keys
            + jnp.einsum(
                "hqk,qhd->khd", grad_scores, query_block, preferred_element_type=jnp.float32
            )
            * scaling
        )
        return ((grad_keys, grad_values), grad_query.astype(jnp.bfloat16))

    zeroed = jnp.zeros((length_all, head_count, HEAD_DIM), jnp.float32)
    (grad_keys, grad_values), grad_queries = lax.scan(
        one_block, (zeroed, zeroed), (query_blocks, grad_blocks, log_totals)
    )
    flat_width = head_count * HEAD_DIM
    return (
        grad_queries.reshape(length_all, flat_width),
        grad_keys.reshape(length_all, flat_width).astype(jnp.bfloat16),
        grad_values.reshape(length_all, flat_width).astype(jnp.bfloat16),
    )


def local(
    latents,
    timesteps,
    class_ids,
    class_table,
    w_mod,
    b_mod,
    w_qkv,
    b_q,
    b_v,
    w_out,
    b_out,
    w_fc1,
    b_fc1,
    w_fc2,
    b_fc2,
    out_cotangent,
):
    micro_count, row_count, width_all = latents.shape
    tokens_here = micro_count * row_count
    columns = class_table.shape[1]
    owner = lax.axis_index("fsdp")
    seq_count = lax.axis_size("seq")
    fsdp_count = lax.axis_size("fsdp")
    class_range = jnp.arange(class_table.shape[0], dtype=jnp.int32)
    one_hot = (class_ids[:, None] == class_range[None, :]).astype(jnp.bfloat16)
    looked_up = jnp.dot(one_hot, class_table, preferred_element_type=jnp.float32)
    timing = lax.dynamic_slice_in_dim(
        time_features(timesteps, width_all), owner * columns, columns, 1
    )
    condition = looked_up + timing
    lifted_full, lift_pull = jax.vjp(lift_silu, condition)
    lifted = lifted_full.astype(jnp.bfloat16)
    mod_width = w_mod.shape[1]
    mod_cols = b_mod.shape[0]
    bias_line = lax.dynamic_update_slice_in_dim(
        jnp.zeros((mod_width,), jnp.float32), b_mod.astype(jnp.float32), owner * mod_cols, 0
    )
    modulation = lax.psum_scatter(
        jnp.dot(lifted, w_mod, preferred_element_type=jnp.float32) + bias_line[None, :],
        "fsdp",
        scatter_dimension=0,
        tiled=True,
    )
    mod_parts = [
        modulation[:, None, position * width_all : (position + 1) * width_all]
        for position in range(6)
    ]
    shift_one, scale_one, gate_one, shift_two, scale_two, gate_two = mod_parts
    gathered = (
        lax.all_gather(w_qkv, "fsdp", axis=0, tiled=True),
        lax.all_gather(b_q, "fsdp", axis=0, tiled=True),
        lax.all_gather(b_v, "fsdp", axis=0, tiled=True),
        lax.all_gather(w_out, "fsdp", axis=0, tiled=True),
        lax.all_gather(b_out, "fsdp", axis=0, tiled=True),
        lax.all_gather(w_fc1, "fsdp", axis=0, tiled=True),
        lax.all_gather(b_fc1, "fsdp", axis=0, tiled=True),
        lax.all_gather(w_fc2, "fsdp", axis=0, tiled=True),
        lax.all_gather(b_fc2, "fsdp", axis=0, tiled=True),
    )
    (
        full_qkv,
        query_bias,
        value_bias,
        full_out,
        out_bias,
        full_fc1,
        up_bias,
        gathered_down_weight,
        down_bias,
    ) = gathered
    ratio = gathered_down_weight.shape[0] // width_all
    inputs_full = latents.astype(jnp.float32)
    normed_one, inverse_one = normalize_keep(inputs_full)
    entry_one = (
        (normed_one * (1.0 + scale_one) + shift_one)
        .astype(jnp.bfloat16)
        .reshape(tokens_here, width_all)
    )
    projected = jnp.dot(entry_one, full_qkv, preferred_element_type=jnp.float32)
    token_shape = (micro_count, row_count, width_all)
    queries = (
        (projected[:, :width_all] + query_bias.astype(jnp.float32))
        .astype(jnp.bfloat16)
        .reshape(token_shape)
    )
    keys_here = projected[:, width_all : 2 * width_all].astype(jnp.bfloat16).reshape(token_shape)
    values_here = (
        (projected[:, 2 * width_all :] + value_bias.astype(jnp.float32))
        .astype(jnp.bfloat16)
        .reshape(token_shape)
    )
    head_queries, head_keys, head_values = (
        lax.all_to_all(queries, "seq", split_axis=2, concat_axis=1, tiled=True),
        lax.all_to_all(keys_here, "seq", split_axis=2, concat_axis=1, tiled=True),
        lax.all_to_all(values_here, "seq", split_axis=2, concat_axis=1, tiled=True),
    )
    block_rows = min(1024, head_queries.shape[1])

    def attend_one(trio):
        return attend_heads(trio[0], trio[1], trio[2], block_rows)

    head_mixed, log_totals = lax.map(attend_one, (head_queries, head_keys, head_values))
    token_mixed = lax.all_to_all(
        head_mixed, "seq", split_axis=1, concat_axis=2, tiled=True
    ).reshape(tokens_here, width_all)
    branch_one = (
        jnp.dot(token_mixed, full_out, preferred_element_type=jnp.float32)
        + out_bias.astype(jnp.float32)
    ).reshape(token_shape)
    middle = inputs_full + gate_one * branch_one
    normed_two, inverse_two = normalize_keep(middle)
    entry_two = (
        (normed_two * (1.0 + scale_two) + shift_two)
        .astype(jnp.bfloat16)
        .reshape(tokens_here, width_all)
    )
    hidden = jnp.dot(entry_two, full_fc1, preferred_element_type=jnp.float32) + up_bias.astype(
        jnp.float32
    )
    active_full, gelu_pull = jax.vjp(gelu_tanh, hidden)
    active = active_full.astype(jnp.bfloat16)
    branch_two = (
        jnp.dot(active, gathered_down_weight, preferred_element_type=jnp.float32)
        + down_bias.astype(jnp.float32)
    ).reshape(token_shape)
    result = (middle + gate_two * branch_two).astype(jnp.bfloat16)
    grad_output = out_cotangent.astype(jnp.float32)
    grad_gate_two = jnp.sum(grad_output * branch_two, axis=1)
    grad_branch_two = (gate_two * grad_output).astype(jnp.bfloat16).reshape(tokens_here, width_all)
    grad_active = compared_with(grad_branch_two, gathered_down_weight)
    grad_hidden = gelu_pull(grad_active)[0].astype(jnp.bfloat16)
    grad_entry_two = compared_with(grad_hidden, full_fc1).reshape(token_shape)
    grad_shift_two = jnp.sum(grad_entry_two, axis=1)
    grad_scale_two = jnp.sum(grad_entry_two * normed_two, axis=1)
    grad_middle = grad_output + normalize_back(
        grad_entry_two * (1.0 + scale_two), normed_two, inverse_two
    )
    grad_gate_one = jnp.sum(grad_middle * branch_one, axis=1)
    grad_branch_one = (gate_one * grad_middle).astype(jnp.bfloat16).reshape(tokens_here, width_all)
    grad_mixed = compared_with(grad_branch_one, full_out).astype(jnp.bfloat16).reshape(token_shape)
    head_grads = lax.all_to_all(grad_mixed, "seq", split_axis=2, concat_axis=1, tiled=True)

    def back_one(grouped):
        return attend_back(grouped[0], grouped[1], grouped[2], grouped[3], grouped[4], block_rows)

    grad_heads_q, grad_heads_k, grad_heads_v = lax.map(
        back_one, (head_queries, head_keys, head_values, head_grads, log_totals)
    )
    grad_queries, grad_keys, grad_values = (
        lax.all_to_all(grad_heads_q, "seq", split_axis=1, concat_axis=2, tiled=True),
        lax.all_to_all(grad_heads_k, "seq", split_axis=1, concat_axis=2, tiled=True),
        lax.all_to_all(grad_heads_v, "seq", split_axis=1, concat_axis=2, tiled=True),
    )
    grad_project = jnp.concatenate([grad_queries, grad_keys, grad_values], axis=2).reshape(
        tokens_here, 3 * width_all
    )
    grad_entry_one = compared_with(grad_project, full_qkv).reshape(token_shape)
    grad_shift_one = jnp.sum(grad_entry_one, axis=1)
    grad_scale_one = jnp.sum(grad_entry_one * normed_one, axis=1)
    grad_latents = grad_middle + normalize_back(
        grad_entry_one * (1.0 + scale_one), normed_one, inverse_one
    )
    grad_mod_part = jnp.concatenate(
        [
            grad_shift_one,
            grad_scale_one,
            grad_gate_one,
            grad_shift_two,
            grad_scale_two,
            grad_gate_two,
        ],
        axis=1,
    )
    grad_mod_seq = lax.psum(grad_mod_part, "seq").astype(jnp.bfloat16)
    grad_mod_all = lax.all_gather(grad_mod_seq, "fsdp", axis=0, tiled=True)
    grad_w_mod = outer_sum(lifted, grad_mod_all)
    grad_b_mod = jnp.sum(
        lax.dynamic_slice_in_dim(grad_mod_all, owner * mod_cols, mod_cols, 1).astype(jnp.float32),
        axis=0,
    )
    grad_lifted = compared_with(grad_mod_all, w_mod)
    grad_condition = lift_pull(grad_lifted)[0]
    grad_table = jnp.dot(
        one_hot.astype(jnp.float32).T,
        grad_condition,
        precision=lax.Precision.HIGHEST,
        preferred_element_type=jnp.float32,
    )
    grad_q_bias = jnp.sum(grad_project[:, :width_all].astype(jnp.float32), axis=0)
    grad_v_bias = jnp.sum(grad_project[:, 2 * width_all :].astype(jnp.float32), axis=0)
    grad_out_bias = jnp.sum(grad_branch_one.astype(jnp.float32), axis=0)
    grad_up_bias = jnp.sum(grad_hidden.astype(jnp.float32), axis=0)
    grad_down_bias = jnp.sum(grad_branch_two.astype(jnp.float32), axis=0)
    rights = (grad_project, grad_branch_one, grad_hidden, grad_branch_two)
    lefts = (
        regroup(entry_one, 1, fsdp_count, seq_count),
        regroup(token_mixed, 1, fsdp_count, seq_count),
        regroup(entry_two, 1, fsdp_count, seq_count),
        regroup(active, 1, fsdp_count, seq_count),
    )
    wide_term = make_term(lefts, rights, ratio)
    wide = lax.psum_scatter(
        wide_term(
            jnp.int32(0), width_all // (fsdp_count * seq_count) * lax.axis_size(("seq", "fsdp"))
        ),
        ("seq", "fsdp"),
        scatter_dimension=0,
        tiled=True,
    )
    biases = (
        lax.psum_scatter(
            regroup(grad_q_bias, 0, fsdp_count, seq_count),
            ("seq", "fsdp"),
            scatter_dimension=0,
            tiled=True,
        ),
        lax.psum_scatter(
            regroup(grad_v_bias, 0, fsdp_count, seq_count),
            ("seq", "fsdp"),
            scatter_dimension=0,
            tiled=True,
        ),
        lax.psum_scatter(
            regroup(grad_out_bias, 0, fsdp_count, seq_count),
            ("seq", "fsdp"),
            scatter_dimension=0,
            tiled=True,
        ),
        lax.psum_scatter(
            regroup(grad_up_bias, 0, fsdp_count, seq_count),
            ("seq", "fsdp"),
            scatter_dimension=0,
            tiled=True,
        ),
        lax.psum_scatter(
            regroup(grad_down_bias, 0, fsdp_count, seq_count),
            ("seq", "fsdp"),
            scatter_dimension=0,
            tiled=True,
        ),
    )
    owned = (
        lax.all_gather(wide, "seq", axis=0, tiled=True),
        lax.all_gather(biases[0], "seq", axis=0, tiled=True),
        lax.all_gather(biases[1], "seq", axis=0, tiled=True),
        lax.all_gather(biases[2], "seq", axis=0, tiled=True),
        lax.all_gather(biases[3], "seq", axis=0, tiled=True),
        lax.all_gather(biases[4], "seq", axis=0, tiled=True),
    )
    wide_owned = owned[0]
    ff_width = full_fc1.shape[1]
    grad_w_qkv = wide_owned[:, : 3 * width_all]
    grad_w_out = wide_owned[:, 3 * width_all : 4 * width_all]
    grad_w_fc1 = wide_owned[:, 4 * width_all : 4 * width_all + ff_width]
    grad_w_fc2 = wide_owned[:, 4 * width_all + ff_width :].reshape(-1, width_all)
    return (
        result,
        grad_latents,
        grad_table,
        grad_w_mod,
        grad_b_mod,
        grad_w_qkv,
        owned[1],
        owned[2],
        grad_w_out,
        owned[3],
        grad_w_fc1,
        owned[4],
        grad_w_fc2,
        owned[5],
    )


def attend_kernel(q_ref, k_ref, v_ref, o_ref, lse_ref):
    for head in range(2):
        at = slice(head * HEAD_DIM, (head + 1) * HEAD_DIM)
        queries = q_ref[:, at] * jnp.bfloat16(HEAD_DIM ** (-0.5))
        scores = compared_with(k_ref[:, at], queries)
        highest = jnp.max(scores, axis=0, keepdims=True)
        powers = jnp.exp(scores - highest)
        totals = jnp.sum(powers, axis=0, keepdims=True)
        probs = (powers * (1.0 / totals)).astype(jnp.bfloat16)
        mixed = jnp.dot(v_ref[:, at].T, probs, preferred_element_type=jnp.float32)
        o_ref[:, at] = mixed.T.astype(jnp.bfloat16)
        lse_ref[0, head : head + 1, :] = highest + jnp.log(totals)


def attend_back_kernel(q_ref, k_ref, v_ref, do_ref, lse_ref, dq_ref, dk_ref, dv_ref):
    for head in range(2):
        at = slice(head * HEAD_DIM, (head + 1) * HEAD_DIM)
        queries = q_ref[:, at] * jnp.bfloat16(HEAD_DIM ** (-0.5))
        keys = k_ref[:, at]
        grad_mixed = do_ref[:, at]
        probs = jnp.exp(compared_with(keys, queries) - lse_ref[0, head : head + 1, :])
        dv_ref[:, at] = jnp.dot(
            probs.astype(jnp.bfloat16), grad_mixed, preferred_element_type=jnp.float32
        ).astype(jnp.bfloat16)
        grad_probs = compared_with(v_ref[:, at], grad_mixed)
        inner = jnp.sum(grad_probs * probs, axis=0, keepdims=True)
        grad_scores = (probs * (grad_probs - inner)).astype(jnp.bfloat16)
        dk_ref[:, at] = jnp.dot(
            grad_scores, queries, preferred_element_type=jnp.float32
        ).astype(jnp.bfloat16)
        scaled_keys = keys * jnp.bfloat16(HEAD_DIM ** (-0.5))
        grad_queries = jnp.dot(scaled_keys.T, grad_scores, preferred_element_type=jnp.float32)
        dq_ref[:, at] = grad_queries.T.astype(jnp.bfloat16)


VMEM_LIMIT = 48 * 1024 * 1024


def attend_local(projected):
    length, wide = projected.shape
    pairs = wide // 3 // 128

    def part(which):
        return pl.BlockSpec((length, 128), lambda i: (0, which * pairs + i))

    cost = pl.CostEstimate(
        flops=pairs * length * length,
        bytes_accessed=length * wide,
        transcendentals=0,
    )
    return pl.pallas_call(
        attend_kernel,
        grid=(pairs,),
        in_specs=[part(0), part(1), part(2)],
        out_specs=[part(0), pl.BlockSpec((1, 2, length), lambda i: (i, 0, 0))],
        out_shape=[
            jax.ShapeDtypeStruct((length, wide // 3), jnp.bfloat16),
            jax.ShapeDtypeStruct((pairs, 2, length), jnp.float32),
        ],
        compiler_params=pltpu.CompilerParams(vmem_limit_bytes=VMEM_LIMIT),
        cost_estimate=cost,
        name="attend",
    )(projected, projected, projected)


def attend_local_back(projected, grad_mixed, log_totals):
    length, wide = projected.shape
    pairs = wide // 3 // 128

    def part(which):
        return pl.BlockSpec((length, 128), lambda i: (0, which * pairs + i))

    cost = pl.CostEstimate(
        flops=pairs * length * length,
        bytes_accessed=length * wide,
        transcendentals=0,
    )
    grads = jax.ShapeDtypeStruct((length, wide // 3), jnp.bfloat16)
    return pl.pallas_call(
        attend_back_kernel,
        grid=(pairs,),
        in_specs=[
            part(0),
            part(1),
            part(2),
            part(0),
            pl.BlockSpec((1, 2, length), lambda i: (i, 0, 0)),
        ],
        out_specs=[part(0), part(0), part(0)],
        out_shape=[grads, grads, grads],
        compiler_params=pltpu.CompilerParams(vmem_limit_bytes=VMEM_LIMIT),
        cost_estimate=cost,
        name="attend_back",
    )(projected, projected, projected, grad_mixed, log_totals)


def swapped_pairs(count, bit):
    return [(place, place ^ bit) for place in range(count)]


def assemble_kernel(place_ref, p00, p01, p10, p11, *out_refs):
    del place_ref
    for which, piece in enumerate((p00, p01, p10, p11)):

        @pl.when(pl.program_id(0) == which)
        def _():
            begin = 0
            for out_ref in out_refs:
                end = begin + out_ref.shape[-1]
                out_ref[0, 0] = piece[0, :, begin:end]
                begin = end


def gather_z(weight):
    z_groups = [
        [base + 4 * step for step in range(lax.axis_size("fsdp") // 4)] for base in range(4)
    ]
    return lax.all_gather(weight, "fsdp", axis=0, tiled=False, axis_index_groups=z_groups)


def flip(tensor, bit):
    return lax.ppermute(tensor, "fsdp", swapped_pairs(lax.axis_size("fsdp"), bit))


def assemble(own, own_core, across, across_core, *widths):
    depth, rows, columns = own.shape
    count = 4 * depth
    weight = own
    owner = lax.axis_index("fsdp")
    places = jnp.bitwise_xor(lax.rem(owner, 4), jnp.arange(4, dtype=jnp.int32))

    def piece_spec(which):
        def block(p, z, place_ref):
            del place_ref
            return (jnp.where(p == which, z, jnp.where(p < which, 0, depth - 1)), 0, 0)

        return pl.BlockSpec((1, rows, columns), block)

    def out_block(p, z, place_ref):
        return (z, place_ref[p], 0, 0)

    whole = pl.pallas_call(
        assemble_kernel,
        grid_spec=pltpu.PrefetchScalarGridSpec(
            num_scalar_prefetch=1,
            grid=(4, depth),
            in_specs=[piece_spec(which) for which in range(4)],
            out_specs=[pl.BlockSpec((1, 1, rows, width), out_block) for width in widths],
        ),
        out_shape=[
            jax.ShapeDtypeStruct((depth, 4, rows, width), weight.dtype) for width in widths
        ],
        compiler_params=pltpu.CompilerParams(vmem_limit_bytes=VMEM_LIMIT),
        cost_estimate=pl.CostEstimate(
            flops=0, bytes_accessed=depth * rows * columns, transcendentals=0
        ),
        name="assemble",
    )(places, own, own_core, across, across_core)
    return [part.reshape(count * rows, -1) for part in whole]


def gather_latents(line):
    count = lax.axis_size("fsdp")
    depth = count // 4
    owner = lax.axis_index("fsdp")
    z_at = lax.div(owner, 4)

    def doubled(tensor, place, axis, other):
        first = jnp.where(place == 0, tensor, other)
        second = jnp.where(place == 0, other, tensor)
        return jnp.stack([first, second], axis=axis)

    tensor = doubled(
        line, lax.axis_index("seq"), 0, lax.ppermute(line, "seq", swapped_pairs(2, 1))
    )
    tensor = doubled(
        tensor, lax.rem(owner, 2), 0, lax.ppermute(tensor, "fsdp", swapped_pairs(count, 1))
    )
    tensor = doubled(
        tensor,
        lax.rem(lax.div(owner, 2), 2),
        0,
        lax.ppermute(tensor, "fsdp", swapped_pairs(count, 2)),
    )
    tensor = tensor.reshape(8, -1)
    slots = [tensor]
    for shift in range(1, depth):
        pairs = [(place, (place + 4 * shift) % count) for place in range(count)]
        slots.append(lax.ppermute(tensor, "fsdp", pairs))
    ordered = []
    for z in range(depth):
        shift = lax.rem(z_at - z + depth, depth)
        chosen = slots[0]
        for step in range(1, depth):
            chosen = jnp.where(shift == step, slots[step], chosen)
        ordered.append(chosen)
    return jnp.concatenate(ordered, axis=0)


def low(tensor):
    return tensor.astype(jnp.bfloat16)


def wide(tensor):
    return tensor.astype(jnp.float32)


def pick(tensor, axis, place):
    return lax.dynamic_index_in_dim(tensor, place, axis, keepdims=False)


def split_core(partial):
    count = lax.axis_size("fsdp")
    core_at = lax.rem(lax.axis_index("fsdp"), 2)
    rows, columns = partial.shape
    blocks = low(partial).reshape(count // 4, 2, 2, rows // count, columns)
    return pick(blocks, 2, core_at), pick(blocks, 2, 1 - core_at)


def split_x(kept, arrived):
    x_at = lax.rem(lax.div(lax.axis_index("fsdp"), 2), 2)
    here = wide(pick(kept, 1, x_at)) + wide(pick(arrived, 1, x_at))
    return here, low(wide(pick(kept, 1, 1 - x_at)) + wide(pick(arrived, 1, 1 - x_at)))


def split_z(here, crossed):
    depth = here.shape[0]
    z_at = lax.div(lax.axis_index("fsdp"), 4)
    leaving = []
    for shift in range(1, depth):
        target = lax.rem(z_at + shift, depth)
        leaving.append(low(pick(here, 0, target) + wide(pick(crossed, 0, target))))
    return pick(here, 0, z_at) + wide(pick(crossed, 0, z_at)), leaving


def send_z(leaving):
    count = lax.axis_size("fsdp")
    arrived = []
    for shift, part in enumerate(leaving, 1):
        pairs = [(place, (place + 4 * shift) % count) for place in range(count)]
        arrived.append(lax.ppermute(part, "fsdp", pairs))
    return arrived


def sum_z(total, arrived):
    for part in arrived:
        total = total + wide(part)
    return low(total)


def sum_seq(mine):
    return wide(mine) + wide(lax.ppermute(mine, "seq", swapped_pairs(2, 1)))


tied = lax.optimization_barrier


def local_whole_latent(
    latents,
    timesteps,
    class_ids,
    class_table,
    w_mod,
    b_mod,
    w_qkv,
    b_q,
    b_v,
    w_out,
    b_out,
    w_fc1,
    b_fc1,
    w_fc2,
    b_fc2,
    out_cotangent,
):
    rows_here, width_all = latents.shape[1:]
    columns = class_table.shape[1]
    owner = lax.axis_index("fsdp")
    mine = lax.axis_index("seq")
    fsdp_count = lax.axis_size("fsdp")
    seq_swap = swapped_pairs(2, 1)

    def whole_latent(pair):
        kept = lax.dynamic_index_in_dim(pair, mine, 0, keepdims=False)
        given = lax.dynamic_index_in_dim(pair, 1 - mine, 0, keepdims=False)
        return jnp.concatenate([kept, lax.ppermute(given, "seq", seq_swap)], axis=0)

    def both_halves(tokens):
        given = lax.ppermute(tokens[rows_here:], "seq", seq_swap)
        kept = tokens[:rows_here]
        first = jnp.where(mine == 0, kept, given)
        second = jnp.where(mine == 0, given, kept)
        return jnp.stack([first, second], axis=0)

    class_range = jnp.arange(class_table.shape[0], dtype=jnp.int32)
    one_hot = (class_ids[:, None] == class_range[None, :]).astype(jnp.bfloat16)
    looked_up = jnp.dot(one_hot, class_table, preferred_element_type=jnp.float32)
    timing = lax.dynamic_slice_in_dim(
        time_features(timesteps, width_all), owner * columns, columns, 1
    )
    condition = looked_up + timing
    lifted_full, lift_pull = jax.vjp(lift_silu, condition)
    lifted = lifted_full.astype(jnp.bfloat16)
    mod_width = w_mod.shape[1]
    mod_cols = b_mod.shape[0]
    bias_line = lax.dynamic_update_slice_in_dim(
        jnp.zeros((mod_width,), jnp.float32), b_mod.astype(jnp.float32), owner * mod_cols, 0
    )
    lifted_mine = lax.dynamic_index_in_dim(
        lifted.reshape(fsdp_count, 2, columns), mine, 1, keepdims=False
    )
    small = [b_q, b_v, b_out, b_fc1, b_fc2]
    small_line = wide(jnp.concatenate(small))
    to_owners = jnp.concatenate(
        [
            jnp.dot(lifted_mine, w_mod, preferred_element_type=jnp.float32) + bias_line[None, :],
            jnp.broadcast_to(small_line[None, :], (fsdp_count, small_line.shape[0])),
        ],
        axis=1,
    )
    from_owners = lax.all_to_all(to_owners, "fsdp", 0, 0, tiled=True)
    own_a = gather_z(jnp.concatenate([w_qkv, w_out], axis=1))
    own_b = gather_z(w_fc1)
    own_a, from_owners = tied((own_a, from_owners))
    core_a = flip(own_a, 1)
    across_a = flip(own_a, 2)

    modulation = jnp.sum(from_owners[:, :mod_width], axis=0, keepdims=True)
    shift_one, scale_one, gate_one, shift_two, scale_two, gate_two = [
        modulation[:, position * width_all : (position + 1) * width_all] for position in range(6)
    ]
    biases = []
    begin = mod_width
    for part in small:
        end = begin + part.shape[0]
        biases.append(from_owners[:, begin:end].reshape(1, -1))
        begin = end
    query_bias, value_bias, out_bias, up_bias, down_bias = biases

    inputs_full = whole_latent(latents).astype(jnp.float32)
    grad_output = whole_latent(out_cotangent).astype(jnp.float32)
    normed_one, inverse_one = normalize_keep(inputs_full)
    entry_one = low(normed_one * (1.0 + scale_one) + shift_one)
    entry_one, across_a = tied((entry_one, across_a))
    across_core_a = flip(across_a, 1)
    full_qkv, full_out = assemble(
        own_a, core_a, across_a, across_core_a, w_qkv.shape[1], w_out.shape[1]
    )
    full_qkv, own_b, w_fc2 = tied((full_qkv, own_b, w_fc2))
    own_c = gather_z(w_fc2)
    core_b = flip(own_b, 1)
    across_b = flip(own_b, 2)
    qkv_bias = jnp.concatenate([query_bias, jnp.zeros_like(query_bias), value_bias], axis=1)
    projected = low(jnp.dot(entry_one, full_qkv, preferred_element_type=jnp.float32) + qkv_bias)
    mixed, log_totals = attend_local(projected)
    branch_one = jnp.dot(mixed, full_out, preferred_element_type=jnp.float32) + out_bias
    middle = inputs_full + gate_one * branch_one
    normed_two, inverse_two = normalize_keep(middle)
    entry_two = low(normed_two * (1.0 + scale_two) + shift_two)
    entry_two, across_b, core_b = tied((entry_two, across_b, core_b))
    across_core_b = flip(across_b, 1)
    own_c, across_core_b = tied((own_c, across_core_b))
    core_c = flip(own_c, 1)
    across_c = flip(own_c, 2)
    (full_fc1,) = assemble(own_b, core_b, across_b, across_core_b, w_fc1.shape[1])
    hidden = jnp.dot(entry_two, full_fc1, preferred_element_type=jnp.float32) + up_bias
    active_full, gelu_pull = jax.vjp(gelu_tanh, hidden)
    active = low(active_full)
    grad_branch_two = low(gate_two * grad_output)
    kept_fc2, leaving_fc2 = split_core(outer_sum(active, grad_branch_two))
    leaving_fc2, across_c, core_c = tied((leaving_fc2, across_c, core_c))
    across_core_c = flip(across_c, 1)
    arrived_fc2 = flip(leaving_fc2, 1)
    (full_fc2,) = assemble(own_c, core_c, across_c, across_core_c, w_fc2.shape[1])
    branch_two = jnp.dot(active, full_fc2, preferred_element_type=jnp.float32) + down_bias
    result = both_halves(low(middle + gate_two * branch_two))
    grad_gate_two = jnp.sum(grad_output * branch_two, axis=0, keepdims=True)
    here_fc2, away_fc2 = split_x(kept_fc2, arrived_fc2)
    grad_branch_two, away_fc2 = tied((grad_branch_two, away_fc2))
    crossed_fc2 = flip(away_fc2, 2)
    grad_active = compared_with(grad_branch_two, full_fc2)
    grad_hidden = low(gelu_pull(grad_active)[0])
    kept_fc1, leaving_fc1 = split_core(outer_sum(entry_two, grad_hidden))
    grad_hidden, leaving_fc1, crossed_fc2 = tied((grad_hidden, leaving_fc1, crossed_fc2))
    arrived_fc1 = flip(leaving_fc1, 1)
    grad_entry_two = compared_with(grad_hidden, full_fc1)
    here_fc1, away_fc1 = split_x(kept_fc1, arrived_fc1)
    total_fc2, leaving_fc2 = split_z(here_fc2, crossed_fc2)
    grad_entry_two, leaving_fc2, away_fc1 = tied((grad_entry_two, leaving_fc2, away_fc1))
    crossed_fc1 = flip(away_fc1, 2)
    grad_shift_two = jnp.sum(grad_entry_two, axis=0, keepdims=True)
    grad_scale_two = jnp.sum(grad_entry_two * normed_two, axis=0, keepdims=True)
    grad_middle = grad_output + normalize_back(
        grad_entry_two * (1.0 + scale_two), normed_two, inverse_two
    )
    grad_gate_one = jnp.sum(grad_middle * branch_one, axis=0, keepdims=True)
    grad_branch_one = low(gate_one * grad_middle)
    landed_fc2 = send_z(leaving_fc2)
    kept_out, leaving_out = split_core(outer_sum(mixed, grad_branch_one))
    leaving_out, grad_branch_one = tied((leaving_out, grad_branch_one))
    arrived_out = flip(leaving_out, 1)
    grad_mixed = low(compared_with(grad_branch_one, full_out))
    here_out, away_out = split_x(kept_out, arrived_out)
    grad_mixed, away_out = tied((grad_mixed, away_out))
    grad_project = jnp.concatenate(attend_local_back(projected, grad_mixed, log_totals), axis=1)
    crossed_fc1, away_out, grad_project, landed_fc2, result = tied(
        (crossed_fc1, away_out, grad_project, landed_fc2, result)
    )
    crossed_out = flip(away_out, 2)
    total_fc1, leaving_fc1 = split_z(here_fc1, crossed_fc1)
    grad_project, leaving_fc1 = tied((grad_project, leaving_fc1))
    landed_fc1 = send_z(leaving_fc1)
    kept_qkv, leaving_qkv = split_core(outer_sum(entry_one, grad_project))
    grad_project, leaving_qkv = tied((grad_project, leaving_qkv))
    arrived_qkv = flip(leaving_qkv, 1)
    grad_entry_one = compared_with(grad_project, full_qkv)
    here_qkv, away_qkv = split_x(kept_qkv, arrived_qkv)
    grad_entry_one, away_qkv, crossed_out = tied((grad_entry_one, away_qkv, crossed_out))
    crossed_qkv = flip(away_qkv, 2)
    total_out, leaving_out = split_z(here_out, crossed_out)
    mine_fc2 = sum_z(total_fc2, landed_fc2)
    grad_entry_one, leaving_out, mine_fc2 = tied((grad_entry_one, leaving_out, mine_fc2))
    landed_out = send_z(leaving_out)
    sum_fc2 = sum_seq(mine_fc2)
    grad_shift_one = jnp.sum(grad_entry_one, axis=0, keepdims=True)
    grad_scale_one = jnp.sum(grad_entry_one * normed_one, axis=0, keepdims=True)
    grad_latents = both_halves(
        grad_middle
        + normalize_back(grad_entry_one * (1.0 + scale_one), normed_one, inverse_one)
    )
    grad_mod_mine = low(
        jnp.concatenate(
            [
                grad_shift_one,
                grad_scale_one,
                grad_gate_one,
                grad_shift_two,
                grad_scale_two,
                grad_gate_two,
            ],
            axis=1,
        )
    )
    grad_mod_mine, landed_fc1, crossed_qkv = tied((grad_mod_mine, landed_fc1, crossed_qkv))
    total_qkv, leaving_qkv = split_z(here_qkv, crossed_qkv)
    mine_fc1 = sum_z(total_fc1, landed_fc1)
    grad_mod_mine, leaving_qkv, mine_fc1 = tied((grad_mod_mine, leaving_qkv, mine_fc1))
    landed_qkv = send_z(leaving_qkv)
    sum_fc1 = sum_seq(mine_fc1)
    grad_mod_all = gather_latents(grad_mod_mine)
    sum_out = sum_seq(sum_z(total_out, landed_out))
    sum_qkv = sum_seq(sum_z(total_qkv, landed_qkv))
    grad_w_mod = outer_sum(lifted, grad_mod_all)
    grad_b_mod = jnp.sum(
        lax.dynamic_slice_in_dim(grad_mod_all, owner * mod_cols, mod_cols, 1).astype(jnp.float32),
        axis=0,
    )
    grad_lifted = compared_with(grad_mod_all, w_mod)
    grad_condition = lift_pull(grad_lifted)[0]
    grad_table = jnp.dot(
        one_hot.astype(jnp.float32).T,
        grad_condition,
        precision=lax.Precision.HIGHEST,
        preferred_element_type=jnp.float32,
    )
    grad_small = [
        wide(grad_project[:, :width_all]),
        wide(grad_project[:, 2 * width_all :]),
        wide(grad_branch_one),
        wide(grad_hidden),
        wide(grad_branch_two),
    ]
    small_sums = jnp.concatenate(
        [jnp.sum(part, axis=0).reshape(fsdp_count, -1) for part in grad_small], axis=1
    )
    small_here = jnp.sum(
        lax.all_to_all(small_sums, "fsdp", 0, 0, tiled=True), axis=0, keepdims=True
    )
    small_total = (small_here + lax.ppermute(small_here, "seq", seq_swap))[0]
    small_grads = []
    begin = 0
    for part in small:
        small_grads.append(small_total[begin : begin + part.shape[0]])
        begin += part.shape[0]
    return (
        result,
        grad_latents,
        grad_table,
        grad_w_mod,
        grad_b_mod,
        sum_qkv,
        small_grads[0],
        small_grads[1],
        sum_out,
        small_grads[2],
        sum_fc1,
        small_grads[3],
        sum_fc2,
        small_grads[4],
    )


def solution(mesh):
    placed = (
        P("fsdp", "seq", None),
        P(),
        P(),
        P(None, "fsdp"),
        P("fsdp", None),
        P("fsdp"),
        P("fsdp", None),
        P("fsdp"),
        P("fsdp"),
        P("fsdp", None),
        P("fsdp"),
        P("fsdp", None),
        P("fsdp"),
        P("fsdp", None),
        P("fsdp"),
        P("fsdp", "seq", None),
    )
    spans = mesh.shape["fsdp"]

    def body(*arrays):
        whole_fits = arrays[0].shape[0] == mesh.shape["seq"] == 2 and spans % 4 == 0
        return (local_whole_latent if whole_fits else local)(*arrays)

    return jax.shard_map(
        body,
        mesh=mesh,
        in_specs=placed,
        out_specs=(
            P("fsdp", "seq", None),
            P("fsdp", "seq", None),
            P(None, "fsdp"),
            P("fsdp", None),
            P("fsdp"),
            P("fsdp", None),
            P("fsdp"),
            P("fsdp"),
            P("fsdp", None),
            P("fsdp"),
            P("fsdp", None),
            P("fsdp"),
            P("fsdp", None),
            P("fsdp"),
        ),
        check_vma=False,
    )
```

```python
import math

import jax
import jax.numpy as jnp
from jax import lax
from jax.experimental import pallas as pl
from jax.experimental.pallas import tpu as pltpu
from jax.sharding import PartitionSpec as P

HEAD_DIM = 64


def time_features(step_ids, columns):
    half_width = columns // 2
    freqs = jnp.exp(-math.log(10000.0) * jnp.arange(half_width, dtype=jnp.float32) / half_width)
    angles = step_ids.astype(jnp.float32)[:, None] * freqs[None, :]
    return jnp.concatenate([jnp.cos(angles), jnp.sin(angles)], axis=1)


def normalize_keep(tensor):
    centered = tensor - jnp.mean(tensor, axis=-1, keepdims=True)
    variance = jnp.mean(centered * centered, axis=-1, keepdims=True)
    inverse = lax.rsqrt(variance + 1e-06)
    return (centered * inverse, inverse)


def normalize_back(grad_hat, normed, inverse):
    mean_grad = jnp.mean(grad_hat, axis=-1, keepdims=True)
    mean_cross = jnp.mean(grad_hat * normed, axis=-1, keepdims=True)
    return inverse * (grad_hat - mean_grad - normed * mean_cross)


def gelu_tanh(tensor):
    return (
        0.5
        * tensor
        * (1.0 + jnp.tanh(0.7978845608028654 * (tensor + 0.044715 * tensor * tensor * tensor)))
    )


def lift_silu(tensor):
    return tensor * jax.nn.sigmoid(tensor)


def outer_sum(earlier_value, latter):
    return lax.dot_general(
        earlier_value, latter, (((0,), (0,)), ((), ())), preferred_element_type=jnp.float32
    )


def compared_with(earlier_value, latter):
    return lax.dot_general(
        earlier_value, latter, (((1,), (1,)), ((), ())), preferred_element_type=jnp.float32
    )


def regroup(tensor, axis_pos, outer_count, inner_count):
    extents = tensor.shape
    splitted = (
        extents[:axis_pos]
        + (outer_count, inner_count, extents[axis_pos] // (outer_count * inner_count))
        + extents[axis_pos + 1 :]
    )
    swapped = jnp.swapaxes(tensor.reshape(splitted), axis_pos, axis_pos + 1)
    return swapped.reshape(extents)


def make_term(lefts, rights, ratio):
    first_left, second_left, third_left, fourth_left = lefts
    first_right, second_right, third_right, fourth_right = rights

    def term(start, count):
        qkv_part = outer_sum(first_left, first_right)
        out_part = outer_sum(second_left, second_right)
        fc1_part = outer_sum(third_left, third_right)
        fc2_part = outer_sum(fourth_left, fourth_right).reshape(
            count, ratio * fourth_right.shape[1]
        )
        return jnp.concatenate([qkv_part, out_part, fc1_part, fc2_part], axis=1)

    return term


def attend_heads(queries, keys_all, values_all, block_rows):
    length_all = queries.shape[0]
    head_count = queries.shape[1] // HEAD_DIM
    scaling = HEAD_DIM ** (-0.5)
    query_blocks = queries.reshape(length_all // block_rows, block_rows, head_count, HEAD_DIM)
    key_heads = keys_all.reshape(length_all, head_count, HEAD_DIM)
    value_heads = values_all.reshape(length_all, head_count, HEAD_DIM)

    def one_block(query_block):
        scores = (
            jnp.einsum("qhd,khd->hqk", query_block, key_heads, preferred_element_type=jnp.float32)
            * scaling
        )
        highest = jnp.max(scores, axis=-1, keepdims=True)
        powers = jnp.exp(scores - highest)
        totals = jnp.sum(powers, axis=-1, keepdims=True)
        weight_tensors = (powers / totals).astype(jnp.bfloat16)
        mixed = jnp.einsum(
            "hqk,khd->qhd", weight_tensors, value_heads, preferred_element_type=jnp.float32
        )
        return (mixed.astype(jnp.bfloat16), (highest + jnp.log(totals))[:, :, 0])

    mixed, log_totals = lax.map(one_block, query_blocks)
    return (mixed.reshape(length_all, head_count * HEAD_DIM), log_totals)


def attend_back(queries, keys_all, values_all, grad_mixed, log_totals, block_rows):
    length_all = queries.shape[0]
    head_count = queries.shape[1] // HEAD_DIM
    scaling = HEAD_DIM ** (-0.5)
    block_count = length_all // block_rows
    query_blocks = queries.reshape(block_count, block_rows, head_count, HEAD_DIM)
    grad_blocks = grad_mixed.reshape(block_count, block_rows, head_count, HEAD_DIM)
    key_heads = keys_all.reshape(length_all, head_count, HEAD_DIM)
    value_heads = values_all.reshape(length_all, head_count, HEAD_DIM)

    def one_block(carried, blocked):
        grad_keys, grad_values = carried
        query_block, grad_block, log_block = blocked
        scores = (
            jnp.einsum("qhd,khd->hqk", query_block, key_heads, preferred_element_type=jnp.float32)
            * scaling
        )
        probs = jnp.exp(scores - log_block[:, :, None])
        grad_values = grad_values + jnp.einsum(
            "hqk,qhd->khd",
            probs.astype(jnp.bfloat16),
            grad_block,
            preferred_element_type=jnp.float32,
        )
        grad_probs = jnp.einsum(
            "qhd,khd->hqk", grad_block, value_heads, preferred_element_type=jnp.float32
        )
        grad_scores = (
            probs * (grad_probs - jnp.sum(grad_probs * probs, axis=-1, keepdims=True))
        ).astype(jnp.bfloat16)
        grad_query = (
            jnp.einsum("hqk,khd->qhd", grad_scores, key_heads, preferred_element_type=jnp.float32)
            * scaling
        )
        grad_keys = (
            grad_keys
            + jnp.einsum(
                "hqk,qhd->khd", grad_scores, query_block, preferred_element_type=jnp.float32
            )
            * scaling
        )
        return ((grad_keys, grad_values), grad_query.astype(jnp.bfloat16))

    zeroed = jnp.zeros((length_all, head_count, HEAD_DIM), jnp.float32)
    (grad_keys, grad_values), grad_queries = lax.scan(
        one_block, (zeroed, zeroed), (query_blocks, grad_blocks, log_totals)
    )
    flat_width = head_count * HEAD_DIM
    return (
        grad_queries.reshape(length_all, flat_width),
        grad_keys.reshape(length_all, flat_width).astype(jnp.bfloat16),
        grad_values.reshape(length_all, flat_width).astype(jnp.bfloat16),
    )


def local(
    latents,
    timesteps,
    class_ids,
    class_table,
    w_mod,
    b_mod,
    w_qkv,
    b_q,
    b_v,
    w_out,
    b_out,
    w_fc1,
    b_fc1,
    w_fc2,
    b_fc2,
    out_cotangent,
):
    micro_count, row_count, width_all = latents.shape
    tokens_here = micro_count * row_count
    columns = class_table.shape[1]
    owner = lax.axis_index("fsdp")
    seq_count = lax.axis_size("seq")
    fsdp_count = lax.axis_size("fsdp")
    class_range = jnp.arange(class_table.shape[0], dtype=jnp.int32)
    one_hot = (class_ids[:, None] == class_range[None, :]).astype(jnp.bfloat16)
    looked_up = jnp.dot(one_hot, class_table, preferred_element_type=jnp.float32)
    timing = lax.dynamic_slice_in_dim(
        time_features(timesteps, width_all), owner * columns, columns, 1
    )
    condition = looked_up + timing
    lifted_full, lift_pull = jax.vjp(lift_silu, condition)
    lifted = lifted_full.astype(jnp.bfloat16)
    mod_width = w_mod.shape[1]
    mod_cols = b_mod.shape[0]
    bias_line = lax.dynamic_update_slice_in_dim(
        jnp.zeros((mod_width,), jnp.float32), b_mod.astype(jnp.float32), owner * mod_cols, 0
    )
    modulation = lax.psum_scatter(
        jnp.dot(lifted, w_mod, preferred_element_type=jnp.float32) + bias_line[None, :],
        "fsdp",
        scatter_dimension=0,
        tiled=True,
    )
    mod_parts = [
        modulation[:, None, position * width_all : (position + 1) * width_all]
        for position in range(6)
    ]
    shift_one, scale_one, gate_one, shift_two, scale_two, gate_two = mod_parts
    gathered = (
        lax.all_gather(w_qkv, "fsdp", axis=0, tiled=True),
        lax.all_gather(b_q, "fsdp", axis=0, tiled=True),
        lax.all_gather(b_v, "fsdp", axis=0, tiled=True),
        lax.all_gather(w_out, "fsdp", axis=0, tiled=True),
        lax.all_gather(b_out, "fsdp", axis=0, tiled=True),
        lax.all_gather(w_fc1, "fsdp", axis=0, tiled=True),
        lax.all_gather(b_fc1, "fsdp", axis=0, tiled=True),
        lax.all_gather(w_fc2, "fsdp", axis=0, tiled=True),
        lax.all_gather(b_fc2, "fsdp", axis=0, tiled=True),
    )
    (
        full_qkv,
        query_bias,
        value_bias,
        full_out,
        out_bias,
        full_fc1,
        up_bias,
        gathered_down_weight,
        down_bias,
    ) = gathered
    ratio = gathered_down_weight.shape[0] // width_all
    inputs_full = latents.astype(jnp.float32)
    normed_one, inverse_one = normalize_keep(inputs_full)
    entry_one = (
        (normed_one * (1.0 + scale_one) + shift_one)
        .astype(jnp.bfloat16)
        .reshape(tokens_here, width_all)
    )
    projected = jnp.dot(entry_one, full_qkv, preferred_element_type=jnp.float32)
    token_shape = (micro_count, row_count, width_all)
    queries = (
        (projected[:, :width_all] + query_bias.astype(jnp.float32))
        .astype(jnp.bfloat16)
        .reshape(token_shape)
    )
    keys_here = projected[:, width_all : 2 * width_all].astype(jnp.bfloat16).reshape(token_shape)
    values_here = (
        (projected[:, 2 * width_all :] + value_bias.astype(jnp.float32))
        .astype(jnp.bfloat16)
        .reshape(token_shape)
    )
    head_queries, head_keys, head_values = (
        lax.all_to_all(queries, "seq", split_axis=2, concat_axis=1, tiled=True),
        lax.all_to_all(keys_here, "seq", split_axis=2, concat_axis=1, tiled=True),
        lax.all_to_all(values_here, "seq", split_axis=2, concat_axis=1, tiled=True),
    )
    block_rows = min(1024, head_queries.shape[1])

    def attend_one(trio):
        return attend_heads(trio[0], trio[1], trio[2], block_rows)

    head_mixed, log_totals = lax.map(attend_one, (head_queries, head_keys, head_values))
    token_mixed = lax.all_to_all(
        head_mixed, "seq", split_axis=1, concat_axis=2, tiled=True
    ).reshape(tokens_here, width_all)
    branch_one = (
        jnp.dot(token_mixed, full_out, preferred_element_type=jnp.float32)
        + out_bias.astype(jnp.float32)
    ).reshape(token_shape)
    middle = inputs_full + gate_one * branch_one
    normed_two, inverse_two = normalize_keep(middle)
    entry_two = (
        (normed_two * (1.0 + scale_two) + shift_two)
        .astype(jnp.bfloat16)
        .reshape(tokens_here, width_all)
    )
    hidden = jnp.dot(entry_two, full_fc1, preferred_element_type=jnp.float32) + up_bias.astype(
        jnp.float32
    )
    active_full, gelu_pull = jax.vjp(gelu_tanh, hidden)
    active = active_full.astype(jnp.bfloat16)
    branch_two = (
        jnp.dot(active, gathered_down_weight, preferred_element_type=jnp.float32)
        + down_bias.astype(jnp.float32)
    ).reshape(token_shape)
    result = (middle + gate_two * branch_two).astype(jnp.bfloat16)
    grad_output = out_cotangent.astype(jnp.float32)
    grad_gate_two = jnp.sum(grad_output * branch_two, axis=1)
    grad_branch_two = (gate_two * grad_output).astype(jnp.bfloat16).reshape(tokens_here, width_all)
    grad_active = compared_with(grad_branch_two, gathered_down_weight)
    grad_hidden = gelu_pull(grad_active)[0].astype(jnp.bfloat16)
    grad_entry_two = compared_with(grad_hidden, full_fc1).reshape(token_shape)
    grad_shift_two = jnp.sum(grad_entry_two, axis=1)
    grad_scale_two = jnp.sum(grad_entry_two * normed_two, axis=1)
    grad_middle = grad_output + normalize_back(
        grad_entry_two * (1.0 + scale_two), normed_two, inverse_two
    )
    grad_gate_one = jnp.sum(grad_middle * branch_one, axis=1)
    grad_branch_one = (gate_one * grad_middle).astype(jnp.bfloat16).reshape(tokens_here, width_all)
    grad_mixed = compared_with(grad_branch_one, full_out).astype(jnp.bfloat16).reshape(token_shape)
    head_grads = lax.all_to_all(grad_mixed, "seq", split_axis=2, concat_axis=1, tiled=True)

    def back_one(grouped):
        return attend_back(grouped[0], grouped[1], grouped[2], grouped[3], grouped[4], block_rows)

    grad_heads_q, grad_heads_k, grad_heads_v = lax.map(
        back_one, (head_queries, head_keys, head_values, head_grads, log_totals)
    )
    grad_queries, grad_keys, grad_values = (
        lax.all_to_all(grad_heads_q, "seq", split_axis=1, concat_axis=2, tiled=True),
        lax.all_to_all(grad_heads_k, "seq", split_axis=1, concat_axis=2, tiled=True),
        lax.all_to_all(grad_heads_v, "seq", split_axis=1, concat_axis=2, tiled=True),
    )
    grad_project = jnp.concatenate([grad_queries, grad_keys, grad_values], axis=2).reshape(
        tokens_here, 3 * width_all
    )
    grad_entry_one = compared_with(grad_project, full_qkv).reshape(token_shape)
    grad_shift_one = jnp.sum(grad_entry_one, axis=1)
    grad_scale_one = jnp.sum(grad_entry_one * normed_one, axis=1)
    grad_latents = grad_middle + normalize_back(
        grad_entry_one * (1.0 + scale_one), normed_one, inverse_one
    )
    grad_mod_part = jnp.concatenate(
        [
            grad_shift_one,
            grad_scale_one,
            grad_gate_one,
            grad_shift_two,
            grad_scale_two,
            grad_gate_two,
        ],
        axis=1,
    )
    grad_mod_seq = lax.psum(grad_mod_part, "seq").astype(jnp.bfloat16)
    grad_mod_all = lax.all_gather(grad_mod_seq, "fsdp", axis=0, tiled=True)
    grad_w_mod = outer_sum(lifted, grad_mod_all)
    grad_b_mod = jnp.sum(
        lax.dynamic_slice_in_dim(grad_mod_all, owner * mod_cols, mod_cols, 1).astype(jnp.float32),
        axis=0,
    )
    grad_lifted = compared_with(grad_mod_all, w_mod)
    grad_condition = lift_pull(grad_lifted)[0]
    grad_table = jnp.dot(
        one_hot.astype(jnp.float32).T,
        grad_condition,
        precision=lax.Precision.HIGHEST,
        preferred_element_type=jnp.float32,
    )
    grad_q_bias = jnp.sum(grad_project[:, :width_all].astype(jnp.float32), axis=0)
    grad_v_bias = jnp.sum(grad_project[:, 2 * width_all :].astype(jnp.float32), axis=0)
    grad_out_bias = jnp.sum(grad_branch_one.astype(jnp.float32), axis=0)
    grad_up_bias = jnp.sum(grad_hidden.astype(jnp.float32), axis=0)
    grad_down_bias = jnp.sum(grad_branch_two.astype(jnp.float32), axis=0)
    rights = (grad_project, grad_branch_one, grad_hidden, grad_branch_two)
    lefts = (
        regroup(entry_one, 1, fsdp_count, seq_count),
        regroup(token_mixed, 1, fsdp_count, seq_count),
        regroup(entry_two, 1, fsdp_count, seq_count),
        regroup(active, 1, fsdp_count, seq_count),
    )
    wide_term = make_term(lefts, rights, ratio)
    wide = lax.psum_scatter(
        wide_term(
            jnp.int32(0), width_all // (fsdp_count * seq_count) * lax.axis_size(("seq", "fsdp"))
        ),
        ("seq", "fsdp"),
        scatter_dimension=0,
        tiled=True,
    )
    biases = (
        lax.psum_scatter(
            regroup(grad_q_bias, 0, fsdp_count, seq_count),
            ("seq", "fsdp"),
            scatter_dimension=0,
            tiled=True,
        ),
        lax.psum_scatter(
            regroup(grad_v_bias, 0, fsdp_count, seq_count),
            ("seq", "fsdp"),
            scatter_dimension=0,
            tiled=True,
        ),
        lax.psum_scatter(
            regroup(grad_out_bias, 0, fsdp_count, seq_count),
            ("seq", "fsdp"),
            scatter_dimension=0,
            tiled=True,
        ),
        lax.psum_scatter(
            regroup(grad_up_bias, 0, fsdp_count, seq_count),
            ("seq", "fsdp"),
            scatter_dimension=0,
            tiled=True,
        ),
        lax.psum_scatter(
            regroup(grad_down_bias, 0, fsdp_count, seq_count),
            ("seq", "fsdp"),
            scatter_dimension=0,
            tiled=True,
        ),
    )
    owned = (
        lax.all_gather(wide, "seq", axis=0, tiled=True),
        lax.all_gather(biases[0], "seq", axis=0, tiled=True),
        lax.all_gather(biases[1], "seq", axis=0, tiled=True),
        lax.all_gather(biases[2], "seq", axis=0, tiled=True),
        lax.all_gather(biases[3], "seq", axis=0, tiled=True),
        lax.all_gather(biases[4], "seq", axis=0, tiled=True),
    )
    wide_owned = owned[0]
    ff_width = full_fc1.shape[1]
    grad_w_qkv = wide_owned[:, : 3 * width_all]
    grad_w_out = wide_owned[:, 3 * width_all : 4 * width_all]
    grad_w_fc1 = wide_owned[:, 4 * width_all : 4 * width_all + ff_width]
    grad_w_fc2 = wide_owned[:, 4 * width_all + ff_width :].reshape(-1, width_all)
    return (
        result,
        grad_latents,
        grad_table,
        grad_w_mod,
        grad_b_mod,
        grad_w_qkv,
        owned[1],
        owned[2],
        grad_w_out,
        owned[3],
        grad_w_fc1,
        owned[4],
        grad_w_fc2,
        owned[5],
    )


def attend_kernel(q_ref, k_ref, v_ref, o_ref, lse_ref):
    for head in range(2):
        at = slice(head * HEAD_DIM, (head + 1) * HEAD_DIM)
        queries = q_ref[:, at] * jnp.bfloat16(HEAD_DIM ** (-0.5))
        scores = compared_with(k_ref[:, at], queries)
        highest = jnp.max(scores, axis=0, keepdims=True)
        powers = jnp.exp(scores - highest)
        totals = jnp.sum(powers, axis=0, keepdims=True)
        probs = (powers * (1.0 / totals)).astype(jnp.bfloat16)
        mixed = jnp.dot(v_ref[:, at].T, probs, preferred_element_type=jnp.float32)
        o_ref[:, at] = mixed.T.astype(jnp.bfloat16)
        lse_ref[0, head : head + 1, :] = highest + jnp.log(totals)


def attend_back_kernel(q_ref, k_ref, v_ref, do_ref, lse_ref, dq_ref, dk_ref, dv_ref):
    for head in range(2):
        at = slice(head * HEAD_DIM, (head + 1) * HEAD_DIM)
        queries = q_ref[:, at] * jnp.bfloat16(HEAD_DIM ** (-0.5))
        keys = k_ref[:, at]
        grad_mixed = do_ref[:, at]
        probs = jnp.exp(compared_with(keys, queries) - lse_ref[0, head : head + 1, :])
        dv_ref[:, at] = jnp.dot(
            probs.astype(jnp.bfloat16), grad_mixed, preferred_element_type=jnp.float32
        ).astype(jnp.bfloat16)
        grad_probs = compared_with(v_ref[:, at], grad_mixed)
        inner = jnp.sum(grad_probs * probs, axis=0, keepdims=True)
        grad_scores = (probs * (grad_probs - inner)).astype(jnp.bfloat16)
        dk_ref[:, at] = jnp.dot(
            grad_scores, queries, preferred_element_type=jnp.float32
        ).astype(jnp.bfloat16)
        scaled_keys = keys * jnp.bfloat16(HEAD_DIM ** (-0.5))
        grad_queries = jnp.dot(scaled_keys.T, grad_scores, preferred_element_type=jnp.float32)
        dq_ref[:, at] = grad_queries.T.astype(jnp.bfloat16)


VMEM_LIMIT = 48 * 1024 * 1024


def attend_local(projected):
    length, wide = projected.shape
    pairs = wide // 3 // 128

    def part(which):
        return pl.BlockSpec((length, 128), lambda i: (0, which * pairs + i))

    cost = pl.CostEstimate(
        flops=pairs * length * length,
        bytes_accessed=length * wide,
        transcendentals=0,
    )
    return pl.pallas_call(
        attend_kernel,
        grid=(pairs,),
        in_specs=[part(0), part(1), part(2)],
        out_specs=[part(0), pl.BlockSpec((1, 2, length), lambda i: (i, 0, 0))],
        out_shape=[
            jax.ShapeDtypeStruct((length, wide // 3), jnp.bfloat16),
            jax.ShapeDtypeStruct((pairs, 2, length), jnp.float32),
        ],
        compiler_params=pltpu.CompilerParams(vmem_limit_bytes=VMEM_LIMIT),
        cost_estimate=cost,
        name="attend",
    )(projected, projected, projected)


def attend_local_back(projected, grad_mixed, log_totals):
    length, wide = projected.shape
    pairs = wide // 3 // 128

    def part(which):
        return pl.BlockSpec((length, 128), lambda i: (0, which * pairs + i))

    cost = pl.CostEstimate(
        flops=pairs * length * length,
        bytes_accessed=length * wide,
        transcendentals=0,
    )
    grads = jax.ShapeDtypeStruct((length, wide // 3), jnp.bfloat16)
    return pl.pallas_call(
        attend_back_kernel,
        grid=(pairs,),
        in_specs=[
            part(0),
            part(1),
            part(2),
            part(0),
            pl.BlockSpec((1, 2, length), lambda i: (i, 0, 0)),
        ],
        out_specs=[part(0), part(0), part(0)],
        out_shape=[grads, grads, grads],
        compiler_params=pltpu.CompilerParams(vmem_limit_bytes=VMEM_LIMIT),
        cost_estimate=cost,
        name="attend_back",
    )(projected, projected, projected, grad_mixed, log_totals)


def swapped_pairs(count, bit):
    return [(place, place ^ bit) for place in range(count)]


def assemble_kernel(place_ref, *refs):
    del place_ref
    pieces, out_refs = refs[:8], refs[8:]
    for which, piece in enumerate(pieces):

        @pl.when(pl.program_id(0) == which)
        def _():
            begin = 0
            for out_ref in out_refs:
                end = begin + out_ref.shape[-1]
                out_ref[0, 0, 0] = piece[0, :, begin:end]
                begin = end


def gather_half(weight):
    rows = weight.shape[0] // 2
    half = lax.dynamic_slice_in_dim(weight, lax.axis_index("seq") * rows, rows, 0)
    z_groups = [
        [base + 4 * step for step in range(lax.axis_size("fsdp") // 4)] for base in range(4)
    ]
    return lax.all_gather(half, "fsdp", axis=0, tiled=False, axis_index_groups=z_groups)


def flip(tensor, bit):
    return lax.ppermute(tensor, "fsdp", swapped_pairs(lax.axis_size("fsdp"), bit))


def flip_seq(tensor):
    return lax.ppermute(tensor, "seq", swapped_pairs(2, 1))


def assemble(own, by_seq, by_x, by_both, *widths):
    depth, rows, columns = own[0].shape
    count = 4 * depth
    pieces = [*own, *by_seq, *by_x, *by_both]
    owner = lax.axis_index("fsdp")
    flips = jnp.asarray([0, 1, 0, 1, 2, 3, 2, 3], jnp.int32)
    halves = jnp.asarray([0, 0, 1, 1, 0, 0, 1, 1], jnp.int32)
    places = jnp.concatenate(
        [
            jnp.bitwise_xor(lax.rem(owner, 4), flips),
            jnp.bitwise_xor(lax.axis_index("seq"), halves),
        ]
    )

    def piece_spec(which):
        def block(p, z, place_ref):
            del place_ref
            return (jnp.where(p == which, z, jnp.where(p < which, 0, depth - 1)), 0, 0)

        return pl.BlockSpec((1, rows, columns), block)

    def out_block(p, z, place_ref):
        return (z, place_ref[p], place_ref[8 + p], 0, 0)

    whole = pl.pallas_call(
        assemble_kernel,
        grid_spec=pltpu.PrefetchScalarGridSpec(
            num_scalar_prefetch=1,
            grid=(8, depth),
            in_specs=[piece_spec(which) for which in range(8)],
            out_specs=[pl.BlockSpec((1, 1, 1, rows, width), out_block) for width in widths],
        ),
        out_shape=[
            jax.ShapeDtypeStruct((depth, 4, 2, rows, width), own[0].dtype) for width in widths
        ],
        compiler_params=pltpu.CompilerParams(vmem_limit_bytes=VMEM_LIMIT),
        cost_estimate=pl.CostEstimate(
            flops=0, bytes_accessed=depth * rows * columns, transcendentals=0
        ),
        name="assemble",
    )(places, *pieces)
    return [part.reshape(2 * count * rows, -1) for part in whole]


def gather_latents(line):
    count = lax.axis_size("fsdp")
    depth = count // 4
    owner = lax.axis_index("fsdp")
    z_at = lax.div(owner, 4)

    def doubled(tensor, place, axis, other):
        first = jnp.where(place == 0, tensor, other)
        second = jnp.where(place == 0, other, tensor)
        return jnp.stack([first, second], axis=axis)

    tensor = doubled(
        line, lax.axis_index("seq"), 0, lax.ppermute(line, "seq", swapped_pairs(2, 1))
    )
    tensor = doubled(
        tensor, lax.rem(owner, 2), 0, lax.ppermute(tensor, "fsdp", swapped_pairs(count, 1))
    )
    tensor = doubled(
        tensor,
        lax.rem(lax.div(owner, 2), 2),
        0,
        lax.ppermute(tensor, "fsdp", swapped_pairs(count, 2)),
    )
    tensor = tensor.reshape(8, -1)
    slots = [tensor]
    for shift in range(1, depth):
        pairs = [(place, (place + 4 * shift) % count) for place in range(count)]
        slots.append(lax.ppermute(tensor, "fsdp", pairs))
    ordered = []
    for z in range(depth):
        shift = lax.rem(z_at - z + depth, depth)
        chosen = slots[0]
        for step in range(1, depth):
            chosen = jnp.where(shift == step, slots[step], chosen)
        ordered.append(chosen)
    return jnp.concatenate(ordered, axis=0)


def low(tensor):
    return tensor.astype(jnp.bfloat16)


def wide(tensor):
    return tensor.astype(jnp.float32)


def pick(tensor, axis, place):
    return lax.dynamic_index_in_dim(tensor, place, axis, keepdims=False)


def split_core(partial):
    count = lax.axis_size("fsdp")
    core_at = lax.rem(lax.axis_index("fsdp"), 2)
    rows, columns = partial.shape
    blocks = low(partial).reshape(count // 4, 2, 2, rows // count, columns)
    return pick(blocks, 2, core_at), pick(blocks, 2, 1 - core_at)


def split_x(kept, arrived):
    x_at = lax.rem(lax.div(lax.axis_index("fsdp"), 2), 2)
    here = wide(pick(kept, 1, x_at)) + wide(pick(arrived, 1, x_at))
    return here, low(wide(pick(kept, 1, 1 - x_at)) + wide(pick(arrived, 1, 1 - x_at)))


def split_z(here, crossed):
    depth = here.shape[0]
    z_at = lax.div(lax.axis_index("fsdp"), 4)
    leaving = []
    for shift in range(1, depth):
        target = lax.rem(z_at + shift, depth)
        leaving.append(low(pick(here, 0, target) + wide(pick(crossed, 0, target))))
    return pick(here, 0, z_at) + wide(pick(crossed, 0, z_at)), leaving


def send_z(leaving):
    count = lax.axis_size("fsdp")
    arrived = []
    for shift, part in enumerate(leaving, 1):
        pairs = [(place, (place + 4 * shift) % count) for place in range(count)]
        arrived.append(lax.ppermute(part, "fsdp", pairs))
    return arrived


def sum_z(total, arrived):
    for part in arrived:
        total = total + wide(part)
    return low(total)


def sum_seq(mine):
    return wide(mine) + wide(lax.ppermute(mine, "seq", swapped_pairs(2, 1)))


tied = lax.optimization_barrier


def local_whole_latent(
    latents,
    timesteps,
    class_ids,
    class_table,
    w_mod,
    b_mod,
    w_qkv,
    b_q,
    b_v,
    w_out,
    b_out,
    w_fc1,
    b_fc1,
    w_fc2,
    b_fc2,
    out_cotangent,
):
    rows_here, width_all = latents.shape[1:]
    columns = class_table.shape[1]
    owner = lax.axis_index("fsdp")
    mine = lax.axis_index("seq")
    fsdp_count = lax.axis_size("fsdp")
    seq_swap = swapped_pairs(2, 1)

    def whole_latent(pair):
        kept = lax.dynamic_index_in_dim(pair, mine, 0, keepdims=False)
        given = lax.dynamic_index_in_dim(pair, 1 - mine, 0, keepdims=False)
        return jnp.concatenate([kept, lax.ppermute(given, "seq", seq_swap)], axis=0)

    def both_halves(tokens):
        given = lax.ppermute(tokens[rows_here:], "seq", seq_swap)
        kept = tokens[:rows_here]
        first = jnp.where(mine == 0, kept, given)
        second = jnp.where(mine == 0, given, kept)
        return jnp.stack([first, second], axis=0)

    class_range = jnp.arange(class_table.shape[0], dtype=jnp.int32)
    one_hot = (class_ids[:, None] == class_range[None, :]).astype(jnp.bfloat16)
    looked_up = jnp.dot(one_hot, class_table, preferred_element_type=jnp.float32)
    timing = lax.dynamic_slice_in_dim(
        time_features(timesteps, width_all), owner * columns, columns, 1
    )
    condition = looked_up + timing
    lifted_full, lift_pull = jax.vjp(lift_silu, condition)
    lifted = lifted_full.astype(jnp.bfloat16)
    mod_width = w_mod.shape[1]
    mod_cols = b_mod.shape[0]
    bias_line = lax.dynamic_update_slice_in_dim(
        jnp.zeros((mod_width,), jnp.float32), b_mod.astype(jnp.float32), owner * mod_cols, 0
    )
    lifted_mine = lax.dynamic_index_in_dim(
        lifted.reshape(fsdp_count, 2, columns), mine, 1, keepdims=False
    )
    small = [b_q, b_v, b_out, b_fc1, b_fc2]
    small_line = wide(jnp.concatenate(small))
    to_owners = jnp.concatenate(
        [
            jnp.dot(lifted_mine, w_mod, preferred_element_type=jnp.float32) + bias_line[None, :],
            jnp.broadcast_to(small_line[None, :], (fsdp_count, small_line.shape[0])),
        ],
        axis=1,
    )
    from_owners = lax.all_to_all(to_owners, "fsdp", 0, 0, tiled=True)
    input_tokens = whole_latent(latents)
    cotangent_tokens = whole_latent(out_cotangent)
    own_a = gather_half(jnp.concatenate([w_qkv, w_out], axis=1))
    own_b = gather_half(w_fc1)
    own_a, from_owners, input_tokens, cotangent_tokens, w_fc2 = tied(
        (own_a, from_owners, input_tokens, cotangent_tokens, w_fc2)
    )
    own_c = gather_half(w_fc2)
    seq_a = flip_seq(own_a)
    x_a = flip(own_a, 2)
    own_b, seq_a = tied((own_b, seq_a))
    both_a = flip(seq_a, 2)
    seq_b = flip_seq(own_b)
    x_b = flip(own_b, 2)

    modulation = jnp.sum(from_owners[:, :mod_width], axis=0, keepdims=True)
    shift_one, scale_one, gate_one, shift_two, scale_two, gate_two = [
        modulation[:, position * width_all : (position + 1) * width_all] for position in range(6)
    ]
    biases = []
    begin = mod_width
    for part in small:
        end = begin + part.shape[0]
        biases.append(from_owners[:, begin:end].reshape(1, -1))
        begin = end
    query_bias, value_bias, out_bias, up_bias, down_bias = biases

    inputs_full = wide(input_tokens)
    grad_output = wide(cotangent_tokens)
    normed_one, inverse_one = normalize_keep(inputs_full)
    entry_one = low(normed_one * (1.0 + scale_one) + shift_one)
    full_qkv, full_out = assemble(
        (own_a, flip(own_a, 1)),
        (seq_a, flip(seq_a, 1)),
        (x_a, flip(x_a, 1)),
        (both_a, flip(both_a, 1)),
        w_qkv.shape[1],
        w_out.shape[1],
    )
    full_qkv, x_b, seq_b, own_c = tied((full_qkv, x_b, seq_b, own_c))
    both_b = flip_seq(x_b)
    seq_c = flip_seq(own_c)
    x_c = flip(own_c, 2)
    qkv_bias = jnp.concatenate([query_bias, jnp.zeros_like(query_bias), value_bias], axis=1)
    projected = low(jnp.dot(entry_one, full_qkv, preferred_element_type=jnp.float32) + qkv_bias)
    mixed, log_totals = attend_local(projected)
    mixed, both_b, seq_c = tied((mixed, both_b, seq_c))
    both_c = flip(seq_c, 2)
    branch_one = jnp.dot(mixed, full_out, preferred_element_type=jnp.float32) + out_bias
    middle = inputs_full + gate_one * branch_one
    normed_two, inverse_two = normalize_keep(middle)
    entry_two = low(normed_two * (1.0 + scale_two) + shift_two)
    (full_fc1,) = assemble(
        (own_b, flip(own_b, 1)),
        (seq_b, flip(seq_b, 1)),
        (x_b, flip(x_b, 1)),
        (both_b, flip(both_b, 1)),
        w_fc1.shape[1],
    )
    full_fc1, x_c = tied((full_fc1, x_c))
    hidden = jnp.dot(entry_two, full_fc1, preferred_element_type=jnp.float32) + up_bias
    active_full, gelu_pull = jax.vjp(gelu_tanh, hidden)
    active = low(active_full)
    grad_branch_two = low(gate_two * grad_output)
    kept_fc2, leaving_fc2 = split_core(outer_sum(active, grad_branch_two))
    leaving_fc2, both_c = tied((leaving_fc2, both_c))
    arrived_fc2 = flip(leaving_fc2, 1)
    (full_fc2,) = assemble(
        (own_c, flip(own_c, 1)),
        (seq_c, flip(seq_c, 1)),
        (x_c, flip(x_c, 1)),
        (both_c, flip(both_c, 1)),
        w_fc2.shape[1],
    )
    branch_two = jnp.dot(active, full_fc2, preferred_element_type=jnp.float32) + down_bias
    result = both_halves(low(middle + gate_two * branch_two))
    grad_gate_two = jnp.sum(grad_output * branch_two, axis=0, keepdims=True)
    here_fc2, away_fc2 = split_x(kept_fc2, arrived_fc2)
    grad_branch_two, away_fc2 = tied((grad_branch_two, away_fc2))
    crossed_fc2 = flip(away_fc2, 2)
    grad_active = compared_with(grad_branch_two, full_fc2)
    grad_hidden = low(gelu_pull(grad_active)[0])
    kept_fc1, leaving_fc1 = split_core(outer_sum(entry_two, grad_hidden))
    grad_hidden, leaving_fc1, crossed_fc2 = tied((grad_hidden, leaving_fc1, crossed_fc2))
    arrived_fc1 = flip(leaving_fc1, 1)
    grad_entry_two = compared_with(grad_hidden, full_fc1)
    here_fc1, away_fc1 = split_x(kept_fc1, arrived_fc1)
    total_fc2, leaving_fc2 = split_z(here_fc2, crossed_fc2)
    grad_entry_two, leaving_fc2, away_fc1 = tied((grad_entry_two, leaving_fc2, away_fc1))
    crossed_fc1 = flip(away_fc1, 2)
    grad_shift_two = jnp.sum(grad_entry_two, axis=0, keepdims=True)
    grad_scale_two = jnp.sum(grad_entry_two * normed_two, axis=0, keepdims=True)
    grad_middle = grad_output + normalize_back(
        grad_entry_two * (1.0 + scale_two), normed_two, inverse_two
    )
    grad_gate_one = jnp.sum(grad_middle * branch_one, axis=0, keepdims=True)
    grad_branch_one = low(gate_one * grad_middle)
    landed_fc2 = send_z(leaving_fc2)
    kept_out, leaving_out = split_core(outer_sum(mixed, grad_branch_one))
    leaving_out, grad_branch_one = tied((leaving_out, grad_branch_one))
    arrived_out = flip(leaving_out, 1)
    grad_mixed = low(compared_with(grad_branch_one, full_out))
    grad_mixed, arrived_out = tied((grad_mixed, arrived_out))
    grad_project = jnp.concatenate(attend_local_back(projected, grad_mixed, log_totals), axis=1)
    crossed_fc1, grad_project, landed_fc2, result = tied(
        (crossed_fc1, grad_project, landed_fc2, result)
    )
    total_fc1, leaving_fc1 = split_z(here_fc1, crossed_fc1)
    grad_project, leaving_fc1 = tied((grad_project, leaving_fc1))
    landed_fc1 = send_z(leaving_fc1)
    kept_qkv, leaving_qkv = split_core(outer_sum(entry_one, grad_project))
    grad_project, leaving_qkv, landed_first = tied((grad_project, leaving_qkv, landed_fc1[0]))
    arrived_qkv = flip(leaving_qkv, 1)
    grad_entry_one = compared_with(grad_project, full_qkv)
    grad_entry_one, arrived_qkv, landed_second = tied(
        (grad_entry_one, arrived_qkv, landed_fc1[1])
    )
    here_last, away_last = [
        jnp.concatenate(parts, axis=-1)
        for parts in zip(split_x(kept_qkv, arrived_qkv), split_x(kept_out, arrived_out))
    ]
    grad_entry_one, away_last = tied((grad_entry_one, away_last))
    crossed_last = flip(away_last, 2)
    sum_fc2 = sum_seq(sum_z(total_fc2, landed_fc2))
    grad_shift_one = jnp.sum(grad_entry_one, axis=0, keepdims=True)
    grad_scale_one = jnp.sum(grad_entry_one * normed_one, axis=0, keepdims=True)
    grad_latents = both_halves(
        grad_middle
        + normalize_back(grad_entry_one * (1.0 + scale_one), normed_one, inverse_one)
    )
    grad_mod_mine = low(
        jnp.concatenate(
            [
                grad_shift_one,
                grad_scale_one,
                grad_gate_one,
                grad_shift_two,
                grad_scale_two,
                grad_gate_two,
            ],
            axis=1,
        )
    )
    mine_fc1 = sum_z(total_fc1, [landed_first, landed_second, *landed_fc1[2:]])
    grad_mod_mine, mine_fc1, crossed_last = tied((grad_mod_mine, mine_fc1, crossed_last))
    sum_fc1 = sum_seq(mine_fc1)
    total_last, leaving_last = split_z(here_last, crossed_last)
    grad_mod_mine, leaving_last, small_inputs = tied(
        (grad_mod_mine, leaving_last, (grad_project, grad_branch_one, grad_hidden, grad_branch_two))
    )
    landed_last = send_z(leaving_last)
    grad_mod_all = gather_latents(grad_mod_mine)
    sum_last = sum_seq(sum_z(total_last, landed_last))
    sum_qkv = sum_last[:, : 3 * width_all]
    sum_out = sum_last[:, 3 * width_all :]
    grad_project, grad_branch_one, grad_hidden, grad_branch_two = small_inputs
    grad_w_mod = outer_sum(lifted, grad_mod_all)
    grad_b_mod = jnp.sum(
        lax.dynamic_slice_in_dim(grad_mod_all, owner * mod_cols, mod_cols, 1).astype(jnp.float32),
        axis=0,
    )
    grad_lifted = compared_with(grad_mod_all, w_mod)
    grad_condition = lift_pull(grad_lifted)[0]
    grad_table = jnp.dot(
        one_hot.astype(jnp.float32).T,
        grad_condition,
        precision=lax.Precision.HIGHEST,
        preferred_element_type=jnp.float32,
    )
    grad_small = [
        wide(grad_project[:, :width_all]),
        wide(grad_project[:, 2 * width_all :]),
        wide(grad_branch_one),
        wide(grad_hidden),
        wide(grad_branch_two),
    ]
    small_sums = jnp.concatenate(
        [jnp.sum(part, axis=0).reshape(fsdp_count, -1) for part in grad_small], axis=1
    )
    small_here = jnp.sum(
        lax.all_to_all(small_sums, "fsdp", 0, 0, tiled=True), axis=0, keepdims=True
    )
    small_total = (small_here + lax.ppermute(small_here, "seq", seq_swap))[0]
    small_grads = []
    begin = 0
    for part in small:
        small_grads.append(small_total[begin : begin + part.shape[0]])
        begin += part.shape[0]
    return (
        result,
        grad_latents,
        grad_table,
        grad_w_mod,
        grad_b_mod,
        sum_qkv,
        small_grads[0],
        small_grads[1],
        sum_out,
        small_grads[2],
        sum_fc1,
        small_grads[3],
        sum_fc2,
        small_grads[4],
    )


def solution(mesh):
    placed = (
        P("fsdp", "seq", None),
        P(),
        P(),
        P(None, "fsdp"),
        P("fsdp", None),
        P("fsdp"),
        P("fsdp", None),
        P("fsdp"),
        P("fsdp"),
        P("fsdp", None),
        P("fsdp"),
        P("fsdp", None),
        P("fsdp"),
        P("fsdp", None),
        P("fsdp"),
        P("fsdp", "seq", None),
    )
    spans = mesh.shape["fsdp"]

    def body(*arrays):
        whole_fits = arrays[0].shape[0] == mesh.shape["seq"] == 2 and spans % 4 == 0
        return (local_whole_latent if whole_fits else local)(*arrays)

    return jax.shard_map(
        body,
        mesh=mesh,
        in_specs=placed,
        out_specs=(
            P("fsdp", "seq", None),
            P("fsdp", "seq", None),
            P(None, "fsdp"),
            P("fsdp", None),
            P("fsdp"),
            P("fsdp", None),
            P("fsdp"),
            P("fsdp"),
            P("fsdp", None),
            P("fsdp"),
            P("fsdp", None),
            P("fsdp"),
            P("fsdp", None),
            P("fsdp"),
        ),
        check_vma=False,
    )
```

```python
import math

import jax
import jax.numpy as jnp
from jax import lax
from jax.experimental import pallas as pl
from jax.experimental.pallas import tpu as pltpu
from jax.sharding import PartitionSpec as P

HEAD_DIM = 64


def time_features(step_ids, columns):
    half_width = columns // 2
    freqs = jnp.exp(-math.log(10000.0) * jnp.arange(half_width, dtype=jnp.float32) / half_width)
    angles = step_ids.astype(jnp.float32)[:, None] * freqs[None, :]
    return jnp.concatenate([jnp.cos(angles), jnp.sin(angles)], axis=1)


def normalize_keep(tensor):
    centered = tensor - jnp.mean(tensor, axis=-1, keepdims=True)
    variance = jnp.mean(centered * centered, axis=-1, keepdims=True)
    inverse = lax.rsqrt(variance + 1e-06)
    return (centered * inverse, inverse)


def normalize_back(grad_hat, normed, inverse):
    mean_grad = jnp.mean(grad_hat, axis=-1, keepdims=True)
    mean_cross = jnp.mean(grad_hat * normed, axis=-1, keepdims=True)
    return inverse * (grad_hat - mean_grad - normed * mean_cross)


def gelu_tanh(tensor):
    return (
        0.5
        * tensor
        * (1.0 + jnp.tanh(0.7978845608028654 * (tensor + 0.044715 * tensor * tensor * tensor)))
    )


def lift_silu(tensor):
    return tensor * jax.nn.sigmoid(tensor)


def outer_sum(earlier_value, latter):
    return lax.dot_general(
        earlier_value, latter, (((0,), (0,)), ((), ())), preferred_element_type=jnp.float32
    )


def compared_with(earlier_value, latter):
    return lax.dot_general(
        earlier_value, latter, (((1,), (1,)), ((), ())), preferred_element_type=jnp.float32
    )


def regroup(tensor, axis_pos, outer_count, inner_count):
    extents = tensor.shape
    splitted = (
        extents[:axis_pos]
        + (outer_count, inner_count, extents[axis_pos] // (outer_count * inner_count))
        + extents[axis_pos + 1 :]
    )
    swapped = jnp.swapaxes(tensor.reshape(splitted), axis_pos, axis_pos + 1)
    return swapped.reshape(extents)


def make_term(lefts, rights, ratio):
    first_left, second_left, third_left, fourth_left = lefts
    first_right, second_right, third_right, fourth_right = rights

    def term(start, count):
        qkv_part = outer_sum(first_left, first_right)
        out_part = outer_sum(second_left, second_right)
        fc1_part = outer_sum(third_left, third_right)
        fc2_part = outer_sum(fourth_left, fourth_right).reshape(
            count, ratio * fourth_right.shape[1]
        )
        return jnp.concatenate([qkv_part, out_part, fc1_part, fc2_part], axis=1)

    return term


def attend_heads(queries, keys_all, values_all, block_rows):
    length_all = queries.shape[0]
    head_count = queries.shape[1] // HEAD_DIM
    scaling = HEAD_DIM ** (-0.5)
    query_blocks = queries.reshape(length_all // block_rows, block_rows, head_count, HEAD_DIM)
    key_heads = keys_all.reshape(length_all, head_count, HEAD_DIM)
    value_heads = values_all.reshape(length_all, head_count, HEAD_DIM)

    def one_block(query_block):
        scores = (
            jnp.einsum("qhd,khd->hqk", query_block, key_heads, preferred_element_type=jnp.float32)
            * scaling
        )
        highest = jnp.max(scores, axis=-1, keepdims=True)
        powers = jnp.exp(scores - highest)
        totals = jnp.sum(powers, axis=-1, keepdims=True)
        weight_tensors = (powers / totals).astype(jnp.bfloat16)
        mixed = jnp.einsum(
            "hqk,khd->qhd", weight_tensors, value_heads, preferred_element_type=jnp.float32
        )
        return (mixed.astype(jnp.bfloat16), (highest + jnp.log(totals))[:, :, 0])

    mixed, log_totals = lax.map(one_block, query_blocks)
    return (mixed.reshape(length_all, head_count * HEAD_DIM), log_totals)


def attend_back(queries, keys_all, values_all, grad_mixed, log_totals, block_rows):
    length_all = queries.shape[0]
    head_count = queries.shape[1] // HEAD_DIM
    scaling = HEAD_DIM ** (-0.5)
    block_count = length_all // block_rows
    query_blocks = queries.reshape(block_count, block_rows, head_count, HEAD_DIM)
    grad_blocks = grad_mixed.reshape(block_count, block_rows, head_count, HEAD_DIM)
    key_heads = keys_all.reshape(length_all, head_count, HEAD_DIM)
    value_heads = values_all.reshape(length_all, head_count, HEAD_DIM)

    def one_block(carried, blocked):
        grad_keys, grad_values = carried
        query_block, grad_block, log_block = blocked
        scores = (
            jnp.einsum("qhd,khd->hqk", query_block, key_heads, preferred_element_type=jnp.float32)
            * scaling
        )
        probs = jnp.exp(scores - log_block[:, :, None])
        grad_values = grad_values + jnp.einsum(
            "hqk,qhd->khd",
            probs.astype(jnp.bfloat16),
            grad_block,
            preferred_element_type=jnp.float32,
        )
        grad_probs = jnp.einsum(
            "qhd,khd->hqk", grad_block, value_heads, preferred_element_type=jnp.float32
        )
        grad_scores = (
            probs * (grad_probs - jnp.sum(grad_probs * probs, axis=-1, keepdims=True))
        ).astype(jnp.bfloat16)
        grad_query = (
            jnp.einsum("hqk,khd->qhd", grad_scores, key_heads, preferred_element_type=jnp.float32)
            * scaling
        )
        grad_keys = (
            grad_keys
            + jnp.einsum(
                "hqk,qhd->khd", grad_scores, query_block, preferred_element_type=jnp.float32
            )
            * scaling
        )
        return ((grad_keys, grad_values), grad_query.astype(jnp.bfloat16))

    zeroed = jnp.zeros((length_all, head_count, HEAD_DIM), jnp.float32)
    (grad_keys, grad_values), grad_queries = lax.scan(
        one_block, (zeroed, zeroed), (query_blocks, grad_blocks, log_totals)
    )
    flat_width = head_count * HEAD_DIM
    return (
        grad_queries.reshape(length_all, flat_width),
        grad_keys.reshape(length_all, flat_width).astype(jnp.bfloat16),
        grad_values.reshape(length_all, flat_width).astype(jnp.bfloat16),
    )


def local(
    latents,
    timesteps,
    class_ids,
    class_table,
    w_mod,
    b_mod,
    w_qkv,
    b_q,
    b_v,
    w_out,
    b_out,
    w_fc1,
    b_fc1,
    w_fc2,
    b_fc2,
    out_cotangent,
):
    micro_count, row_count, width_all = latents.shape
    tokens_here = micro_count * row_count
    columns = class_table.shape[1]
    owner = lax.axis_index("fsdp")
    seq_count = lax.axis_size("seq")
    fsdp_count = lax.axis_size("fsdp")
    class_range = jnp.arange(class_table.shape[0], dtype=jnp.int32)
    one_hot = (class_ids[:, None] == class_range[None, :]).astype(jnp.bfloat16)
    looked_up = jnp.dot(one_hot, class_table, preferred_element_type=jnp.float32)
    timing = lax.dynamic_slice_in_dim(
        time_features(timesteps, width_all), owner * columns, columns, 1
    )
    condition = looked_up + timing
    lifted_full, lift_pull = jax.vjp(lift_silu, condition)
    lifted = lifted_full.astype(jnp.bfloat16)
    mod_width = w_mod.shape[1]
    mod_cols = b_mod.shape[0]
    bias_line = lax.dynamic_update_slice_in_dim(
        jnp.zeros((mod_width,), jnp.float32), b_mod.astype(jnp.float32), owner * mod_cols, 0
    )
    modulation = lax.psum_scatter(
        jnp.dot(lifted, w_mod, preferred_element_type=jnp.float32) + bias_line[None, :],
        "fsdp",
        scatter_dimension=0,
        tiled=True,
    )
    mod_parts = [
        modulation[:, None, position * width_all : (position + 1) * width_all]
        for position in range(6)
    ]
    shift_one, scale_one, gate_one, shift_two, scale_two, gate_two = mod_parts
    gathered = (
        lax.all_gather(w_qkv, "fsdp", axis=0, tiled=True),
        lax.all_gather(b_q, "fsdp", axis=0, tiled=True),
        lax.all_gather(b_v, "fsdp", axis=0, tiled=True),
        lax.all_gather(w_out, "fsdp", axis=0, tiled=True),
        lax.all_gather(b_out, "fsdp", axis=0, tiled=True),
        lax.all_gather(w_fc1, "fsdp", axis=0, tiled=True),
        lax.all_gather(b_fc1, "fsdp", axis=0, tiled=True),
        lax.all_gather(w_fc2, "fsdp", axis=0, tiled=True),
        lax.all_gather(b_fc2, "fsdp", axis=0, tiled=True),
    )
    (
        full_qkv,
        query_bias,
        value_bias,
        full_out,
        out_bias,
        full_fc1,
        up_bias,
        gathered_down_weight,
        down_bias,
    ) = gathered
    ratio = gathered_down_weight.shape[0] // width_all
    inputs_full = latents.astype(jnp.float32)
    normed_one, inverse_one = normalize_keep(inputs_full)
    entry_one = (
        (normed_one * (1.0 + scale_one) + shift_one)
        .astype(jnp.bfloat16)
        .reshape(tokens_here, width_all)
    )
    projected = jnp.dot(entry_one, full_qkv, preferred_element_type=jnp.float32)
    token_shape = (micro_count, row_count, width_all)
    queries = (
        (projected[:, :width_all] + query_bias.astype(jnp.float32))
        .astype(jnp.bfloat16)
        .reshape(token_shape)
    )
    keys_here = projected[:, width_all : 2 * width_all].astype(jnp.bfloat16).reshape(token_shape)
    values_here = (
        (projected[:, 2 * width_all :] + value_bias.astype(jnp.float32))
        .astype(jnp.bfloat16)
        .reshape(token_shape)
    )
    head_queries, head_keys, head_values = (
        lax.all_to_all(queries, "seq", split_axis=2, concat_axis=1, tiled=True),
        lax.all_to_all(keys_here, "seq", split_axis=2, concat_axis=1, tiled=True),
        lax.all_to_all(values_here, "seq", split_axis=2, concat_axis=1, tiled=True),
    )
    block_rows = min(1024, head_queries.shape[1])

    def attend_one(trio):
        return attend_heads(trio[0], trio[1], trio[2], block_rows)

    head_mixed, log_totals = lax.map(attend_one, (head_queries, head_keys, head_values))
    token_mixed = lax.all_to_all(
        head_mixed, "seq", split_axis=1, concat_axis=2, tiled=True
    ).reshape(tokens_here, width_all)
    branch_one = (
        jnp.dot(token_mixed, full_out, preferred_element_type=jnp.float32)
        + out_bias.astype(jnp.float32)
    ).reshape(token_shape)
    middle = inputs_full + gate_one * branch_one
    normed_two, inverse_two = normalize_keep(middle)
    entry_two = (
        (normed_two * (1.0 + scale_two) + shift_two)
        .astype(jnp.bfloat16)
        .reshape(tokens_here, width_all)
    )
    hidden = jnp.dot(entry_two, full_fc1, preferred_element_type=jnp.float32) + up_bias.astype(
        jnp.float32
    )
    active_full, gelu_pull = jax.vjp(gelu_tanh, hidden)
    active = active_full.astype(jnp.bfloat16)
    branch_two = (
        jnp.dot(active, gathered_down_weight, preferred_element_type=jnp.float32)
        + down_bias.astype(jnp.float32)
    ).reshape(token_shape)
    result = (middle + gate_two * branch_two).astype(jnp.bfloat16)
    grad_output = out_cotangent.astype(jnp.float32)
    grad_gate_two = jnp.sum(grad_output * branch_two, axis=1)
    grad_branch_two = (gate_two * grad_output).astype(jnp.bfloat16).reshape(tokens_here, width_all)
    grad_active = compared_with(grad_branch_two, gathered_down_weight)
    grad_hidden = gelu_pull(grad_active)[0].astype(jnp.bfloat16)
    grad_entry_two = compared_with(grad_hidden, full_fc1).reshape(token_shape)
    grad_shift_two = jnp.sum(grad_entry_two, axis=1)
    grad_scale_two = jnp.sum(grad_entry_two * normed_two, axis=1)
    grad_middle = grad_output + normalize_back(
        grad_entry_two * (1.0 + scale_two), normed_two, inverse_two
    )
    grad_gate_one = jnp.sum(grad_middle * branch_one, axis=1)
    grad_branch_one = (gate_one * grad_middle).astype(jnp.bfloat16).reshape(tokens_here, width_all)
    grad_mixed = compared_with(grad_branch_one, full_out).astype(jnp.bfloat16).reshape(token_shape)
    head_grads = lax.all_to_all(grad_mixed, "seq", split_axis=2, concat_axis=1, tiled=True)

    def back_one(grouped):
        return attend_back(grouped[0], grouped[1], grouped[2], grouped[3], grouped[4], block_rows)

    grad_heads_q, grad_heads_k, grad_heads_v = lax.map(
        back_one, (head_queries, head_keys, head_values, head_grads, log_totals)
    )
    grad_queries, grad_keys, grad_values = (
        lax.all_to_all(grad_heads_q, "seq", split_axis=1, concat_axis=2, tiled=True),
        lax.all_to_all(grad_heads_k, "seq", split_axis=1, concat_axis=2, tiled=True),
        lax.all_to_all(grad_heads_v, "seq", split_axis=1, concat_axis=2, tiled=True),
    )
    grad_project = jnp.concatenate([grad_queries, grad_keys, grad_values], axis=2).reshape(
        tokens_here, 3 * width_all
    )
    grad_entry_one = compared_with(grad_project, full_qkv).reshape(token_shape)
    grad_shift_one = jnp.sum(grad_entry_one, axis=1)
    grad_scale_one = jnp.sum(grad_entry_one * normed_one, axis=1)
    grad_latents = grad_middle + normalize_back(
        grad_entry_one * (1.0 + scale_one), normed_one, inverse_one
    )
    grad_mod_part = jnp.concatenate(
        [
            grad_shift_one,
            grad_scale_one,
            grad_gate_one,
            grad_shift_two,
            grad_scale_two,
            grad_gate_two,
        ],
        axis=1,
    )
    grad_mod_seq = lax.psum(grad_mod_part, "seq").astype(jnp.bfloat16)
    grad_mod_all = lax.all_gather(grad_mod_seq, "fsdp", axis=0, tiled=True)
    grad_w_mod = outer_sum(lifted, grad_mod_all)
    grad_b_mod = jnp.sum(
        lax.dynamic_slice_in_dim(grad_mod_all, owner * mod_cols, mod_cols, 1).astype(jnp.float32),
        axis=0,
    )
    grad_lifted = compared_with(grad_mod_all, w_mod)
    grad_condition = lift_pull(grad_lifted)[0]
    grad_table = jnp.dot(
        one_hot.astype(jnp.float32).T,
        grad_condition,
        precision=lax.Precision.HIGHEST,
        preferred_element_type=jnp.float32,
    )
    grad_q_bias = jnp.sum(grad_project[:, :width_all].astype(jnp.float32), axis=0)
    grad_v_bias = jnp.sum(grad_project[:, 2 * width_all :].astype(jnp.float32), axis=0)
    grad_out_bias = jnp.sum(grad_branch_one.astype(jnp.float32), axis=0)
    grad_up_bias = jnp.sum(grad_hidden.astype(jnp.float32), axis=0)
    grad_down_bias = jnp.sum(grad_branch_two.astype(jnp.float32), axis=0)
    rights = (grad_project, grad_branch_one, grad_hidden, grad_branch_two)
    lefts = (
        regroup(entry_one, 1, fsdp_count, seq_count),
        regroup(token_mixed, 1, fsdp_count, seq_count),
        regroup(entry_two, 1, fsdp_count, seq_count),
        regroup(active, 1, fsdp_count, seq_count),
    )
    wide_term = make_term(lefts, rights, ratio)
    wide = lax.psum_scatter(
        wide_term(
            jnp.int32(0), width_all // (fsdp_count * seq_count) * lax.axis_size(("seq", "fsdp"))
        ),
        ("seq", "fsdp"),
        scatter_dimension=0,
        tiled=True,
    )
    biases = (
        lax.psum_scatter(
            regroup(grad_q_bias, 0, fsdp_count, seq_count),
            ("seq", "fsdp"),
            scatter_dimension=0,
            tiled=True,
        ),
        lax.psum_scatter(
            regroup(grad_v_bias, 0, fsdp_count, seq_count),
            ("seq", "fsdp"),
            scatter_dimension=0,
            tiled=True,
        ),
        lax.psum_scatter(
            regroup(grad_out_bias, 0, fsdp_count, seq_count),
            ("seq", "fsdp"),
            scatter_dimension=0,
            tiled=True,
        ),
        lax.psum_scatter(
            regroup(grad_up_bias, 0, fsdp_count, seq_count),
            ("seq", "fsdp"),
            scatter_dimension=0,
            tiled=True,
        ),
        lax.psum_scatter(
            regroup(grad_down_bias, 0, fsdp_count, seq_count),
            ("seq", "fsdp"),
            scatter_dimension=0,
            tiled=True,
        ),
    )
    owned = (
        lax.all_gather(wide, "seq", axis=0, tiled=True),
        lax.all_gather(biases[0], "seq", axis=0, tiled=True),
        lax.all_gather(biases[1], "seq", axis=0, tiled=True),
        lax.all_gather(biases[2], "seq", axis=0, tiled=True),
        lax.all_gather(biases[3], "seq", axis=0, tiled=True),
        lax.all_gather(biases[4], "seq", axis=0, tiled=True),
    )
    wide_owned = owned[0]
    ff_width = full_fc1.shape[1]
    grad_w_qkv = wide_owned[:, : 3 * width_all]
    grad_w_out = wide_owned[:, 3 * width_all : 4 * width_all]
    grad_w_fc1 = wide_owned[:, 4 * width_all : 4 * width_all + ff_width]
    grad_w_fc2 = wide_owned[:, 4 * width_all + ff_width :].reshape(-1, width_all)
    return (
        result,
        grad_latents,
        grad_table,
        grad_w_mod,
        grad_b_mod,
        grad_w_qkv,
        owned[1],
        owned[2],
        grad_w_out,
        owned[3],
        grad_w_fc1,
        owned[4],
        grad_w_fc2,
        owned[5],
    )


def attend_kernel(q_ref, k_ref, v_ref, o_ref, lse_ref):
    for head in range(2):
        at = slice(head * HEAD_DIM, (head + 1) * HEAD_DIM)
        queries = q_ref[:, at] * jnp.bfloat16(HEAD_DIM ** (-0.5))
        scores = compared_with(k_ref[:, at], queries)
        highest = jnp.max(scores, axis=0, keepdims=True)
        powers = jnp.exp(scores - highest)
        totals = jnp.sum(powers, axis=0, keepdims=True)
        probs = (powers * (1.0 / totals)).astype(jnp.bfloat16)
        mixed = jnp.dot(v_ref[:, at].T, probs, preferred_element_type=jnp.float32)
        o_ref[:, at] = mixed.T.astype(jnp.bfloat16)
        lse_ref[0, head : head + 1, :] = highest + jnp.log(totals)


def attend_back_kernel(q_ref, k_ref, v_ref, do_ref, lse_ref, dq_ref, dk_ref, dv_ref):
    for head in range(2):
        at = slice(head * HEAD_DIM, (head + 1) * HEAD_DIM)
        queries = q_ref[:, at] * jnp.bfloat16(HEAD_DIM ** (-0.5))
        keys = k_ref[:, at]
        grad_mixed = do_ref[:, at]
        probs = jnp.exp(compared_with(keys, queries) - lse_ref[0, head : head + 1, :])
        dv_ref[:, at] = jnp.dot(
            probs.astype(jnp.bfloat16), grad_mixed, preferred_element_type=jnp.float32
        ).astype(jnp.bfloat16)
        grad_probs = compared_with(v_ref[:, at], grad_mixed)
        inner = jnp.sum(grad_probs * probs, axis=0, keepdims=True)
        grad_scores = (probs * (grad_probs - inner)).astype(jnp.bfloat16)
        dk_ref[:, at] = jnp.dot(
            grad_scores, queries, preferred_element_type=jnp.float32
        ).astype(jnp.bfloat16)
        scaled_keys = keys * jnp.bfloat16(HEAD_DIM ** (-0.5))
        grad_queries = jnp.dot(scaled_keys.T, grad_scores, preferred_element_type=jnp.float32)
        dq_ref[:, at] = grad_queries.T.astype(jnp.bfloat16)


VMEM_LIMIT = 48 * 1024 * 1024


def attend_local(projected):
    length, wide = projected.shape
    pairs = wide // 3 // 128

    def part(which):
        return pl.BlockSpec((length, 128), lambda i: (0, which * pairs + i))

    cost = pl.CostEstimate(
        flops=pairs * length * length,
        bytes_accessed=length * wide,
        transcendentals=0,
    )
    return pl.pallas_call(
        attend_kernel,
        grid=(pairs,),
        in_specs=[part(0), part(1), part(2)],
        out_specs=[part(0), pl.BlockSpec((1, 2, length), lambda i: (i, 0, 0))],
        out_shape=[
            jax.ShapeDtypeStruct((length, wide // 3), jnp.bfloat16),
            jax.ShapeDtypeStruct((pairs, 2, length), jnp.float32),
        ],
        compiler_params=pltpu.CompilerParams(vmem_limit_bytes=VMEM_LIMIT),
        cost_estimate=cost,
        name="attend",
    )(projected, projected, projected)


def attend_local_back(projected, grad_mixed, log_totals):
    length, wide = projected.shape
    pairs = wide // 3 // 128

    def part(which):
        return pl.BlockSpec((length, 128), lambda i: (0, which * pairs + i))

    cost = pl.CostEstimate(
        flops=pairs * length * length,
        bytes_accessed=length * wide,
        transcendentals=0,
    )
    grads = jax.ShapeDtypeStruct((length, wide // 3), jnp.bfloat16)
    return pl.pallas_call(
        attend_back_kernel,
        grid=(pairs,),
        in_specs=[
            part(0),
            part(1),
            part(2),
            part(0),
            pl.BlockSpec((1, 2, length), lambda i: (i, 0, 0)),
        ],
        out_specs=[part(0), part(0), part(0)],
        out_shape=[grads, grads, grads],
        compiler_params=pltpu.CompilerParams(vmem_limit_bytes=VMEM_LIMIT),
        cost_estimate=cost,
        name="attend_back",
    )(projected, projected, projected, grad_mixed, log_totals)


def swapped_pairs(count, bit):
    return [(place, place ^ bit) for place in range(count)]


def assemble_kernel(place_ref, *refs):
    del place_ref
    pieces, out_refs = refs[:8], refs[8:]
    for which, piece in enumerate(pieces):

        @pl.when(pl.program_id(0) == which)
        def _():
            begin = 0
            for out_ref in out_refs:
                end = begin + out_ref.shape[-1]
                out_ref[:, 0, 0] = piece[:, :, begin:end]
                begin = end


def gather_half(weight):
    rows = weight.shape[0] // 2
    half = lax.dynamic_slice_in_dim(weight, lax.axis_index("seq") * rows, rows, 0)
    z_groups = [
        [base + 4 * step for step in range(lax.axis_size("fsdp") // 4)] for base in range(4)
    ]
    return lax.all_gather(half, "fsdp", axis=0, tiled=False, axis_index_groups=z_groups)


def flip(tensor, bit):
    return lax.ppermute(tensor, "fsdp", swapped_pairs(lax.axis_size("fsdp"), bit))


def flip_seq(tensor):
    return lax.ppermute(tensor, "seq", swapped_pairs(2, 1))


def assemble(own, by_seq, by_x, by_both, *widths):
    depth, rows, columns = own[0].shape
    count = 4 * depth
    pieces = [*own, *by_seq, *by_x, *by_both]
    owner = lax.axis_index("fsdp")
    flips = jnp.asarray([0, 1, 0, 1, 2, 3, 2, 3], jnp.int32)
    halves = jnp.asarray([0, 0, 1, 1, 0, 0, 1, 1], jnp.int32)
    places = jnp.concatenate(
        [
            jnp.bitwise_xor(lax.rem(owner, 4), flips),
            jnp.bitwise_xor(lax.axis_index("seq"), halves),
        ]
    )

    piece_spec = pl.BlockSpec((depth, rows, columns), lambda p, place_ref: (0, 0, 0))

    def out_block(p, place_ref):
        return (0, place_ref[p], place_ref[8 + p], 0, 0)

    whole = pl.pallas_call(
        assemble_kernel,
        grid_spec=pltpu.PrefetchScalarGridSpec(
            num_scalar_prefetch=1,
            grid=(8,),
            in_specs=[piece_spec] * 8,
            out_specs=[pl.BlockSpec((depth, 1, 1, rows, width), out_block) for width in widths],
        ),
        out_shape=[
            jax.ShapeDtypeStruct((depth, 4, 2, rows, width), own[0].dtype) for width in widths
        ],
        compiler_params=pltpu.CompilerParams(vmem_limit_bytes=VMEM_LIMIT),
        cost_estimate=pl.CostEstimate(
            flops=0, bytes_accessed=depth * rows * columns, transcendentals=0
        ),
        name="assemble",
    )(places, *pieces)
    return [part.reshape(2 * count * rows, -1) for part in whole]


def doubled(tensor, place, axis, other):
    first = jnp.where(place == 0, tensor, other)
    second = jnp.where(place == 0, other, tensor)
    return jnp.stack([first, second], axis=axis)


def gather_latents(line):
    count = lax.axis_size("fsdp")
    depth = count // 4
    owner = lax.axis_index("fsdp")
    z_at = lax.div(owner, 4)
    tensor = doubled(line, lax.axis_index("seq"), 0, flip_seq(line))
    tensor = doubled(tensor, lax.rem(owner, 2), 0, flip(tensor, 1))
    tensor = tensor.reshape(4, -1)
    slots = [tensor]
    for shift in range(1, depth):
        pairs = [(place, (place + 4 * shift) % count) for place in range(count)]
        slots.append(lax.ppermute(tensor, "fsdp", pairs))
    ordered = []
    for z in range(depth):
        shift = lax.rem(z_at - z + depth, depth)
        chosen = slots[0]
        for step in range(1, depth):
            chosen = jnp.where(shift == step, slots[step], chosen)
        ordered.append(chosen)
    return jnp.stack(ordered, axis=0)


def gather_latents_x(tensor):
    x_at = lax.rem(lax.div(lax.axis_index("fsdp"), 2), 2)
    both = doubled(tensor, x_at, 1, flip(tensor, 2))
    return both.reshape(8 * tensor.shape[0], -1)


def low(tensor):
    return tensor.astype(jnp.bfloat16)


def wide(tensor):
    return tensor.astype(jnp.float32)


def pick(tensor, axis, place):
    return lax.dynamic_index_in_dim(tensor, place, axis, keepdims=False)


def split_core(partial):
    count = lax.axis_size("fsdp")
    core_at = lax.rem(lax.axis_index("fsdp"), 2)
    rows, columns = partial.shape
    blocks = low(partial).reshape(count // 4, 2, 2, rows // count, columns)
    return pick(blocks, 2, core_at), pick(blocks, 2, 1 - core_at)


def split_x(kept, arrived):
    x_at = lax.rem(lax.div(lax.axis_index("fsdp"), 2), 2)
    here = wide(pick(kept, 1, x_at)) + wide(pick(arrived, 1, x_at))
    return here, low(wide(pick(kept, 1, 1 - x_at)) + wide(pick(arrived, 1, 1 - x_at)))


def split_z(here, crossed):
    depth = here.shape[0]
    z_at = lax.div(lax.axis_index("fsdp"), 4)
    leaving = []
    for shift in range(1, depth):
        target = lax.rem(z_at + shift, depth)
        leaving.append(low(pick(here, 0, target) + wide(pick(crossed, 0, target))))
    return pick(here, 0, z_at) + wide(pick(crossed, 0, z_at)), leaving


def send_z(leaving):
    count = lax.axis_size("fsdp")
    arrived = []
    for shift, part in enumerate(leaving, 1):
        pairs = [(place, (place + 4 * shift) % count) for place in range(count)]
        arrived.append(lax.ppermute(part, "fsdp", pairs))
    return arrived


def sum_z(total, arrived):
    for part in arrived:
        total = total + wide(part)
    return low(total)


def sum_seq(mine):
    return wide(mine) + wide(lax.ppermute(mine, "seq", swapped_pairs(2, 1)))


tied = lax.optimization_barrier


def local_whole_latent(
    latents,
    timesteps,
    class_ids,
    class_table,
    w_mod,
    b_mod,
    w_qkv,
    b_q,
    b_v,
    w_out,
    b_out,
    w_fc1,
    b_fc1,
    w_fc2,
    b_fc2,
    out_cotangent,
):
    rows_here, width_all = latents.shape[1:]
    columns = class_table.shape[1]
    owner = lax.axis_index("fsdp")
    mine = lax.axis_index("seq")
    fsdp_count = lax.axis_size("fsdp")
    seq_swap = swapped_pairs(2, 1)

    def whole_latent(pair):
        kept = lax.dynamic_index_in_dim(pair, mine, 0, keepdims=False)
        given = lax.dynamic_index_in_dim(pair, 1 - mine, 0, keepdims=False)
        return jnp.concatenate([kept, lax.ppermute(given, "seq", seq_swap)], axis=0)

    def both_halves(tokens):
        given = lax.ppermute(tokens[rows_here:], "seq", seq_swap)
        kept = tokens[:rows_here]
        first = jnp.where(mine == 0, kept, given)
        second = jnp.where(mine == 0, given, kept)
        return jnp.stack([first, second], axis=0)

    class_range = jnp.arange(class_table.shape[0], dtype=jnp.int32)
    one_hot = (class_ids[:, None] == class_range[None, :]).astype(jnp.bfloat16)
    looked_up = jnp.dot(one_hot, class_table, preferred_element_type=jnp.float32)
    timing = lax.dynamic_slice_in_dim(
        time_features(timesteps, width_all), owner * columns, columns, 1
    )
    condition = looked_up + timing
    lifted_full, lift_pull = jax.vjp(lift_silu, condition)
    lifted = lifted_full.astype(jnp.bfloat16)
    mod_width = w_mod.shape[1]
    mod_cols = b_mod.shape[0]
    bias_line = lax.dynamic_update_slice_in_dim(
        jnp.zeros((mod_width,), jnp.float32), b_mod.astype(jnp.float32), owner * mod_cols, 0
    )
    lifted_mine = lax.dynamic_index_in_dim(
        lifted.reshape(fsdp_count, 2, columns), mine, 1, keepdims=False
    )
    small = [b_q, b_v, b_out, b_fc1, b_fc2]
    small_line = wide(jnp.concatenate(small))
    to_owners = jnp.concatenate(
        [
            jnp.dot(lifted_mine, w_mod, preferred_element_type=jnp.float32) + bias_line[None, :],
            jnp.broadcast_to(small_line[None, :], (fsdp_count, small_line.shape[0])),
        ],
        axis=1,
    )
    from_owners = lax.all_to_all(to_owners, "fsdp", 0, 0, tiled=True)
    input_tokens = whole_latent(latents)
    cotangent_tokens = whole_latent(out_cotangent)
    own_a = gather_half(jnp.concatenate([w_qkv, w_out], axis=1))
    own_b = gather_half(w_fc1)
    own_a, from_owners, input_tokens, cotangent_tokens, w_fc2 = tied(
        (own_a, from_owners, input_tokens, cotangent_tokens, w_fc2)
    )
    own_c = gather_half(w_fc2)
    seq_a = flip_seq(own_a)
    x_a = flip(own_a, 2)
    own_b, seq_a = tied((own_b, seq_a))
    both_a = flip(seq_a, 2)
    seq_b = flip_seq(own_b)
    x_b = flip(own_b, 2)

    modulation = jnp.sum(from_owners[:, :mod_width], axis=0, keepdims=True)
    shift_one, scale_one, gate_one, shift_two, scale_two, gate_two = [
        modulation[:, position * width_all : (position + 1) * width_all] for position in range(6)
    ]
    biases = []
    begin = mod_width
    for part in small:
        end = begin + part.shape[0]
        biases.append(from_owners[:, begin:end].reshape(1, -1))
        begin = end
    query_bias, value_bias, out_bias, up_bias, down_bias = biases

    inputs_full = wide(input_tokens)
    grad_output = wide(cotangent_tokens)
    normed_one, inverse_one = normalize_keep(inputs_full)
    entry_one = low(normed_one * (1.0 + scale_one) + shift_one)
    full_qkv, full_out = assemble(
        (own_a, flip(own_a, 1)),
        (seq_a, flip(seq_a, 1)),
        (x_a, flip(x_a, 1)),
        (both_a, flip(both_a, 1)),
        w_qkv.shape[1],
        w_out.shape[1],
    )
    full_qkv, x_b, seq_b, own_c = tied((full_qkv, x_b, seq_b, own_c))
    both_b = flip_seq(x_b)
    seq_c = flip_seq(own_c)
    x_c = flip(own_c, 2)
    qkv_bias = jnp.concatenate([query_bias, jnp.zeros_like(query_bias), value_bias], axis=1)
    projected = low(jnp.dot(entry_one, full_qkv, preferred_element_type=jnp.float32) + qkv_bias)
    mixed, log_totals = attend_local(projected)
    mixed, both_b = tied((mixed, both_b))
    branch_one = jnp.dot(mixed, full_out, preferred_element_type=jnp.float32) + out_bias
    middle = inputs_full + gate_one * branch_one
    normed_two, inverse_two = normalize_keep(middle)
    entry_two = low(normed_two * (1.0 + scale_two) + shift_two)
    (full_fc1,) = assemble(
        (own_b, flip(own_b, 1)),
        (seq_b, flip(seq_b, 1)),
        (x_b, flip(x_b, 1)),
        (both_b, flip(both_b, 1)),
        w_fc1.shape[1],
    )
    full_fc1, x_c, seq_c = tied((full_fc1, x_c, seq_c))
    both_c = flip(seq_c, 2)
    hidden = jnp.dot(entry_two, full_fc1, preferred_element_type=jnp.float32) + up_bias
    active_full, gelu_pull = jax.vjp(gelu_tanh, hidden)
    active = low(active_full)
    grad_branch_two = low(gate_two * grad_output)
    kept_fc2, leaving_fc2 = split_core(outer_sum(active, grad_branch_two))
    leaving_fc2, both_c = tied((leaving_fc2, both_c))
    arrived_fc2 = flip(leaving_fc2, 1)
    here_fc2, away_fc2 = split_x(kept_fc2, arrived_fc2)
    own_c, away_fc2 = tied((own_c, away_fc2))
    crossed_fc2 = flip(away_fc2, 2)
    (full_fc2,) = assemble(
        (own_c, flip(own_c, 1)),
        (seq_c, flip(seq_c, 1)),
        (x_c, flip(x_c, 1)),
        (both_c, flip(both_c, 1)),
        w_fc2.shape[1],
    )
    branch_two = jnp.dot(active, full_fc2, preferred_element_type=jnp.float32) + down_bias
    result = both_halves(low(middle + gate_two * branch_two))
    grad_gate_two = jnp.sum(grad_output * branch_two, axis=0, keepdims=True)
    grad_active = compared_with(grad_branch_two, full_fc2)
    grad_hidden = low(gelu_pull(grad_active)[0])
    kept_fc1, leaving_fc1 = split_core(outer_sum(entry_two, grad_hidden))
    grad_hidden, leaving_fc1, crossed_fc2 = tied((grad_hidden, leaving_fc1, crossed_fc2))
    arrived_fc1 = flip(leaving_fc1, 1)
    grad_entry_two = compared_with(grad_hidden, full_fc1)
    here_fc1, away_fc1 = split_x(kept_fc1, arrived_fc1)
    total_fc2, leaving_fc2 = split_z(here_fc2, crossed_fc2)
    grad_entry_two, leaving_fc2, away_fc1 = tied((grad_entry_two, leaving_fc2, away_fc1))
    crossed_fc1 = flip(away_fc1, 2)
    grad_shift_two = jnp.sum(grad_entry_two, axis=0, keepdims=True)
    grad_scale_two = jnp.sum(grad_entry_two * normed_two, axis=0, keepdims=True)
    grad_middle = grad_output + normalize_back(
        grad_entry_two * (1.0 + scale_two), normed_two, inverse_two
    )
    grad_gate_one = jnp.sum(grad_middle * branch_one, axis=0, keepdims=True)
    grad_branch_one = low(gate_one * grad_middle)
    landed_fc2 = send_z(leaving_fc2)
    kept_out, leaving_out = split_core(outer_sum(mixed, grad_branch_one))
    leaving_out, grad_branch_one = tied((leaving_out, grad_branch_one))
    arrived_out = flip(leaving_out, 1)
    grad_mixed = low(compared_with(grad_branch_one, full_out))
    grad_mixed, arrived_out = tied((grad_mixed, arrived_out))
    grad_project = jnp.concatenate(attend_local_back(projected, grad_mixed, log_totals), axis=1)
    crossed_fc1, grad_project, landed_fc2, result = tied(
        (crossed_fc1, grad_project, landed_fc2, result)
    )
    total_fc1, leaving_fc1 = split_z(here_fc1, crossed_fc1)
    grad_project, leaving_fc1 = tied((grad_project, leaving_fc1))
    landed_fc1 = send_z(leaving_fc1)
    kept_qkv, leaving_qkv = split_core(outer_sum(entry_one, grad_project))
    grad_project, leaving_qkv, landed_first = tied((grad_project, leaving_qkv, landed_fc1[0]))
    arrived_qkv = flip(leaving_qkv, 1)
    grad_entry_one = compared_with(grad_project, full_qkv)
    grad_entry_one, arrived_qkv = tied((grad_entry_one, arrived_qkv))
    here_last, away_last = [
        jnp.concatenate(parts, axis=-1)
        for parts in zip(split_x(kept_qkv, arrived_qkv), split_x(kept_out, arrived_out))
    ]
    small_inputs = (grad_project, grad_branch_one, grad_hidden, grad_branch_two)
    grad_entry_one, away_last, small_inputs, total_fc1 = tied(
        (grad_entry_one, away_last, small_inputs, total_fc1)
    )
    middle_row = away_last.shape[1] // 2
    crossed_early = flip(away_last[:, :middle_row], 2)
    crossed_late = flip(away_last[:, middle_row:], 2)
    sum_fc2 = sum_seq(sum_z(total_fc2, landed_fc2))
    grad_shift_one = jnp.sum(grad_entry_one, axis=0, keepdims=True)
    grad_scale_one = jnp.sum(grad_entry_one * normed_one, axis=0, keepdims=True)
    grad_latents = both_halves(
        grad_middle
        + normalize_back(grad_entry_one * (1.0 + scale_one), normed_one, inverse_one)
    )
    grad_mod_mine = low(
        jnp.concatenate(
            [
                grad_shift_one,
                grad_scale_one,
                grad_gate_one,
                grad_shift_two,
                grad_scale_two,
                grad_gate_two,
            ],
            axis=1,
        )
    )
    grad_mod_mine, small_inputs, crossed_early = tied(
        (grad_mod_mine, small_inputs, crossed_early)
    )
    grad_mod_z = gather_latents(grad_mod_mine)
    grad_project, grad_branch_one, grad_hidden, grad_branch_two = small_inputs
    grad_small = [
        wide(grad_project[:, :width_all]),
        wide(grad_project[:, 2 * width_all :]),
        wide(grad_branch_one),
        wide(grad_hidden),
        wide(grad_branch_two),
    ]
    small_sums = jnp.concatenate(
        [jnp.sum(part, axis=0).reshape(fsdp_count, -1) for part in grad_small], axis=1
    )
    small_here = jnp.sum(
        lax.all_to_all(small_sums, "fsdp", 0, 0, tiled=True), axis=0, keepdims=True
    )
    mine_fc1 = sum_z(total_fc1, [landed_first, *landed_fc1[1:]])
    mine_fc1, crossed_late, small_here, grad_mod_z, grad_latents = tied(
        (mine_fc1, crossed_late, small_here, grad_mod_z, grad_latents)
    )
    crossed_last = jnp.concatenate([crossed_early, crossed_late], axis=1)
    sum_fc1 = sum_seq(mine_fc1)
    total_last, leaving_last = split_z(here_last, crossed_last)
    landed_last = send_z(leaving_last)
    grad_mod_all = gather_latents_x(grad_mod_z)
    sum_last = sum_seq(sum_z(total_last, landed_last))
    sum_qkv = sum_last[:, : 3 * width_all]
    sum_out = sum_last[:, 3 * width_all :]
    small_total = (small_here + lax.ppermute(small_here, "seq", seq_swap))[0]
    small_grads = []
    begin = 0
    for part in small:
        small_grads.append(small_total[begin : begin + part.shape[0]])
        begin += part.shape[0]
    grad_w_mod = outer_sum(lifted, grad_mod_all)
    grad_b_mod = jnp.sum(
        lax.dynamic_slice_in_dim(grad_mod_all, owner * mod_cols, mod_cols, 1).astype(jnp.float32),
        axis=0,
    )
    grad_lifted = compared_with(grad_mod_all, w_mod)
    grad_condition = lift_pull(grad_lifted)[0]
    grad_table = jnp.dot(
        one_hot.astype(jnp.float32).T,
        grad_condition,
        precision=lax.Precision.HIGHEST,
        preferred_element_type=jnp.float32,
    )
    return (
        result,
        grad_latents,
        grad_table,
        grad_w_mod,
        grad_b_mod,
        sum_qkv,
        small_grads[0],
        small_grads[1],
        sum_out,
        small_grads[2],
        sum_fc1,
        small_grads[3],
        sum_fc2,
        small_grads[4],
    )


def solution(mesh):
    placed = (
        P("fsdp", "seq", None),
        P(),
        P(),
        P(None, "fsdp"),
        P("fsdp", None),
        P("fsdp"),
        P("fsdp", None),
        P("fsdp"),
        P("fsdp"),
        P("fsdp", None),
        P("fsdp"),
        P("fsdp", None),
        P("fsdp"),
        P("fsdp", None),
        P("fsdp"),
        P("fsdp", "seq", None),
    )
    spans = mesh.shape["fsdp"]

    def body(*arrays):
        whole_fits = arrays[0].shape[0] == mesh.shape["seq"] == 2 and spans % 4 == 0
        return (local_whole_latent if whole_fits else local)(*arrays)

    return jax.shard_map(
        body,
        mesh=mesh,
        in_specs=placed,
        out_specs=(
            P("fsdp", "seq", None),
            P("fsdp", "seq", None),
            P(None, "fsdp"),
            P("fsdp", None),
            P("fsdp"),
            P("fsdp", None),
            P("fsdp"),
            P("fsdp"),
            P("fsdp", None),
            P("fsdp"),
            P("fsdp", None),
            P("fsdp"),
            P("fsdp", None),
            P("fsdp"),
        ),
        check_vma=False,
    )
```

```python
import math

import jax
import jax.numpy as jnp
from jax import lax
from jax.experimental import pallas as pl
from jax.experimental.pallas import tpu as pltpu
from jax.sharding import PartitionSpec as P

HEAD_DIM = 64


def time_features(step_ids, columns):
    half_width = columns // 2
    freqs = jnp.exp(-math.log(10000.0) * jnp.arange(half_width, dtype=jnp.float32) / half_width)
    angles = step_ids.astype(jnp.float32)[:, None] * freqs[None, :]
    return jnp.concatenate([jnp.cos(angles), jnp.sin(angles)], axis=1)


def normalize_keep(tensor):
    centered = tensor - jnp.mean(tensor, axis=-1, keepdims=True)
    variance = jnp.mean(centered * centered, axis=-1, keepdims=True)
    inverse = lax.rsqrt(variance + 1e-06)
    return (centered * inverse, inverse)


def normalize_back(grad_hat, normed, inverse):
    mean_grad = jnp.mean(grad_hat, axis=-1, keepdims=True)
    mean_cross = jnp.mean(grad_hat * normed, axis=-1, keepdims=True)
    return inverse * (grad_hat - mean_grad - normed * mean_cross)


def gelu_tanh(tensor):
    return (
        0.5
        * tensor
        * (1.0 + jnp.tanh(0.7978845608028654 * (tensor + 0.044715 * tensor * tensor * tensor)))
    )


def lift_silu(tensor):
    return tensor * jax.nn.sigmoid(tensor)


def outer_sum(earlier_value, latter):
    return lax.dot_general(
        earlier_value, latter, (((0,), (0,)), ((), ())), preferred_element_type=jnp.float32
    )


def compared_with(earlier_value, latter):
    return lax.dot_general(
        earlier_value, latter, (((1,), (1,)), ((), ())), preferred_element_type=jnp.float32
    )


def regroup(tensor, axis_pos, outer_count, inner_count):
    extents = tensor.shape
    splitted = (
        extents[:axis_pos]
        + (outer_count, inner_count, extents[axis_pos] // (outer_count * inner_count))
        + extents[axis_pos + 1 :]
    )
    swapped = jnp.swapaxes(tensor.reshape(splitted), axis_pos, axis_pos + 1)
    return swapped.reshape(extents)


def make_term(lefts, rights, ratio):
    first_left, second_left, third_left, fourth_left = lefts
    first_right, second_right, third_right, fourth_right = rights

    def term(start, count):
        qkv_part = outer_sum(first_left, first_right)
        out_part = outer_sum(second_left, second_right)
        fc1_part = outer_sum(third_left, third_right)
        fc2_part = outer_sum(fourth_left, fourth_right).reshape(
            count, ratio * fourth_right.shape[1]
        )
        return jnp.concatenate([qkv_part, out_part, fc1_part, fc2_part], axis=1)

    return term


def attend_heads(queries, keys_all, values_all, block_rows):
    length_all = queries.shape[0]
    head_count = queries.shape[1] // HEAD_DIM
    scaling = HEAD_DIM ** (-0.5)
    query_blocks = queries.reshape(length_all // block_rows, block_rows, head_count, HEAD_DIM)
    key_heads = keys_all.reshape(length_all, head_count, HEAD_DIM)
    value_heads = values_all.reshape(length_all, head_count, HEAD_DIM)

    def one_block(query_block):
        scores = (
            jnp.einsum("qhd,khd->hqk", query_block, key_heads, preferred_element_type=jnp.float32)
            * scaling
        )
        highest = jnp.max(scores, axis=-1, keepdims=True)
        powers = jnp.exp(scores - highest)
        totals = jnp.sum(powers, axis=-1, keepdims=True)
        weight_tensors = (powers / totals).astype(jnp.bfloat16)
        mixed = jnp.einsum(
            "hqk,khd->qhd", weight_tensors, value_heads, preferred_element_type=jnp.float32
        )
        return (mixed.astype(jnp.bfloat16), (highest + jnp.log(totals))[:, :, 0])

    mixed, log_totals = lax.map(one_block, query_blocks)
    return (mixed.reshape(length_all, head_count * HEAD_DIM), log_totals)


def attend_back(queries, keys_all, values_all, grad_mixed, log_totals, block_rows):
    length_all = queries.shape[0]
    head_count = queries.shape[1] // HEAD_DIM
    scaling = HEAD_DIM ** (-0.5)
    block_count = length_all // block_rows
    query_blocks = queries.reshape(block_count, block_rows, head_count, HEAD_DIM)
    grad_blocks = grad_mixed.reshape(block_count, block_rows, head_count, HEAD_DIM)
    key_heads = keys_all.reshape(length_all, head_count, HEAD_DIM)
    value_heads = values_all.reshape(length_all, head_count, HEAD_DIM)

    def one_block(carried, blocked):
        grad_keys, grad_values = carried
        query_block, grad_block, log_block = blocked
        scores = (
            jnp.einsum("qhd,khd->hqk", query_block, key_heads, preferred_element_type=jnp.float32)
            * scaling
        )
        probs = jnp.exp(scores - log_block[:, :, None])
        grad_values = grad_values + jnp.einsum(
            "hqk,qhd->khd",
            probs.astype(jnp.bfloat16),
            grad_block,
            preferred_element_type=jnp.float32,
        )
        grad_probs = jnp.einsum(
            "qhd,khd->hqk", grad_block, value_heads, preferred_element_type=jnp.float32
        )
        grad_scores = (
            probs * (grad_probs - jnp.sum(grad_probs * probs, axis=-1, keepdims=True))
        ).astype(jnp.bfloat16)
        grad_query = (
            jnp.einsum("hqk,khd->qhd", grad_scores, key_heads, preferred_element_type=jnp.float32)
            * scaling
        )
        grad_keys = (
            grad_keys
            + jnp.einsum(
                "hqk,qhd->khd", grad_scores, query_block, preferred_element_type=jnp.float32
            )
            * scaling
        )
        return ((grad_keys, grad_values), grad_query.astype(jnp.bfloat16))

    zeroed = jnp.zeros((length_all, head_count, HEAD_DIM), jnp.float32)
    (grad_keys, grad_values), grad_queries = lax.scan(
        one_block, (zeroed, zeroed), (query_blocks, grad_blocks, log_totals)
    )
    flat_width = head_count * HEAD_DIM
    return (
        grad_queries.reshape(length_all, flat_width),
        grad_keys.reshape(length_all, flat_width).astype(jnp.bfloat16),
        grad_values.reshape(length_all, flat_width).astype(jnp.bfloat16),
    )


def local(
    latents,
    timesteps,
    class_ids,
    class_table,
    w_mod,
    b_mod,
    w_qkv,
    b_q,
    b_v,
    w_out,
    b_out,
    w_fc1,
    b_fc1,
    w_fc2,
    b_fc2,
    out_cotangent,
):
    micro_count, row_count, width_all = latents.shape
    tokens_here = micro_count * row_count
    columns = class_table.shape[1]
    owner = lax.axis_index("fsdp")
    seq_count = lax.axis_size("seq")
    fsdp_count = lax.axis_size("fsdp")
    class_range = jnp.arange(class_table.shape[0], dtype=jnp.int32)
    one_hot = (class_ids[:, None] == class_range[None, :]).astype(jnp.bfloat16)
    looked_up = jnp.dot(one_hot, class_table, preferred_element_type=jnp.float32)
    timing = lax.dynamic_slice_in_dim(
        time_features(timesteps, width_all), owner * columns, columns, 1
    )
    condition = looked_up + timing
    lifted_full, lift_pull = jax.vjp(lift_silu, condition)
    lifted = lifted_full.astype(jnp.bfloat16)
    mod_width = w_mod.shape[1]
    mod_cols = b_mod.shape[0]
    bias_line = lax.dynamic_update_slice_in_dim(
        jnp.zeros((mod_width,), jnp.float32), b_mod.astype(jnp.float32), owner * mod_cols, 0
    )
    modulation = lax.psum_scatter(
        jnp.dot(lifted, w_mod, preferred_element_type=jnp.float32) + bias_line[None, :],
        "fsdp",
        scatter_dimension=0,
        tiled=True,
    )
    mod_parts = [
        modulation[:, None, position * width_all : (position + 1) * width_all]
        for position in range(6)
    ]
    shift_one, scale_one, gate_one, shift_two, scale_two, gate_two = mod_parts
    gathered = (
        lax.all_gather(w_qkv, "fsdp", axis=0, tiled=True),
        lax.all_gather(b_q, "fsdp", axis=0, tiled=True),
        lax.all_gather(b_v, "fsdp", axis=0, tiled=True),
        lax.all_gather(w_out, "fsdp", axis=0, tiled=True),
        lax.all_gather(b_out, "fsdp", axis=0, tiled=True),
        lax.all_gather(w_fc1, "fsdp", axis=0, tiled=True),
        lax.all_gather(b_fc1, "fsdp", axis=0, tiled=True),
        lax.all_gather(w_fc2, "fsdp", axis=0, tiled=True),
        lax.all_gather(b_fc2, "fsdp", axis=0, tiled=True),
    )
    (
        full_qkv,
        query_bias,
        value_bias,
        full_out,
        out_bias,
        full_fc1,
        up_bias,
        gathered_down_weight,
        down_bias,
    ) = gathered
    ratio = gathered_down_weight.shape[0] // width_all
    inputs_full = latents.astype(jnp.float32)
    normed_one, inverse_one = normalize_keep(inputs_full)
    entry_one = (
        (normed_one * (1.0 + scale_one) + shift_one)
        .astype(jnp.bfloat16)
        .reshape(tokens_here, width_all)
    )
    projected = jnp.dot(entry_one, full_qkv, preferred_element_type=jnp.float32)
    token_shape = (micro_count, row_count, width_all)
    queries = (
        (projected[:, :width_all] + query_bias.astype(jnp.float32))
        .astype(jnp.bfloat16)
        .reshape(token_shape)
    )
    keys_here = projected[:, width_all : 2 * width_all].astype(jnp.bfloat16).reshape(token_shape)
    values_here = (
        (projected[:, 2 * width_all :] + value_bias.astype(jnp.float32))
        .astype(jnp.bfloat16)
        .reshape(token_shape)
    )
    head_queries, head_keys, head_values = (
        lax.all_to_all(queries, "seq", split_axis=2, concat_axis=1, tiled=True),
        lax.all_to_all(keys_here, "seq", split_axis=2, concat_axis=1, tiled=True),
        lax.all_to_all(values_here, "seq", split_axis=2, concat_axis=1, tiled=True),
    )
    block_rows = min(1024, head_queries.shape[1])

    def attend_one(trio):
        return attend_heads(trio[0], trio[1], trio[2], block_rows)

    head_mixed, log_totals = lax.map(attend_one, (head_queries, head_keys, head_values))
    token_mixed = lax.all_to_all(
        head_mixed, "seq", split_axis=1, concat_axis=2, tiled=True
    ).reshape(tokens_here, width_all)
    branch_one = (
        jnp.dot(token_mixed, full_out, preferred_element_type=jnp.float32)
        + out_bias.astype(jnp.float32)
    ).reshape(token_shape)
    middle = inputs_full + gate_one * branch_one
    normed_two, inverse_two = normalize_keep(middle)
    entry_two = (
        (normed_two * (1.0 + scale_two) + shift_two)
        .astype(jnp.bfloat16)
        .reshape(tokens_here, width_all)
    )
    hidden = jnp.dot(entry_two, full_fc1, preferred_element_type=jnp.float32) + up_bias.astype(
        jnp.float32
    )
    active_full, gelu_pull = jax.vjp(gelu_tanh, hidden)
    active = active_full.astype(jnp.bfloat16)
    branch_two = (
        jnp.dot(active, gathered_down_weight, preferred_element_type=jnp.float32)
        + down_bias.astype(jnp.float32)
    ).reshape(token_shape)
    result = (middle + gate_two * branch_two).astype(jnp.bfloat16)
    grad_output = out_cotangent.astype(jnp.float32)
    grad_gate_two = jnp.sum(grad_output * branch_two, axis=1)
    grad_branch_two = (gate_two * grad_output).astype(jnp.bfloat16).reshape(tokens_here, width_all)
    grad_active = compared_with(grad_branch_two, gathered_down_weight)
    grad_hidden = gelu_pull(grad_active)[0].astype(jnp.bfloat16)
    grad_entry_two = compared_with(grad_hidden, full_fc1).reshape(token_shape)
    grad_shift_two = jnp.sum(grad_entry_two, axis=1)
    grad_scale_two = jnp.sum(grad_entry_two * normed_two, axis=1)
    grad_middle = grad_output + normalize_back(
        grad_entry_two * (1.0 + scale_two), normed_two, inverse_two
    )
    grad_gate_one = jnp.sum(grad_middle * branch_one, axis=1)
    grad_branch_one = (gate_one * grad_middle).astype(jnp.bfloat16).reshape(tokens_here, width_all)
    grad_mixed = compared_with(grad_branch_one, full_out).astype(jnp.bfloat16).reshape(token_shape)
    head_grads = lax.all_to_all(grad_mixed, "seq", split_axis=2, concat_axis=1, tiled=True)

    def back_one(grouped):
        return attend_back(grouped[0], grouped[1], grouped[2], grouped[3], grouped[4], block_rows)

    grad_heads_q, grad_heads_k, grad_heads_v = lax.map(
        back_one, (head_queries, head_keys, head_values, head_grads, log_totals)
    )
    grad_queries, grad_keys, grad_values = (
        lax.all_to_all(grad_heads_q, "seq", split_axis=1, concat_axis=2, tiled=True),
        lax.all_to_all(grad_heads_k, "seq", split_axis=1, concat_axis=2, tiled=True),
        lax.all_to_all(grad_heads_v, "seq", split_axis=1, concat_axis=2, tiled=True),
    )
    grad_project = jnp.concatenate([grad_queries, grad_keys, grad_values], axis=2).reshape(
        tokens_here, 3 * width_all
    )
    grad_entry_one = compared_with(grad_project, full_qkv).reshape(token_shape)
    grad_shift_one = jnp.sum(grad_entry_one, axis=1)
    grad_scale_one = jnp.sum(grad_entry_one * normed_one, axis=1)
    grad_latents = grad_middle + normalize_back(
        grad_entry_one * (1.0 + scale_one), normed_one, inverse_one
    )
    grad_mod_part = jnp.concatenate(
        [
            grad_shift_one,
            grad_scale_one,
            grad_gate_one,
            grad_shift_two,
            grad_scale_two,
            grad_gate_two,
        ],
        axis=1,
    )
    grad_mod_seq = lax.psum(grad_mod_part, "seq").astype(jnp.bfloat16)
    grad_mod_all = lax.all_gather(grad_mod_seq, "fsdp", axis=0, tiled=True)
    grad_w_mod = outer_sum(lifted, grad_mod_all)
    grad_b_mod = jnp.sum(
        lax.dynamic_slice_in_dim(grad_mod_all, owner * mod_cols, mod_cols, 1).astype(jnp.float32),
        axis=0,
    )
    grad_lifted = compared_with(grad_mod_all, w_mod)
    grad_condition = lift_pull(grad_lifted)[0]
    grad_table = jnp.dot(
        one_hot.astype(jnp.float32).T,
        grad_condition,
        precision=lax.Precision.HIGHEST,
        preferred_element_type=jnp.float32,
    )
    grad_q_bias = jnp.sum(grad_project[:, :width_all].astype(jnp.float32), axis=0)
    grad_v_bias = jnp.sum(grad_project[:, 2 * width_all :].astype(jnp.float32), axis=0)
    grad_out_bias = jnp.sum(grad_branch_one.astype(jnp.float32), axis=0)
    grad_up_bias = jnp.sum(grad_hidden.astype(jnp.float32), axis=0)
    grad_down_bias = jnp.sum(grad_branch_two.astype(jnp.float32), axis=0)
    rights = (grad_project, grad_branch_one, grad_hidden, grad_branch_two)
    lefts = (
        regroup(entry_one, 1, fsdp_count, seq_count),
        regroup(token_mixed, 1, fsdp_count, seq_count),
        regroup(entry_two, 1, fsdp_count, seq_count),
        regroup(active, 1, fsdp_count, seq_count),
    )
    wide_term = make_term(lefts, rights, ratio)
    wide = lax.psum_scatter(
        wide_term(
            jnp.int32(0), width_all // (fsdp_count * seq_count) * lax.axis_size(("seq", "fsdp"))
        ),
        ("seq", "fsdp"),
        scatter_dimension=0,
        tiled=True,
    )
    biases = (
        lax.psum_scatter(
            regroup(grad_q_bias, 0, fsdp_count, seq_count),
            ("seq", "fsdp"),
            scatter_dimension=0,
            tiled=True,
        ),
        lax.psum_scatter(
            regroup(grad_v_bias, 0, fsdp_count, seq_count),
            ("seq", "fsdp"),
            scatter_dimension=0,
            tiled=True,
        ),
        lax.psum_scatter(
            regroup(grad_out_bias, 0, fsdp_count, seq_count),
            ("seq", "fsdp"),
            scatter_dimension=0,
            tiled=True,
        ),
        lax.psum_scatter(
            regroup(grad_up_bias, 0, fsdp_count, seq_count),
            ("seq", "fsdp"),
            scatter_dimension=0,
            tiled=True,
        ),
        lax.psum_scatter(
            regroup(grad_down_bias, 0, fsdp_count, seq_count),
            ("seq", "fsdp"),
            scatter_dimension=0,
            tiled=True,
        ),
    )
    owned = (
        lax.all_gather(wide, "seq", axis=0, tiled=True),
        lax.all_gather(biases[0], "seq", axis=0, tiled=True),
        lax.all_gather(biases[1], "seq", axis=0, tiled=True),
        lax.all_gather(biases[2], "seq", axis=0, tiled=True),
        lax.all_gather(biases[3], "seq", axis=0, tiled=True),
        lax.all_gather(biases[4], "seq", axis=0, tiled=True),
    )
    wide_owned = owned[0]
    ff_width = full_fc1.shape[1]
    grad_w_qkv = wide_owned[:, : 3 * width_all]
    grad_w_out = wide_owned[:, 3 * width_all : 4 * width_all]
    grad_w_fc1 = wide_owned[:, 4 * width_all : 4 * width_all + ff_width]
    grad_w_fc2 = wide_owned[:, 4 * width_all + ff_width :].reshape(-1, width_all)
    return (
        result,
        grad_latents,
        grad_table,
        grad_w_mod,
        grad_b_mod,
        grad_w_qkv,
        owned[1],
        owned[2],
        grad_w_out,
        owned[3],
        grad_w_fc1,
        owned[4],
        grad_w_fc2,
        owned[5],
    )


def attend_kernel(q_ref, k_ref, v_ref, o_ref, lse_ref):
    for head in range(2):
        at = slice(head * HEAD_DIM, (head + 1) * HEAD_DIM)
        queries = q_ref[:, at] * jnp.bfloat16(HEAD_DIM ** (-0.5))
        scores = compared_with(k_ref[:, at], queries)
        highest = jnp.max(scores, axis=0, keepdims=True)
        powers = jnp.exp(scores - highest)
        totals = jnp.sum(powers, axis=0, keepdims=True)
        probs = (powers * (1.0 / totals)).astype(jnp.bfloat16)
        mixed = jnp.dot(v_ref[:, at].T, probs, preferred_element_type=jnp.float32)
        o_ref[:, at] = mixed.T.astype(jnp.bfloat16)
        lse_ref[0, head : head + 1, :] = highest + jnp.log(totals)


def attend_back_kernel(q_ref, k_ref, v_ref, do_ref, lse_ref, dq_ref, dk_ref, dv_ref):
    for head in range(2):
        at = slice(head * HEAD_DIM, (head + 1) * HEAD_DIM)
        queries = q_ref[:, at] * jnp.bfloat16(HEAD_DIM ** (-0.5))
        keys = k_ref[:, at]
        grad_mixed = do_ref[:, at]
        probs = jnp.exp(compared_with(keys, queries) - lse_ref[0, head : head + 1, :])
        dv_ref[:, at] = jnp.dot(
            probs.astype(jnp.bfloat16), grad_mixed, preferred_element_type=jnp.float32
        ).astype(jnp.bfloat16)
        grad_probs = compared_with(v_ref[:, at], grad_mixed)
        inner = jnp.sum(grad_probs * probs, axis=0, keepdims=True)
        grad_scores = (probs * (grad_probs - inner)).astype(jnp.bfloat16)
        dk_ref[:, at] = jnp.dot(
            grad_scores, queries, preferred_element_type=jnp.float32
        ).astype(jnp.bfloat16)
        scaled_keys = keys * jnp.bfloat16(HEAD_DIM ** (-0.5))
        grad_queries = jnp.dot(scaled_keys.T, grad_scores, preferred_element_type=jnp.float32)
        dq_ref[:, at] = grad_queries.T.astype(jnp.bfloat16)


VMEM_LIMIT = 48 * 1024 * 1024


def attend_local(projected):
    length, wide = projected.shape
    pairs = wide // 3 // 128

    def part(which):
        return pl.BlockSpec((length, 128), lambda i: (0, which * pairs + i))

    cost = pl.CostEstimate(
        flops=pairs * length * length,
        bytes_accessed=length * wide,
        transcendentals=0,
    )
    return pl.pallas_call(
        attend_kernel,
        grid=(pairs,),
        in_specs=[part(0), part(1), part(2)],
        out_specs=[part(0), pl.BlockSpec((1, 2, length), lambda i: (i, 0, 0))],
        out_shape=[
            jax.ShapeDtypeStruct((length, wide // 3), jnp.bfloat16),
            jax.ShapeDtypeStruct((pairs, 2, length), jnp.float32),
        ],
        compiler_params=pltpu.CompilerParams(vmem_limit_bytes=VMEM_LIMIT),
        cost_estimate=cost,
        name="attend",
    )(projected, projected, projected)


def attend_local_back(projected, grad_mixed, log_totals):
    length, wide = projected.shape
    pairs = wide // 3 // 128

    def part(which):
        return pl.BlockSpec((length, 128), lambda i: (0, which * pairs + i))

    cost = pl.CostEstimate(
        flops=pairs * length * length,
        bytes_accessed=length * wide,
        transcendentals=0,
    )
    grads = jax.ShapeDtypeStruct((length, wide // 3), jnp.bfloat16)
    return pl.pallas_call(
        attend_back_kernel,
        grid=(pairs,),
        in_specs=[
            part(0),
            part(1),
            part(2),
            part(0),
            pl.BlockSpec((1, 2, length), lambda i: (i, 0, 0)),
        ],
        out_specs=[part(0), part(0), part(0)],
        out_shape=[grads, grads, grads],
        compiler_params=pltpu.CompilerParams(vmem_limit_bytes=VMEM_LIMIT),
        cost_estimate=cost,
        name="attend_back",
    )(projected, projected, projected, grad_mixed, log_totals)


def swapped_pairs(count, bit):
    return [(place, place ^ bit) for place in range(count)]


def assemble_kernel(place_ref, *refs):
    del place_ref
    pieces, out_refs = refs[:8], refs[8:]
    for which, piece in enumerate(pieces):

        @pl.when(pl.program_id(0) == which)
        def _():
            begin = 0
            for out_ref in out_refs:
                end = begin + out_ref.shape[-1]
                out_ref[:, 0, 0] = piece[:, :, begin:end]
                begin = end


def gather_half(weight):
    rows = weight.shape[0] // 2
    half = lax.dynamic_slice_in_dim(weight, lax.axis_index("seq") * rows, rows, 0)
    z_groups = [
        [base + 4 * step for step in range(lax.axis_size("fsdp") // 4)] for base in range(4)
    ]
    return lax.all_gather(half, "fsdp", axis=0, tiled=False, axis_index_groups=z_groups)


def flip(tensor, bit):
    return lax.ppermute(tensor, "fsdp", swapped_pairs(lax.axis_size("fsdp"), bit))


def flip_seq(tensor):
    return lax.ppermute(tensor, "seq", swapped_pairs(2, 1))


def assemble(own, by_seq, by_x, by_both, *widths):
    depth, rows, columns = own[0].shape
    count = 4 * depth
    pieces = [*own, *by_seq, *by_x, *by_both]
    owner = lax.axis_index("fsdp")
    flips = jnp.asarray([0, 1, 0, 1, 2, 3, 2, 3], jnp.int32)
    halves = jnp.asarray([0, 0, 1, 1, 0, 0, 1, 1], jnp.int32)
    places = jnp.concatenate(
        [
            jnp.bitwise_xor(lax.rem(owner, 4), flips),
            jnp.bitwise_xor(lax.axis_index("seq"), halves),
        ]
    )

    piece_spec = pl.BlockSpec((depth, rows, columns), lambda p, place_ref: (0, 0, 0))

    def out_block(p, place_ref):
        return (0, place_ref[p], place_ref[8 + p], 0, 0)

    whole = pl.pallas_call(
        assemble_kernel,
        grid_spec=pltpu.PrefetchScalarGridSpec(
            num_scalar_prefetch=1,
            grid=(8,),
            in_specs=[piece_spec] * 8,
            out_specs=[pl.BlockSpec((depth, 1, 1, rows, width), out_block) for width in widths],
        ),
        out_shape=[
            jax.ShapeDtypeStruct((depth, 4, 2, rows, width), own[0].dtype) for width in widths
        ],
        compiler_params=pltpu.CompilerParams(vmem_limit_bytes=VMEM_LIMIT),
        cost_estimate=pl.CostEstimate(
            flops=0, bytes_accessed=depth * rows * columns, transcendentals=0
        ),
        name="assemble",
    )(places, *pieces)
    return [part.reshape(2 * count * rows, -1) for part in whole]


def doubled(tensor, place, axis, other):
    first = jnp.where(place == 0, tensor, other)
    second = jnp.where(place == 0, other, tensor)
    return jnp.stack([first, second], axis=axis)


def gather_latents(line):
    count = lax.axis_size("fsdp")
    depth = count // 4
    owner = lax.axis_index("fsdp")
    z_at = lax.div(owner, 4)
    tensor = doubled(line, lax.axis_index("seq"), 0, flip_seq(line))
    tensor = doubled(tensor, lax.rem(owner, 2), 0, flip(tensor, 1))
    tensor = tensor.reshape(4, -1)
    slots = [tensor]
    for shift in range(1, depth):
        pairs = [(place, (place + 4 * shift) % count) for place in range(count)]
        slots.append(lax.ppermute(tensor, "fsdp", pairs))
    ordered = []
    for z in range(depth):
        shift = lax.rem(z_at - z + depth, depth)
        chosen = slots[0]
        for step in range(1, depth):
            chosen = jnp.where(shift == step, slots[step], chosen)
        ordered.append(chosen)
    return jnp.stack(ordered, axis=0)


def gather_latents_x(tensor):
    x_at = lax.rem(lax.div(lax.axis_index("fsdp"), 2), 2)
    both = doubled(tensor, x_at, 1, flip(tensor, 2))
    return both.reshape(8 * tensor.shape[0], -1)


def low(tensor):
    return tensor.astype(jnp.bfloat16)


def wide(tensor):
    return tensor.astype(jnp.float32)


def pick(tensor, axis, place):
    return lax.dynamic_index_in_dim(tensor, place, axis, keepdims=False)


def split_core(partial):
    count = lax.axis_size("fsdp")
    core_at = lax.rem(lax.axis_index("fsdp"), 2)
    rows, columns = partial.shape
    blocks = low(partial).reshape(count // 4, 2, 2, rows // count, columns)
    return pick(blocks, 2, core_at), pick(blocks, 2, 1 - core_at)


def split_x(kept, arrived):
    x_at = lax.rem(lax.div(lax.axis_index("fsdp"), 2), 2)
    here = wide(pick(kept, 1, x_at)) + wide(pick(arrived, 1, x_at))
    return here, low(wide(pick(kept, 1, 1 - x_at)) + wide(pick(arrived, 1, 1 - x_at)))


def split_z(here, crossed):
    depth = here.shape[0]
    z_at = lax.div(lax.axis_index("fsdp"), 4)
    leaving = []
    for shift in range(1, depth):
        target = lax.rem(z_at + shift, depth)
        leaving.append(low(pick(here, 0, target) + wide(pick(crossed, 0, target))))
    return pick(here, 0, z_at) + wide(pick(crossed, 0, z_at)), leaving


def send_z(leaving):
    count = lax.axis_size("fsdp")
    arrived = []
    for shift, part in enumerate(leaving, 1):
        pairs = [(place, (place + 4 * shift) % count) for place in range(count)]
        arrived.append(lax.ppermute(part, "fsdp", pairs))
    return arrived


def sum_z(total, arrived):
    for part in arrived:
        total = total + wide(part)
    return low(total)


def sum_seq(mine):
    return wide(mine) + wide(lax.ppermute(mine, "seq", swapped_pairs(2, 1)))


tied = lax.optimization_barrier


def local_whole_latent(
    latents,
    timesteps,
    class_ids,
    class_table,
    w_mod,
    b_mod,
    w_qkv,
    b_q,
    b_v,
    w_out,
    b_out,
    w_fc1,
    b_fc1,
    w_fc2,
    b_fc2,
    out_cotangent,
):
    rows_here, width_all = latents.shape[1:]
    columns = class_table.shape[1]
    owner = lax.axis_index("fsdp")
    mine = lax.axis_index("seq")
    fsdp_count = lax.axis_size("fsdp")
    seq_swap = swapped_pairs(2, 1)

    def whole_latent(pair):
        kept = lax.dynamic_index_in_dim(pair, mine, 0, keepdims=False)
        given = lax.dynamic_index_in_dim(pair, 1 - mine, 0, keepdims=False)
        return jnp.concatenate([kept, lax.ppermute(given, "seq", seq_swap)], axis=0)

    def both_halves(tokens):
        given = lax.ppermute(tokens[rows_here:], "seq", seq_swap)
        kept = tokens[:rows_here]
        first = jnp.where(mine == 0, kept, given)
        second = jnp.where(mine == 0, given, kept)
        return jnp.stack([first, second], axis=0)

    class_range = jnp.arange(class_table.shape[0], dtype=jnp.int32)
    one_hot = (class_ids[:, None] == class_range[None, :]).astype(jnp.bfloat16)
    looked_up = jnp.dot(one_hot, class_table, preferred_element_type=jnp.float32)
    timing = lax.dynamic_slice_in_dim(
        time_features(timesteps, width_all), owner * columns, columns, 1
    )
    condition = looked_up + timing
    lifted_full, lift_pull = jax.vjp(lift_silu, condition)
    lifted = lifted_full.astype(jnp.bfloat16)
    mod_width = w_mod.shape[1]
    mod_cols = b_mod.shape[0]
    bias_line = lax.dynamic_update_slice_in_dim(
        jnp.zeros((mod_width,), jnp.float32), b_mod.astype(jnp.float32), owner * mod_cols, 0
    )
    lifted_mine = lax.dynamic_index_in_dim(
        lifted.reshape(fsdp_count, 2, columns), mine, 1, keepdims=False
    )
    small = [b_q, b_v, b_out, b_fc1, b_fc2]
    small_line = wide(jnp.concatenate(small))
    to_owners = jnp.concatenate(
        [
            jnp.dot(lifted_mine, w_mod, preferred_element_type=jnp.float32) + bias_line[None, :],
            jnp.broadcast_to(small_line[None, :], (fsdp_count, small_line.shape[0])),
        ],
        axis=1,
    )
    from_owners = lax.all_to_all(to_owners, "fsdp", 0, 0, tiled=True)
    input_tokens = whole_latent(latents)
    cotangent_tokens = whole_latent(out_cotangent)
    own_a = gather_half(jnp.concatenate([w_qkv, w_out], axis=1))
    own_b = gather_half(w_fc1)
    own_a, from_owners, input_tokens, cotangent_tokens, w_fc2 = tied(
        (own_a, from_owners, input_tokens, cotangent_tokens, w_fc2)
    )
    own_c = gather_half(w_fc2)
    seq_a = flip_seq(own_a)
    x_a = flip(own_a, 2)
    own_b, seq_a = tied((own_b, seq_a))
    both_a = flip(seq_a, 2)
    seq_b = flip_seq(own_b)
    x_b = flip(own_b, 2)

    modulation = jnp.sum(from_owners[:, :mod_width], axis=0, keepdims=True)
    shift_one, scale_one, gate_one, shift_two, scale_two, gate_two = [
        modulation[:, position * width_all : (position + 1) * width_all] for position in range(6)
    ]
    biases = []
    begin = mod_width
    for part in small:
        end = begin + part.shape[0]
        biases.append(from_owners[:, begin:end].reshape(1, -1))
        begin = end
    query_bias, value_bias, out_bias, up_bias, down_bias = biases

    inputs_full = wide(input_tokens)
    grad_output = wide(cotangent_tokens)
    normed_one, inverse_one = normalize_keep(inputs_full)
    entry_one = low(normed_one * (1.0 + scale_one) + shift_one)
    full_qkv, full_out = assemble(
        (own_a, flip(own_a, 1)),
        (seq_a, flip(seq_a, 1)),
        (x_a, flip(x_a, 1)),
        (both_a, flip(both_a, 1)),
        w_qkv.shape[1],
        w_out.shape[1],
    )
    qkv_bias = jnp.concatenate([query_bias, jnp.zeros_like(query_bias), value_bias], axis=1)
    projected = low(jnp.dot(entry_one, full_qkv, preferred_element_type=jnp.float32) + qkv_bias)
    projected, x_b, seq_b, own_c = tied((projected, x_b, seq_b, own_c))
    both_b = flip_seq(x_b)
    seq_c = flip_seq(own_c)
    x_c = flip(own_c, 2)
    mixed, log_totals = attend_local(projected)
    branch_one = jnp.dot(mixed, full_out, preferred_element_type=jnp.float32) + out_bias
    middle = inputs_full + gate_one * branch_one
    normed_two, inverse_two = normalize_keep(middle)
    entry_two = low(normed_two * (1.0 + scale_two) + shift_two)
    (full_fc1,) = assemble(
        (own_b, flip(own_b, 1)),
        (seq_b, flip(seq_b, 1)),
        (x_b, flip(x_b, 1)),
        (both_b, flip(both_b, 1)),
        w_fc1.shape[1],
    )
    full_fc1, x_c, seq_c = tied((full_fc1, x_c, seq_c))
    both_c = flip(seq_c, 2)
    hidden = jnp.dot(entry_two, full_fc1, preferred_element_type=jnp.float32) + up_bias
    active_full, gelu_pull = jax.vjp(gelu_tanh, hidden)
    active = low(active_full)
    grad_branch_two = low(gate_two * grad_output)
    kept_fc2, leaving_fc2 = split_core(outer_sum(active, grad_branch_two))
    leaving_fc2, both_c = tied((leaving_fc2, both_c))
    arrived_fc2 = flip(leaving_fc2, 1)
    here_fc2, away_fc2 = split_x(kept_fc2, arrived_fc2)
    own_c, away_fc2 = tied((own_c, away_fc2))
    crossed_fc2 = flip(away_fc2, 2)
    (full_fc2,) = assemble(
        (own_c, flip(own_c, 1)),
        (seq_c, flip(seq_c, 1)),
        (x_c, flip(x_c, 1)),
        (both_c, flip(both_c, 1)),
        w_fc2.shape[1],
    )
    branch_two = jnp.dot(active, full_fc2, preferred_element_type=jnp.float32) + down_bias
    result_tokens = low(middle + gate_two * branch_two)
    grad_gate_two = jnp.sum(grad_output * branch_two, axis=0, keepdims=True)
    grad_active = compared_with(grad_branch_two, full_fc2)
    grad_hidden = low(gelu_pull(grad_active)[0])
    kept_fc1, leaving_fc1 = split_core(outer_sum(entry_two, grad_hidden))
    grad_hidden, leaving_fc1, crossed_fc2 = tied((grad_hidden, leaving_fc1, crossed_fc2))
    arrived_fc1 = flip(leaving_fc1, 1)
    grad_entry_two = compared_with(grad_hidden, full_fc1)
    here_fc1, away_fc1 = split_x(kept_fc1, arrived_fc1)
    total_fc2, leaving_fc2 = split_z(here_fc2, crossed_fc2)
    grad_entry_two, leaving_fc2, away_fc1 = tied((grad_entry_two, leaving_fc2, away_fc1))
    crossed_fc1 = flip(away_fc1, 2)
    grad_shift_two = jnp.sum(grad_entry_two, axis=0, keepdims=True)
    grad_scale_two = jnp.sum(grad_entry_two * normed_two, axis=0, keepdims=True)
    grad_middle = grad_output + normalize_back(
        grad_entry_two * (1.0 + scale_two), normed_two, inverse_two
    )
    grad_gate_one = jnp.sum(grad_middle * branch_one, axis=0, keepdims=True)
    grad_branch_one = low(gate_one * grad_middle)
    landed_fc2 = send_z(leaving_fc2)
    kept_out, leaving_out = split_core(outer_sum(mixed, grad_branch_one))
    leaving_out, grad_branch_one = tied((leaving_out, grad_branch_one))
    arrived_out = flip(leaving_out, 1)
    grad_mixed = low(compared_with(grad_branch_one, full_out))
    grad_mixed, arrived_out = tied((grad_mixed, arrived_out))
    grad_project = jnp.concatenate(attend_local_back(projected, grad_mixed, log_totals), axis=1)
    crossed_fc1, grad_project, landed_fc2 = tied((crossed_fc1, grad_project, landed_fc2))
    total_fc1, leaving_fc1 = split_z(here_fc1, crossed_fc1)
    grad_project, leaving_fc1 = tied((grad_project, leaving_fc1))
    landed_fc1 = send_z(leaving_fc1)
    kept_qkv, leaving_qkv = split_core(outer_sum(entry_one, grad_project))
    grad_project, leaving_qkv, landed_first = tied((grad_project, leaving_qkv, landed_fc1[0]))
    arrived_qkv = flip(leaving_qkv, 1)
    grad_entry_one = compared_with(grad_project, full_qkv)
    grad_entry_one, arrived_qkv = tied((grad_entry_one, arrived_qkv))
    here_last, away_last = [
        jnp.concatenate(parts, axis=-1)
        for parts in zip(split_x(kept_qkv, arrived_qkv), split_x(kept_out, arrived_out))
    ]
    small_inputs = (grad_project, grad_branch_one, grad_hidden, grad_branch_two)
    grad_entry_one, away_last, small_inputs, total_fc1, total_fc2, result_tokens = tied(
        (grad_entry_one, away_last, small_inputs, total_fc1, total_fc2, result_tokens)
    )
    result = both_halves(result_tokens)
    middle_row = away_last.shape[1] // 2
    crossed_early = flip(away_last[:, :middle_row], 2)
    crossed_late = flip(away_last[:, middle_row:], 2)
    sum_fc2 = sum_seq(sum_z(total_fc2, landed_fc2))
    grad_shift_one = jnp.sum(grad_entry_one, axis=0, keepdims=True)
    grad_scale_one = jnp.sum(grad_entry_one * normed_one, axis=0, keepdims=True)
    grad_latents = both_halves(
        grad_middle
        + normalize_back(grad_entry_one * (1.0 + scale_one), normed_one, inverse_one)
    )
    grad_mod_mine = low(
        jnp.concatenate(
            [
                grad_shift_one,
                grad_scale_one,
                grad_gate_one,
                grad_shift_two,
                grad_scale_two,
                grad_gate_two,
            ],
            axis=1,
        )
    )
    grad_mod_mine, small_inputs, crossed_early = tied(
        (grad_mod_mine, small_inputs, crossed_early)
    )
    grad_mod_z = gather_latents(grad_mod_mine)
    grad_project, grad_branch_one, grad_hidden, grad_branch_two = small_inputs
    grad_small = [
        wide(grad_project[:, :width_all]),
        wide(grad_project[:, 2 * width_all :]),
        wide(grad_branch_one),
        wide(grad_hidden),
        wide(grad_branch_two),
    ]
    small_sums = jnp.concatenate(
        [jnp.sum(part, axis=0).reshape(fsdp_count, -1) for part in grad_small], axis=1
    )
    small_here = jnp.sum(
        lax.all_to_all(small_sums, "fsdp", 0, 0, tiled=True), axis=0, keepdims=True
    )
    mine_fc1 = sum_z(total_fc1, [landed_first, *landed_fc1[1:]])
    mine_fc1, crossed_late, small_here, grad_mod_z, grad_latents, result = tied(
        (mine_fc1, crossed_late, small_here, grad_mod_z, grad_latents, result)
    )
    crossed_last = jnp.concatenate([crossed_early, crossed_late], axis=1)
    sum_fc1 = sum_seq(mine_fc1)
    total_last, leaving_last = split_z(here_last, crossed_last)
    landed_last = send_z(leaving_last)
    grad_mod_all = gather_latents_x(grad_mod_z)
    sum_last = sum_seq(sum_z(total_last, landed_last))
    sum_qkv = sum_last[:, : 3 * width_all]
    sum_out = sum_last[:, 3 * width_all :]
    small_total = (small_here + lax.ppermute(small_here, "seq", seq_swap))[0]
    small_grads = []
    begin = 0
    for part in small:
        small_grads.append(small_total[begin : begin + part.shape[0]])
        begin += part.shape[0]
    grad_w_mod = outer_sum(lifted, grad_mod_all)
    grad_b_mod = jnp.sum(
        lax.dynamic_slice_in_dim(grad_mod_all, owner * mod_cols, mod_cols, 1).astype(jnp.float32),
        axis=0,
    )
    grad_lifted = compared_with(grad_mod_all, w_mod)
    grad_condition = lift_pull(grad_lifted)[0]
    grad_table = jnp.dot(
        one_hot.astype(jnp.float32).T,
        grad_condition,
        precision=lax.Precision.HIGHEST,
        preferred_element_type=jnp.float32,
    )
    return (
        result,
        grad_latents,
        grad_table,
        grad_w_mod,
        grad_b_mod,
        sum_qkv,
        small_grads[0],
        small_grads[1],
        sum_out,
        small_grads[2],
        sum_fc1,
        small_grads[3],
        sum_fc2,
        small_grads[4],
    )


def solution(mesh):
    placed = (
        P("fsdp", "seq", None),
        P(),
        P(),
        P(None, "fsdp"),
        P("fsdp", None),
        P("fsdp"),
        P("fsdp", None),
        P("fsdp"),
        P("fsdp"),
        P("fsdp", None),
        P("fsdp"),
        P("fsdp", None),
        P("fsdp"),
        P("fsdp", None),
        P("fsdp"),
        P("fsdp", "seq", None),
    )
    spans = mesh.shape["fsdp"]

    def body(*arrays):
        whole_fits = arrays[0].shape[0] == mesh.shape["seq"] == 2 and spans % 4 == 0
        return (local_whole_latent if whole_fits else local)(*arrays)

    return jax.shard_map(
        body,
        mesh=mesh,
        in_specs=placed,
        out_specs=(
            P("fsdp", "seq", None),
            P("fsdp", "seq", None),
            P(None, "fsdp"),
            P("fsdp", None),
            P("fsdp"),
            P("fsdp", None),
            P("fsdp"),
            P("fsdp"),
            P("fsdp", None),
            P("fsdp"),
            P("fsdp", None),
            P("fsdp"),
            P("fsdp", None),
            P("fsdp"),
        ),
        check_vma=False,
    )
```
